32 devices in a mesh: section: 2 (over core), rows: 16 (over z, y, x).
Axes of the slice: x: 2, y: 2, z: 4, core: 2. Of those that a mesh axis runs over, the one named last changes fastest.
Arguments:
- token_states: bfloat16 [2, 64, 288, 768], P('section', 'rows'), may hold values from -6 to 6
- lengths: int32 [2, 64], P('section', 'rows'), may hold values from 50 to 288, as said below
- key_mask: int32 [2, 64, 288], P('section', 'rows'), may hold values 0 or 1
- cotangent: bfloat16 [2, 64, 288, 768], P('section', 'rows'), may hold values from -6 to 6
- attention_in: bfloat16 [2, 768, 2304], P('section'), may hold values from -0.21875 to 0.21875
- attention_bias: bfloat16 [2, 2, 768], P('section'), may hold values from -1.75 to 1.75
- attention_out: bfloat16 [2, 768, 768], P('section'), may hold values from -1.75 to 1.75
- output_bias: bfloat16 [2, 768], P('section'), may hold values from -1.75 to 1.75
- gain_one: bfloat16 [2, 768], P('section'), may hold values from 0.5 to 1.5
- shift_one: bfloat16 [2, 768], P('section'), may hold values from -1.75 to 1.75
- expand_weight: bfloat16 [2, 768, 3072], P('section'), may hold values from -0.21875 to 0.21875
- expand_bias: bfloat16 [2, 3072], P('section'), may hold values from -1.75 to 1.75
- contract_weight: bfloat16 [2, 3072, 768], P('section'), may hold values from -0.109375 to 0.109375
- contract_bias: bfloat16 [2, 768], P('section'), may hold values from -1.75 to 1.75
- gain_two: bfloat16 [2, 768], P('section'), may hold values from 0.5 to 1.5
- shift_two: bfloat16 [2, 768], P('section'), may hold values from -1.75 to 1.75
- projection: bfloat16 [768, 128], replicated, may hold values from -0.21875 to 0.21875
- passage_table: bfloat16 [4096, 128], replicated, may hold values from -1 to 1
- candidates: int32 [64, 8], P('rows'), may hold values from 0 to 4095
Outputs:
- states_out: float32 [2, 64, 288, 768], P('section', 'rows')
- states_grad: float32 [2, 64, 288, 768], P('section', 'rows')
- grad_attention_in: float32 [2, 768, 2304], P('section', None, 'rows')
- grad_attention_bias: float32 [2, 2, 768], P('section', None, 'rows')
- grad_attention_out: float32 [2, 768, 768], P('section', None, 'rows')
- grad_output_bias: float32 [2, 768], P('section', 'rows')
- grad_gain_one: float32 [2, 768], P('section', 'rows')
- grad_shift_one: float32 [2, 768], P('section', 'rows')
- grad_expand_weight: float32 [2, 768, 3072], P('section', None, 'rows')
- grad_expand_bias: float32 [2, 3072], P('section', 'rows')
- grad_contract_weight: float32 [2, 3072, 768], P('section', None, 'rows')
- grad_contract_bias: float32 [2, 768], P('section', 'rows')
- grad_gain_two: float32 [2, 768], P('section', 'rows')
- grad_shift_two: float32 [2, 768], P('section', 'rows')
- grad_projection: float32 [768, 128], replicated
The draws below stay inside these ranges and needn't reach their ends.
Inputs may be any that keep to these rules, and one draw needn't show every extreme that they name: `lengths`: in every draw, each section has a sequence of length exactly 288 and one of length exactly 50.
All inputs are finite; a program needn't handle non-finite values. No bound on the sum of `key_mask` on one device may be relied on, other than what follows from the above.
Results may differ from the reference program's by a relative error of at most 0.02.
Values may be sent and summed in bfloat16 or wider, within the bound.
No kernel may reach another device: no remote copies, remote signals or barrier semaphores. Data moves between devices by JAX's collectives and lax.ppermute only.
A program may use at most 320 MiB of HBM per device.

```python
import math
import jax
import jax.numpy as jnp
from jax import lax

D = 768
HD = 64
FF = 3072
PROJ = 128
TOPK = 8
L = 288
SHORT = 50
DOCS = 4096
SEQS = 64


def draw_lengths(key, part):
    key = jax.random.fold_in(key, 11)
    base = jax.random.randint(key, (2, SEQS), SHORT, L + 1)
    where_long = jax.random.randint(jax.random.fold_in(key, 1), (2,), 0, SEQS)
    columns = jnp.arange(SEQS)[None, :]
    base = jnp.where(columns == where_long[:, None], L, base)
    base = jnp.where(columns == (where_long[:, None] + 1) % SEQS, SHORT, base)
    return base.astype(jnp.int32)


def place_ends(drawn, own_key, smallest, high):
    dims = drawn.shape
    index_at = [jax.random.randint(jax.random.fold_in(own_key, axis), (), 0, dims[axis]) for axis in range(len(dims))]
    drawn = drawn.at[tuple(index_at)].set(smallest)
    longest = dims.index(max(dims))
    index_at[longest] = (index_at[longest] + 1) % dims[longest]
    return drawn.at[tuple(index_at)].set(high)


def with_spikes(drawn, key, source, target, shards_of, factor):
    def block_of(dim):
        return (jnp.arange(drawn.shape[dim]) // (drawn.shape[dim] // shards_of)).reshape((-1,) + (1,) * (drawn.ndim - 1 - dim))

    one_side = jax.random.permutation(key, shards_of)[block_of(target)]
    other_side = (block_of(target) + shards_of // 2) % shards_of
    return jnp.where((block_of(source) == one_side) | (block_of(source) == other_side), factor * drawn, drawn)


def shard_levels(rng, extent, shards, smallest, high):
    def one(dim, blocks):
        heights = jax.random.uniform(jax.random.fold_in(jax.random.fold_in(rng, 6), dim), (blocks,), jnp.float32, smallest / len(shards), high / len(shards))
        return jnp.repeat(jnp.exp(heights), extent[dim] // blocks).reshape((-1,) + (1,) * (len(extent) - dim - 1))

    level = one(*shards[0])
    for cut in shards[1:]:
        level = level * one(*cut)
    return level


def normal_values(stream_key, dims, scale, reach, cuts=(), kind=jnp.bfloat16):
    drawn = jax.random.normal(stream_key, dims, jnp.float32) * scale
    if len(cuts) > 0:
        drawn = shard_levels(stream_key, dims, cuts, -0.22, 0.18) * drawn
    return jnp.clip(drawn, min=-reach, max=reach).astype(kind)


def gaussian_with(stream_key, dims, scale, bound, cuts, heavy, kind=jnp.bfloat16):
    result = scale * jax.random.normal(stream_key, dims, jnp.float32)
    if cuts:
        result = result * shard_levels(stream_key, dims, cuts, -0.22, 0.18)
    return jnp.clip(with_spikes(result, jax.random.fold_in(stream_key, 3), *heavy), -bound, bound).astype(kind)


def setup_inputs(seed: int = 0) -> dict:
    seeds = jax.random.split(jax.random.key(seed), 20)
    return {
        "token_states": normal_values(seeds[0], (2, SEQS, L, D), 1.0, 6.0, ((0, 2), (1, 16))),
        "lengths": draw_lengths(jax.random.fold_in(seeds[19], 71), 0),
        "key_mask": place_ends((jax.random.randint(seeds[2], (2, SEQS, L), 0, 8) < 7).astype(jnp.int32), jax.random.fold_in(seeds[2], 1), 0, 1),
        "cotangent": gaussian_with(seeds[3], (2, SEQS, L, D), 1.0, 6.0, ((0, 2), (1, 16)), (1, 3, 16, 2.0)),
        "attention_in": normal_values(seeds[4], (2, D, 3 * D), D ** -0.5, 0.21875, ((0, 2),)),
        "attention_bias": normal_values(seeds[5], (2, 2, D), 0.3, 1.75, ((0, 2),)),
        "attention_out": normal_values(seeds[6], (2, D, D), (D // 64) ** -0.5, 1.75, ((0, 2),)),
        "output_bias": normal_values(seeds[7], (2, D), 0.3, 1.75, ((0, 2),)),
        "gain_one": jnp.clip(1.0 + 0.1 * jax.random.normal(seeds[8], (2, D), jnp.float32), 0.5, 1.5).astype(jnp.bfloat16),
        "shift_one": normal_values(seeds[9], (2, D), 0.3, 1.75, ((0, 2),)),
        "expand_weight": normal_values(seeds[10], (2, D, FF), D ** -0.5, 0.21875, ((0, 2),)),
        "expand_bias": normal_values(seeds[11], (2, FF), 0.3, 1.75, ((0, 2),)),
        "contract_weight": normal_values(seeds[12], (2, FF, D), FF ** -0.5, 0.109375, ((0, 2),)),
        "contract_bias": normal_values(seeds[13], (2, D), 0.3, 1.75, ((0, 2),)),
        "gain_two": jnp.clip(1.0 + 0.1 * jax.random.normal(seeds[14], (2, D), jnp.float32), 0.5, 1.5).astype(jnp.bfloat16),
        "shift_two": normal_values(seeds[15], (2, D), 0.3, 1.75, ((0, 2),)),
        "projection": normal_values(seeds[16], (D, PROJ), D ** -0.5, 0.21875),
        "passage_table": normal_values(seeds[17], (DOCS, PROJ), 0.18, 1.0),
        "candidates": place_ends(jax.random.randint(seeds[18], (SEQS, TOPK), 0, DOCS), jax.random.fold_in(seeds[18], 1), 0, DOCS - 1).astype(jnp.int32),
    }


@jax.custom_vjp
def low(v):
    return lax.optimization_barrier(v.astype(jnp.bfloat16)).astype(jnp.float32)

@jax.custom_vjp
def low_back(v):
    return v

def low_keep(v):
    return (low(v), None)

def low_pass(kept, grad):
    return (grad,)

def back_keep(v):
    return (v, None)

def back_low(kept, grad):
    return (low(grad),)
low.defvjp(low_keep, low_pass)
low_back.defvjp(back_keep, back_low)
NEGATIVE = -1000000000.0

def dense(left, right):
    return jnp.einsum('...i,ij->...j', left, right, precision=lax.Precision.HIGHEST)

def norm_apply(hidden, gain, shift):
    mean_value = lax.optimization_barrier(jnp.mean(hidden, axis=-1, keepdims=True))
    centered = hidden - mean_value
    variance = lax.optimization_barrier(jnp.mean(centered * centered, axis=-1, keepdims=True))
    return centered * lax.rsqrt(variance + 1e-12) * gain + shift

def run_layer(layer_weights, inputs, valid):
    attention_in, attention_bias, attention_out, output_bias, gain_one, shift_one, expand_weight, expand_bias, contract_weight, contract_bias, gain_two, shift_two = layer_weights
    sequences = inputs.shape[0]
    length = inputs.shape[1]
    width = inputs.shape[2]
    heads = width // HD
    scale_factor = 1.0 / math.sqrt(HD)
    bias_full = jnp.concatenate([attention_bias[0], jnp.zeros_like(attention_bias[0]), attention_bias[1]])
    mixed = low_back(low(dense(low(inputs), attention_in) + bias_full))
    split = mixed.reshape(sequences, length, 3, heads, HD)
    scores = jnp.einsum('sqhd,skhd->shqk', split[:, :, 0], split[:, :, 1], precision=lax.Precision.HIGHEST) * scale_factor
    scores = low_back(jnp.where(valid[:, None, None, :], scores, NEGATIVE))
    attention = low(jax.nn.softmax(scores, axis=-1))
    context = jnp.einsum('shqk,skhd->sqhd', attention, split[:, :, 2], precision=lax.Precision.HIGHEST)
    context = low_back(low(context)).reshape(sequences, length, width)
    attended = low_back(dense(context, attention_out) + output_bias)
    first = norm_apply(inputs + attended, gain_one, shift_one)
    hidden_pre = low_back(dense(low(first), expand_weight) + expand_bias)
    active = low(jax.nn.gelu(hidden_pre, approximate=False))
    feed = low_back(dense(active, contract_weight) + contract_bias)
    return norm_apply(first + feed, gain_two, shift_two)

def layer_in_groups(layer_weights, inputs, valid):
    sequences = inputs.shape[0]
    group = min(8, sequences)
    shaped = inputs.reshape(sequences // group, group, inputs.shape[1], inputs.shape[2])
    valid_shaped = valid.reshape(sequences // group, group, valid.shape[1])

    def one_group(pair):
        return run_layer(layer_weights, pair[0], pair[1])
    outputs = lax.map(jax.checkpoint(one_group), (shaped, valid_shaped))
    return outputs.reshape(inputs.shape)

def reference(token_states, lengths, key_mask, cotangent, attention_in, attention_bias, attention_out, output_bias, gain_one, shift_one, expand_weight, expand_bias, contract_weight, contract_bias, gain_two, shift_two, projection, passage_table, candidates):
    positions = jnp.arange(L)
    valid = (positions < lengths[:, :, None]) & (key_mask == 1) | (positions == 0)
    retrieved = passage_table.astype(jnp.float32)[candidates]
    layer_weights = tuple((array.astype(jnp.float32) for array in (attention_in, attention_bias, attention_out, output_bias, gain_one, shift_one, expand_weight, expand_bias, contract_weight, contract_bias, gain_two, shift_two)))

    def forward(stacked, projection_wide, queries, passages):
        first_weights = tuple((array[0] for array in stacked))
        second_weights = tuple((array[1] for array in stacked))
        query_out = layer_in_groups(first_weights, queries, valid[0])
        summary = low(query_out[:, 0, :])
        embedding = low_back(low(dense(summary, projection_wide)))
        match = low_back(jnp.einsum('sp,skp->sk', embedding, retrieved, precision=lax.Precision.HIGHEST))
        weight = TOPK * jax.nn.softmax(match, axis=-1)[:, 0]
        reader_in = passages.at[:, 0, :].add(low_back(summary))
        reader_out = layer_in_groups(second_weights, reader_in, valid[1])
        return (query_out, reader_out * weight[:, None, None])
    primal, pullback = jax.vjp(forward, layer_weights, projection.astype(jnp.float32), token_states[0].astype(jnp.float32), token_states[1].astype(jnp.float32))
    grad_weights, grad_projection, grad_queries, grad_passages = pullback((cotangent[0].astype(jnp.float32), cotangent[1].astype(jnp.float32)))
    return (jnp.stack([primal[0], primal[1]]), jnp.stack([grad_queries, grad_passages]), grad_weights[0], grad_weights[1], grad_weights[2], grad_weights[3], grad_weights[4], grad_weights[5], grad_weights[6], grad_weights[7], grad_weights[8], grad_weights[9], grad_weights[10], grad_weights[11], grad_projection)
```

```python
import functools
import math

import jax
import jax.numpy as jnp
from jax import lax
from jax.experimental import pallas as pl
from jax.experimental.pallas import tpu as pltpu
from jax.sharding import PartitionSpec as P

HD = 64
TOPK = 8
NEGATIVE = -1000000000.0
SCALE = 1.0 / math.sqrt(HD)
LANES = 128
ROW_TILE = 16
F32 = jnp.float32
LOW = jnp.bfloat16
NT = (((1,), (1,)), ((), ()))
TN = (((0,), (0,)), ((), ()))
MIB = 1 << 20


def dot(left, right):
    return jnp.dot(left, right, preferred_element_type=F32)


def dot_nt(left, right):
    return lax.dot_general(left, right, NT, preferred_element_type=F32)


def dot_tn(left, right):
    return lax.dot_general(left, right, TN, preferred_element_type=F32)


def params(limit):
    return pltpu.CompilerParams(vmem_limit_bytes=limit * MIB)


def cost(flops, moved):
    return pl.CostEstimate(flops=int(flops), bytes_accessed=int(moved), transcendentals=0)


ANYWHERE = pl.BlockSpec(memory_space=pl.ANY)


def fixed(shape):
    return pl.BlockSpec(shape, lambda *ids: (0,) * len(shape), pipeline_mode=pl.Buffered(1))


def norm_stats(hidden):
    mean = jnp.mean(hidden, axis=-1, keepdims=True)
    centered = hidden - mean
    root = lax.rsqrt(jnp.mean(centered * centered, axis=-1, keepdims=True) + 1e-12)
    return centered * root, root


def norm_back(grad, gain, normal, root):
    scaled = gain * grad
    mean = jnp.mean(scaled, axis=-1, keepdims=True)
    along = jnp.mean(scaled * normal, axis=-1, keepdims=True)
    return root * (scaled - mean - normal * along)


def gelu_both(u):
    phi = 0.5 + 0.5 * lax.erf(u * (1.0 / math.sqrt(2.0)))
    slope = phi + u * (jnp.exp(-0.5 * u * u) * (1.0 / math.sqrt(2.0 * math.pi)))
    return u * phi, slope


def head_rows(width):
    shape = (ROW_TILE, width)
    return lax.broadcasted_iota(jnp.int32, shape, 1) // HD == lax.broadcasted_iota(jnp.int32, shape, 0)


def pick(ref, row, columns=slice(None)):
    block = ref[:, columns]
    rows = lax.broadcasted_iota(jnp.int32, (block.shape[0], 1), 0)
    return jnp.sum(jnp.where(rows == row, block, 0.0), axis=0, keepdims=True)


def put(ref, row, value, columns=slice(None)):
    block = ref[:, columns]
    rows = lax.broadcasted_iota(jnp.int32, (block.shape[0], 1), 0)
    ref[:, columns] = jnp.where(rows == row, value, block)


def project_kernel(x_ref, w_ref, b_ref, o_ref, x0_ref):
    step = pl.program_id(0)
    bias = b_ref[...].astype(F32)
    bias = jnp.where(step == 0, bias[0:1, :], jnp.where(step == 2, bias[1:2, :], 0.0))
    for part in range(x_ref.shape[1]):
        o_ref[part] = (dot(x_ref[0, part], w_ref[...]) + bias).astype(LOW)
        x0_ref[part : part + 1, :] = x_ref[0, part, 0:1, :].astype(F32)


def project(x, weight, bias):
    _, count, length, width = x.shape
    return pl.pallas_call(
        project_kernel,
        grid=(3,),
        out_shape=(
            jax.ShapeDtypeStruct((count, length, 3 * width), LOW),
            jax.ShapeDtypeStruct((count, width), F32),
        ),
        in_specs=[
            fixed((1, count, length, width)),
            pl.BlockSpec((width, width), lambda i: (0, i)),
            fixed((2, width)),
        ],
        out_specs=(pl.BlockSpec((count, length, width), lambda i: (0, 0, i)), fixed((count, width))),
        compiler_params=params(32),
        cost_estimate=cost(6 * count * length * width * width, 14 * MIB),
        name="project_qkv",
    )(x, weight, bias)


def first_rows_kernel(
    mixed_ref, valid_ref, x0_ref, wo_ref, bo_ref, g1_ref, c1_ref, we_ref, be_ref, wc_ref, bc_ref,
    g2_ref, c2_ref, pr_ref, out_ref, ctx_ref, first_ref, acc_ref,
):
    step = pl.program_id(0)
    count = x0_ref.shape[0]
    width = wo_ref.shape[0]
    chunks = pl.num_programs(0) - count

    @pl.when(step < count)
    def _():
        heads = head_rows(width)
        query = mixed_ref[0, 0:1, 0:width].astype(F32) * SCALE
        spread = jnp.where(heads, query, 0.0).astype(LOW)
        scores = dot_nt(spread, mixed_ref[0, :, width : 2 * width])
        scores = jnp.where(valid_ref[0] > 0, scores, NEGATIVE)
        exponent = jnp.exp(scores - jnp.max(scores, axis=-1, keepdims=True))
        chance = (exponent / jnp.sum(exponent, axis=-1, keepdims=True)).astype(LOW)
        context = dot(chance, mixed_ref[0, :, 2 * width :])
        context = jnp.sum(jnp.where(heads, context, 0.0), axis=0, keepdims=True)
        ctx_ref[pl.ds(step, 1), :] = context

    @pl.when(step == count - 1)
    def _():
        hidden = x0_ref[...] + dot(ctx_ref[0:count, :].astype(LOW), wo_ref[...]) + bo_ref[...].astype(F32)
        normal, root = norm_stats(hidden)
        first_ref[...] = normal * g1_ref[...].astype(F32) + c1_ref[...].astype(F32)

    @pl.when(step >= count)
    def _():
        u = dot(first_ref[...].astype(LOW), we_ref[...]) + be_ref[...].astype(F32)
        active, slope = gelu_both(u)
        part = dot(active.astype(LOW), wc_ref[...])

        @pl.when(step == count)
        def _():
            acc_ref[...] = part

        @pl.when(step > count)
        def _():
            acc_ref[...] += part

    @pl.when(step == pl.num_programs(0) - 1)
    def _():
        normal, root = norm_stats(first_ref[...] + acc_ref[...] + bc_ref[...].astype(F32))
        summary = (normal * g2_ref[...].astype(F32) + c2_ref[...].astype(F32)).astype(LOW)
        out_ref[:, 0:width] = summary
        out_ref[:, width:] = dot(summary, pr_ref[...]).astype(LOW)


def first_rows(mixed, valid, x0, weights, projection):
    (_, _, wo, bo, g1, c1, we, be, wc, bc, g2, c2) = weights
    count, length, wide = mixed.shape
    width, hidden = we.shape
    chunk = 768
    chunks = hidden // chunk
    proj = projection.shape[1]

    def seq(i):
        return jnp.minimum(i, count - 1)

    def part(i):
        return jnp.maximum(i - count, 0)

    row = fixed((1, width))
    return pl.pallas_call(
        first_rows_kernel,
        grid=(count + chunks,),
        out_shape=jax.ShapeDtypeStruct((count, width + proj), LOW),
        in_specs=[
            pl.BlockSpec((1, length, wide), lambda i: (seq(i), 0, 0)),
            pl.BlockSpec((1, 1, length), lambda i: (seq(i), 0, 0)),
            fixed((count, width)),
            fixed((width, width)),
            row, row, row,
            pl.BlockSpec((width, chunk), lambda i: (0, part(i))),
            pl.BlockSpec((1, chunk), lambda i: (0, part(i))),
            pl.BlockSpec((chunk, width), lambda i: (part(i), 0)),
            row, row, row,
            fixed((width, proj)),
        ],
        out_specs=fixed((count, width + proj)),
        scratch_shapes=[
            pltpu.VMEM((8, width), F32),
            pltpu.VMEM((count, width), F32),
            pltpu.VMEM((count, width), F32),
        ],
        compiler_params=params(32),
        cost_estimate=cost(40 * MIB, 17 * MIB),
        name="first_rows_forward",
    )(mixed, valid, x0, wo, bo, g1, c1, we, be, wc, bc, g2, c2, projection)


def with_first(block, row):
    rows = lax.broadcasted_iota(jnp.int32, (ROW_TILE, 1), 0)
    top = jnp.where(rows == 0, row, block[0:ROW_TILE].astype(F32)).astype(block.dtype)
    return jnp.concatenate([top, block[ROW_TILE:]], axis=0)


def pair_of(mixed_ref, m0_ref, pair, width, seq):
    found = []
    for which in range(3):
        columns = pl.ds(which * width + pair * LANES, LANES)
        found.append(with_first(mixed_ref[0, :, columns], pick(m0_ref, seq, columns)))
    return found


def attention_forward_kernel(
    mixed_ref, m0_ref, x_ref, x0_ref, valid_ref, wo_ref, bo_ref, g_ref, c_ref,
    p_ref, ctx_ref, first_ref, low_ref, normal_ref, root_ref, xlow_ref, p0_ref, early_ref, n0_ref, r0_ref,
):
    seq = pl.program_id(0)
    length, width = x_ref.shape[2:]
    valid = valid_ref[0] > 0
    lane = lax.broadcasted_iota(jnp.int32, (1, LANES), 1)
    p0_ref[0] = jnp.zeros(p0_ref.shape[1:], LOW)
    for pair in range(width // LANES):
        columns = pl.ds(pair * LANES, LANES)
        query, key, value = pair_of(mixed_ref, m0_ref, pair, width, seq)
        results = []
        for half in range(2):
            mask = jnp.where(lane // HD == half, SCALE, 0.0).astype(LOW)
            scores = dot_nt(query * mask, key)
            scores = jnp.where(valid, scores, NEGATIVE)
            exponent = jnp.exp(scores - jnp.max(scores, axis=-1, keepdims=True))
            total = jnp.sum(exponent, axis=-1, keepdims=True)
            chance = (exponent * (1.0 / total)).astype(LOW)
            p_ref[0, 2 * pair + half] = chance
            p0_ref[0, 2 * pair + half : 2 * pair + half + 1, :] = chance[0:1, :]
            results.append(dot(chance, value))
        ctx_ref[0, :, columns] = jnp.where(lane < HD, results[0], results[1]).astype(LOW)
    rows = lax.broadcasted_iota(jnp.int32, (length, 1), 0)
    inputs = jnp.where(rows == 0, pick(x0_ref, seq), x_ref[0, 0].astype(F32))
    xlow_ref[0] = inputs.astype(LOW)
    hidden = inputs + dot(ctx_ref[0], wo_ref[...]) + bo_ref[...].astype(F32)
    normal, root = norm_stats(hidden)
    first = normal * g_ref[...].astype(F32) + c_ref[...].astype(F32)
    first_ref[0] = first
    low_ref[0] = first.astype(LOW)
    normal_ref[0] = normal.astype(LOW)
    root_ref[0] = jnp.broadcast_to(root, root_ref.shape[1:])
    put(early_ref, seq, first[0:1, :], slice(0, width))
    put(early_ref, seq, ctx_ref[0, 0:1, :].astype(F32), slice(width, 2 * width))
    put(n0_ref, seq, normal[0:1, :])
    put(r0_ref, seq, jnp.broadcast_to(root[0:1, :], (1, LANES)))


def attention_forward(mixed, m0, x, x0, valid, wo, bo, gain, shift):
    count, length, wide = mixed.shape
    width = wide // 3
    heads = width // HD

    def per(*shape):
        return pl.BlockSpec((1,) + shape, lambda i: (i,) + (0,) * len(shape))

    row = fixed((1, width))
    return pl.pallas_call(
        attention_forward_kernel,
        grid=(count,),
        out_shape=(
            jax.ShapeDtypeStruct((count, heads, length, length), LOW),
            jax.ShapeDtypeStruct((count, length, width), LOW),
            jax.ShapeDtypeStruct((count, length, width), F32),
            jax.ShapeDtypeStruct((count, length, width), LOW),
            jax.ShapeDtypeStruct((count, length, width), LOW),
            jax.ShapeDtypeStruct((count, length, LANES), F32),
            jax.ShapeDtypeStruct((count, length, width), LOW),
            jax.ShapeDtypeStruct((count, ROW_TILE, length), LOW),
            jax.ShapeDtypeStruct((count, 2 * width), F32),
            jax.ShapeDtypeStruct((count, width), F32),
            jax.ShapeDtypeStruct((count, LANES), F32),
        ),
        in_specs=[
            per(length, wide),
            fixed((count, wide)),
            pl.BlockSpec((1, 1, length, width), lambda i: (0, i, 0, 0)),
            fixed((count, width)),
            per(1, length),
            fixed((width, width)),
            row, row, row,
        ],
        out_specs=(
            per(heads, length, length),
            per(length, width),
            per(length, width),
            per(length, width),
            per(length, width),
            per(length, LANES),
            per(length, width),
            per(ROW_TILE, length),
            fixed((count, 2 * width)),
            fixed((count, width)),
            fixed((count, LANES)),
        ),
        compiler_params=params(60),
        cost_estimate=cost(12 * 1000**3, 26 * MIB),
        name="attention_forward",
    )(mixed, m0, x, x0, valid, wo, bo, gain, shift)


def turn(into_ref, from_ref):
    wide = from_ref.shape[1]
    tile = 384 if wide % 384 == 0 else LANES
    for column in range(0, wide, tile):
        into_ref[column : column + tile, :] = from_ref[:, column : column + tile].T


def grad_rows(place_ref, half, at_ref, right, out_ref, shards, kept, offset=0):
    span = at_ref.shape[0] // shards
    pitch = out_ref.shape[0] // (shards // 2)
    per = max(1, 384 // span)
    for group in range(0, shards // 2, per):
        pieces = []
        for shard in range(group, group + per):
            start = pl.multiple_of(place_ref[half, shard + kept * (shards // 2)] * span, ROW_TILE)
            pieces.append(at_ref[pl.ds(start, span), :])
        left = pieces[0] if per == 1 else jnp.concatenate(pieces, axis=0)
        result = dot(left, right).astype(LOW)
        for index in range(per):
            at = (group + index) * pitch + offset
            out_ref[at : at + span, :] = result[index * span : (index + 1) * span]


def feed_forward_kernel(
    place_ref, scal_ref, x_ref, we_ref, be_ref, wc_hbm, first_ref, bc_ref, g_ref, c_ref, cot_ref,
    slope_ref, out_ref, zg_ref, fg_ref, sums_ref, wg_ref, z0_ref, r0_ref, a0_ref, s0_ref,
    send0_ref, send1_ref, keep0_ref, keep1_ref,
    act_ref, wc_ref, feed_ref, low_ref, turned_ref, sem,
    *, chunks, tiles, shards,
):
    step = pl.program_id(0)
    length, width = first_ref.shape[1:]
    count = x_ref.shape[0] // length
    chunk = we_ref.shape[1]
    second = chunks + count + 1
    copy = pltpu.make_async_copy(wc_hbm, wc_ref, sem)

    @pl.when(step == 0)
    def _():
        copy.start()

    @pl.when(step < chunks)
    def _():
        u = dot(x_ref[...], we_ref[...]) + be_ref[...].astype(F32)
        active, slope = gelu_both(u)
        active = active.astype(LOW)
        act_ref[:, pl.ds(pl.multiple_of(step * chunk, LANES), chunk)] = active
        slope_ref[...] = slope.astype(LOW)
        for part in range(count):
            a0_ref[part : part + 1, :] = active[part * length : part * length + 1, :].astype(F32)
            s0_ref[part : part + 1, :] = slope[part * length : part * length + 1, :]

    def feed(seq):
        rows = pl.ds(pl.multiple_of(seq * length, ROW_TILE), length)
        feed_ref[lax.rem(seq, 2)] = dot(act_ref[rows, :], wc_ref[...])

    def norm(seq):
        weight = scal_ref[seq]
        keep = scal_ref[count]
        normal, root = norm_stats(first_ref[0] + feed_ref[lax.rem(seq, 2)] + bc_ref[...].astype(F32))
        gain = g_ref[...].astype(F32)
        result = normal * gain + c_ref[...].astype(F32)
        cot = cot_ref[0].astype(F32)
        out_ref[0] = weight * result
        put(wg_ref, seq, jnp.sum(cot * result, axis=0, keepdims=True))
        put(z0_ref, seq, normal[0:1, :])
        put(r0_ref, seq, jnp.broadcast_to(root[0:1, :], (1, LANES)))
        rows = lax.broadcasted_iota(jnp.int32, (length, 1), 0)
        grad = cot * jnp.where(rows == 0, weight * keep, weight)
        z_grad = norm_back(grad, gain, normal, root)
        zg_ref[0] = z_grad
        feed_grad = z_grad.astype(LOW)
        fg_ref[0] = feed_grad
        low_ref[pl.ds(pl.multiple_of(seq * length, ROW_TILE), length), :] = feed_grad
        sums_ref[0:1, :] += jnp.sum(grad * normal, axis=0, keepdims=True)
        sums_ref[1:2, :] += jnp.sum(grad, axis=0, keepdims=True)
        sums_ref[2:3, :] += jnp.sum(feed_grad.astype(F32), axis=0, keepdims=True)

    @pl.when(step == chunks)
    def _():
        copy.wait()
        sums_ref[...] = jnp.zeros(sums_ref.shape, F32)
        feed(0)

    @pl.when((step > chunks) & (step < second - 1))
    def _():
        feed(step - chunks)
        norm(step - chunks - 1)

    @pl.when(step == second - 1)
    def _():
        norm(count - 1)

    @pl.when(step == second)
    def _():
        turn(turned_ref, low_ref)

    def grads(half, send_ref, keep_ref):
        tile = send_ref.shape[1]
        columns = pl.ds(pl.multiple_of((step - second) * tile, LANES), tile)
        right = act_ref[:, columns]
        grad_rows(place_ref, half, turned_ref, right, send_ref, shards, 0)
        grad_rows(place_ref, half, turned_ref, right, keep_ref, shards, 1)

    @pl.when((step >= second) & (step < second + tiles))
    def _():
        grads(0, send0_ref, keep0_ref)

    @pl.when(step >= second + tiles)
    def _():
        grads(1, send1_ref, keep1_ref)


def feed_forward(place, scal, x, first, we, be, wc, bc, gain, shift, cot, shards):
    count, length, width = first.shape
    rows = count * length
    hidden = we.shape[1]
    chunk = 1024
    chunks = hidden // chunk
    tile = 512
    tiles = hidden // 2 // tile
    second = chunks + count + 1

    def part(i):
        return jnp.minimum(i, chunks - 1)

    def seq(i):
        return jnp.clip(i - chunks - 1, 0, count - 1)

    def early(i):
        return (0, jnp.clip(i - second, 0, tiles - 1))

    def late(i):
        return (0, jnp.clip(i - second - tiles, 0, tiles - 1))

    def per(*shape):
        return pl.BlockSpec((1,) + shape, lambda i: (seq(i),) + (0,) * len(shape))

    row = fixed((1, width))
    cut = jax.ShapeDtypeStruct((width // 2, hidden // 2), LOW)
    block = (width // 2, tile)
    return pl.pallas_call(
        functools.partial(feed_forward_kernel, chunks=chunks, tiles=tiles, shards=shards),
        grid=(second + 2 * tiles,),
        out_shape=(
            jax.ShapeDtypeStruct((rows, hidden), LOW),
            jax.ShapeDtypeStruct((count, length, width), F32),
            jax.ShapeDtypeStruct((count, length, width), F32),
            jax.ShapeDtypeStruct((count, length, width), LOW),
            jax.ShapeDtypeStruct((8, width), F32),
            jax.ShapeDtypeStruct((count, width), F32),
            jax.ShapeDtypeStruct((count, width), F32),
            jax.ShapeDtypeStruct((count, LANES), F32),
            jax.ShapeDtypeStruct((count, hidden), F32),
            jax.ShapeDtypeStruct((count, hidden), F32),
            cut, cut, cut, cut,
        ),
        in_specs=[
            pl.BlockSpec(memory_space=pltpu.SMEM),
            pl.BlockSpec(memory_space=pltpu.SMEM),
            fixed((rows, width)),
            pl.BlockSpec((width, chunk), lambda i: (0, part(i))),
            pl.BlockSpec((1, chunk), lambda i: (0, part(i))),
            ANYWHERE,
            per(length, width),
            row, row, row,
            per(length, width),
        ],
        out_specs=(
            pl.BlockSpec((rows, chunk), lambda i: (0, part(i))),
            per(length, width),
            per(length, width),
            per(length, width),
            fixed((8, width)),
            fixed((count, width)),
            fixed((count, width)),
            fixed((count, LANES)),
            pl.BlockSpec((count, chunk), lambda i: (0, part(i))),
            pl.BlockSpec((count, chunk), lambda i: (0, part(i))),
            pl.BlockSpec(block, early),
            pl.BlockSpec(block, late),
            pl.BlockSpec(block, early),
            pl.BlockSpec(block, late),
        ),
        scratch_shapes=[
            pltpu.VMEM((rows, hidden), LOW),
            pltpu.VMEM((hidden, width), LOW),
            pltpu.VMEM((2, length, width), F32),
            pltpu.VMEM((rows, width), LOW),
            pltpu.VMEM((width, rows), LOW),
            pltpu.SemaphoreType.DMA,
        ],
        compiler_params=params(60),
        cost_estimate=cost(25 * 1000**3, 50 * MIB),
        name="feed_forward",
    )(place, scal, x, we, be, wc, first, bc, gain, shift, cot)


def feed_backward_kernel(
    place_ref, fg_ref, slope_ref, wc_ref, we_hbm, zg_ref, normal_ref, root_ref, g_ref, x_ref,
    eb_ref, hgrad_ref, ag_ref, sums_ref, h0_ref,
    es0_ref, es1_ref, ek0_ref, ek1_ref,
    hg_ref, hidden_ref, we_ref, back_ref, sem,
    *, chunks, shards,
):
    step = pl.program_id(0)
    length, width = zg_ref.shape[1:]
    count = fg_ref.shape[0] // length
    chunk = slope_ref.shape[1]
    second = chunks + count + 1
    copy = pltpu.make_async_copy(we_hbm, we_ref, sem)

    @pl.when(step == 0)
    def _():
        copy.start()

    @pl.when(step < chunks)
    def _():
        grad = (dot_nt(fg_ref[...], wc_ref[...]) * slope_ref[...].astype(F32)).astype(LOW)
        at = pl.multiple_of(step * chunk, LANES)
        hg_ref[:, pl.ds(at, chunk)] = grad
        eb_ref[...] = jnp.sum(grad.astype(F32), axis=0, keepdims=True)
        hidden_ref[pl.ds(at, chunk), :] = grad.T

    def feed(seq):
        rows = pl.ds(pl.multiple_of(seq * length, ROW_TILE), length)
        back_ref[lax.rem(seq, 2)] = dot_nt(hg_ref[rows, :], we_ref[...])

    def norm(seq):
        grad = zg_ref[0] + back_ref[lax.rem(seq, 2)]
        normal = normal_ref[0].astype(F32)
        h_grad = norm_back(grad, g_ref[...].astype(F32), normal, root_ref[0, :, 0:1])
        hgrad_ref[0] = h_grad
        put(h0_ref, seq, h_grad[0:1, :])
        attended = h_grad.astype(LOW)
        ag_ref[0] = attended
        sums_ref[0:1, :] += jnp.sum(grad * normal, axis=0, keepdims=True)
        sums_ref[1:2, :] += jnp.sum(grad, axis=0, keepdims=True)
        sums_ref[2:3, :] += jnp.sum(attended.astype(F32), axis=0, keepdims=True)

    @pl.when(step == chunks)
    def _():
        copy.wait()
        sums_ref[...] = jnp.zeros(sums_ref.shape, F32)
        feed(0)

    @pl.when((step > chunks) & (step < second - 1))
    def _():
        feed(step - chunks)
        norm(step - chunks - 1)

    @pl.when(step == second - 1)
    def _():
        norm(count - 1)

    half = width // 2
    for half_index, send_ref, keep_ref in ((0, es0_ref, ek0_ref), (1, es1_ref, ek1_ref)):
        for kept, out_ref in ((0, send_ref), (1, keep_ref)):

            @pl.when(step == second + 2 * half_index + kept)
            def _():
                right = x_ref[:, half_index * half : (half_index + 1) * half]
                grad_rows(place_ref, half_index, hidden_ref, right, out_ref, shards, kept)


def feed_backward(place, fg, slope, wc, we, zg, normal, root, gain, x, shards):
    count, length, width = zg.shape
    rows, hidden = slope.shape
    chunk = 1024
    chunks = hidden // chunk

    def part(i):
        return jnp.minimum(i, chunks - 1)

    def seq(i):
        return jnp.clip(i - chunks - 1, 0, count - 1)

    def per(*shape):
        return pl.BlockSpec((1,) + shape, lambda i: (seq(i),) + (0,) * len(shape))

    cut = jax.ShapeDtypeStruct((hidden // 2, width // 2), LOW)
    return pl.pallas_call(
        functools.partial(feed_backward_kernel, chunks=chunks, shards=shards),
        grid=(chunks + count + 5,),
        out_shape=(
            jax.ShapeDtypeStruct((1, hidden), F32),
            jax.ShapeDtypeStruct((count, length, width), F32),
            jax.ShapeDtypeStruct((count, length, width), LOW),
            jax.ShapeDtypeStruct((8, width), F32),
            jax.ShapeDtypeStruct((count, width), F32),
            cut, cut, cut, cut,
        ),
        in_specs=[
            pl.BlockSpec(memory_space=pltpu.SMEM),
            fixed((rows, width)),
            pl.BlockSpec((rows, chunk), lambda i: (0, part(i))),
            pl.BlockSpec((chunk, width), lambda i: (part(i), 0)),
            ANYWHERE,
            per(length, width),
            per(length, width),
            per(length, LANES),
            fixed((1, width)),
            fixed((rows, width)),
        ],
        out_specs=(
            pl.BlockSpec((1, chunk), lambda i: (0, part(i))),
            per(length, width),
            per(length, width),
            fixed((8, width)),
            fixed((count, width)),
        )
        + (fixed((hidden // 2, width // 2)),) * 4,
        scratch_shapes=[
            pltpu.VMEM((rows, hidden), LOW),
            pltpu.VMEM((hidden, rows), LOW),
            pltpu.VMEM((width, hidden), LOW),
            pltpu.VMEM((2, length, width), F32),
            pltpu.SemaphoreType.DMA,
        ],
        compiler_params=params(60),
        cost_estimate=cost(25 * 1000**3, 50 * MIB),
        name="feed_backward",
    )(place, fg, slope, wc, we, zg, normal, root, gain, x)


def attention_backward_kernel(
    place_ref, ag_ref, wo_ref, p_ref, mixed_ref, m0_ref, x_ref, ctx_ref, *refs, shards
):
    (
        mg_ref, mg0_ref, s0_ref, s1_ref, k0_ref, k1_ref,
        dctx_ref, all_ref, turned_ref, low_ref, other_ref,
    ) = refs[-11:]
    step = pl.program_id(0)
    length, width = ag_ref.shape[1:]
    count = x_ref.shape[0] // length

    @pl.when(step < count)
    def _():
        dctx_ref[...] = dot_nt(ag_ref[0], wo_ref[...]).astype(LOW)
        lane = lax.broadcasted_iota(jnp.int32, (1, LANES), 1)
        rows = pl.ds(pl.multiple_of(step * length, ROW_TILE), length)
        low_ref[rows, :] = ag_ref[0]
        for pair in range(width // LANES):
            query, key, value = pair_of(mixed_ref, m0_ref, pair, width, step)
            grad = dctx_ref[:, pl.ds(pair * LANES, LANES)]
            grads = []
            for half in range(2):
                mask = jnp.where(lane // HD == half, 1.0, 0.0).astype(LOW)
                chance_low = p_ref[0, 2 * pair + half]
                chance = chance_low.astype(F32)
                p_grad = dot_nt(grad * mask, value)
                inner = jnp.sum(p_grad * chance, axis=-1, keepdims=True)
                s_grad = (chance * (p_grad - inner)).astype(LOW)
                grads.append((dot(s_grad, key), dot_tn(s_grad, query), dot_tn(chance_low, grad)))
            for which in range(3):
                both = jnp.where(lane < HD, grads[0][which], grads[1][which])
                if which < 2:
                    both = both * SCALE
                columns = pl.ds(which * width + pair * LANES, LANES)
                low = both.astype(LOW)
                mg_ref[0, :, columns] = low
                all_ref[rows, columns] = low
                put(mg0_ref, step, low[0:1, :].astype(F32), columns)

    @pl.when(step == count)
    def _():
        turn(turned_ref, all_ref)
        turn(other_ref, low_ref)

    half = width // 2
    for half_index, send_ref, keep_ref in ((0, s0_ref, k0_ref), (1, s1_ref, k1_ref)):
        for kept, out_ref in ((0, send_ref), (1, keep_ref)):

            @pl.when(step == count + 2 * half_index + kept)
            def _():
                columns = slice(half_index * half, (half_index + 1) * half)
                grad_rows(place_ref, half_index, turned_ref, x_ref[:, columns], out_ref, shards, kept)
                at = turned_ref.shape[0] // shards
                grad_rows(place_ref, half_index, other_ref, ctx_ref[:, columns], out_ref, shards, kept, at)


def attention_backward(place, ag, wo, p, mixed, m0, x, ctx, after, shards):
    count, length, wide = mixed.shape
    width = wide // 3
    heads = width // HD
    rows = count * length

    def per(*shape):
        return pl.BlockSpec((1,) + shape, lambda i: (jnp.minimum(i, count - 1),) + (0,) * len(shape))

    cut = ((wide + width) // 2, width // 2)
    return pl.pallas_call(
        functools.partial(attention_backward_kernel, shards=shards),
        grid=(count + 4,),
        out_shape=(
            jax.ShapeDtypeStruct((count, length, wide), LOW),
            jax.ShapeDtypeStruct((count, wide), F32),
        )
        + (jax.ShapeDtypeStruct(cut, LOW),) * 4,
        in_specs=[
            pl.BlockSpec(memory_space=pltpu.SMEM),
            per(length, width),
            fixed((width, width)),
            per(heads, length, length),
            per(length, wide),
            fixed((count, wide)),
            fixed((rows, width)),
            fixed((rows, width)),
        ]
        + [ANYWHERE] * len(after),
        out_specs=(per(length, wide), fixed((count, wide))) + (fixed(cut),) * 4,
        scratch_shapes=[
            pltpu.VMEM((length, width), LOW),
            pltpu.VMEM((rows, wide), LOW),
            pltpu.VMEM((wide, rows), LOW),
            pltpu.VMEM((rows, width), LOW),
            pltpu.VMEM((width, rows), LOW),
        ],
        compiler_params=params(60),
        cost_estimate=cost(24 * 1000**3, 32 * MIB),
        name="attention_backward",
    )(place, ag, wo, p, mixed, m0, x, ctx, *after)


def shard_groups(count, wide):
    span = wide // count
    first = [span * shard // HD for shard in range(count)]
    most = max((span * shard + span - 1) // HD - first[shard] + 1 for shard in range(count))
    return [min(one, wide // HD - most) for one in first], most


def input_grad_kernel(mg_ref, w_ref, hgrad_ref, *refs):
    out_ref, sums_ref = refs[-2:]
    width = hgrad_ref.shape[2]
    out_ref[0] = dot_nt(mg_ref[0], w_ref[...]) + hgrad_ref[0]

    @pl.when(pl.program_id(0) == 0)
    def _():
        sums_ref[...] = jnp.zeros(sums_ref.shape, F32)

    sums_ref[0:1, :] += jnp.sum(mg_ref[0, :, 0:width].astype(F32), axis=0, keepdims=True)
    sums_ref[1:2, :] += jnp.sum(mg_ref[0, :, 2 * width :].astype(F32), axis=0, keepdims=True)


def input_grad(mg, weight, hgrad, after):
    count, length, wide = mg.shape
    width = wide // 3

    def per(*shape):
        return pl.BlockSpec((1,) + shape, lambda i: (i,) + (0,) * len(shape))

    return pl.pallas_call(
        input_grad_kernel,
        grid=(count,),
        out_shape=(jax.ShapeDtypeStruct((count, length, width), F32), jax.ShapeDtypeStruct((8, width), F32)),
        in_specs=[per(length, wide), fixed((width, wide)), per(length, width)] + [ANYWHERE] * len(after),
        out_specs=(per(length, width), fixed((8, width))),
        compiler_params=params(40),
        cost_estimate=cost(6 * 1000**3, 16 * MIB),
        name="input_grad",
    )(mg, weight, hgrad, *after)


def last_kernel(
    g0_ref, z0_ref, r2_ref, g2_ref, slope_ref, wc_ref, we_ref, n0_ref, r1_ref, g1_ref, wo_ref, wi_hbm,
    p0_ref, mixed_ref, m0_ref, x_ref, main_ref, s2_ref, s1_ref, s0_ref, eb_ref, *refs, groups
):
    (
        out_ref, hg_ref, fg_ref, ag_ref, coef_ref, y_ref, sums_ref, ebout_ref,
        zg_ref, acc_ref, hz_ref, dctx_ref, rows_ref, wi_ref, sem,
    ) = refs[-15:]
    step = pl.program_id(0)
    count, width = g0_ref.shape
    chunks = pl.num_programs(0) - count
    copy = pltpu.make_async_copy(wi_hbm, wi_ref, sem)

    @pl.when(step == 0)
    def _():
        copy.start()
        grad = g0_ref[...]
        z_grad = norm_back(grad, g2_ref[...].astype(F32), z0_ref[...], r2_ref[:, 0:1])
        zg_ref[...] = z_grad
        low = z_grad.astype(LOW)
        fg_ref[...] = low
        sums_ref[0:2, :] = s0_ref[0:2, :]
        sums_ref[6:7, :] = s2_ref[0:1, :] + jnp.sum(grad * z0_ref[...], axis=0, keepdims=True)
        sums_ref[7:8, :] = s2_ref[1:2, :] + jnp.sum(grad, axis=0, keepdims=True)
        sums_ref[5:6, :] = s2_ref[2:3, :] + jnp.sum(low.astype(F32), axis=0, keepdims=True)
        acc_ref[...] = jnp.zeros(acc_ref.shape, F32)

    @pl.when(step < chunks)
    def _():
        grad = (dot_nt(fg_ref[...], wc_ref[...]) * slope_ref[...].astype(F32)).astype(LOW)
        hg_ref[...] = grad
        ebout_ref[...] = eb_ref[...] + jnp.sum(grad.astype(F32), axis=0, keepdims=True)
        acc_ref[...] += dot_nt(grad, we_ref[...])

    @pl.when(step == chunks - 1)
    def _():
        grad = zg_ref[...] + acc_ref[...]
        normal = n0_ref[...]
        h_grad = norm_back(grad, g1_ref[...].astype(F32), normal, r1_ref[:, 0:1])
        hz_ref[0:count, :] = h_grad
        low = h_grad.astype(LOW)
        ag_ref[...] = low
        sums_ref[3:4, :] = s1_ref[0:1, :] + jnp.sum(grad * normal, axis=0, keepdims=True)
        sums_ref[4:5, :] = s1_ref[1:2, :] + jnp.sum(grad, axis=0, keepdims=True)
        sums_ref[2:3, :] = s1_ref[2:3, :] + jnp.sum(low.astype(F32), axis=0, keepdims=True)
        dctx_ref[0:count, :] = dot_nt(low, wo_ref[...])
        copy.wait()

    @pl.when(step >= chunks)
    def _():
        seq = step - chunks
        heads = head_rows(width)
        own = dctx_ref[pl.ds(seq, 1), :]
        grad = jnp.where(heads, own, 0.0).astype(LOW)
        query0 = pick(m0_ref, seq, slice(0, width))
        query = jnp.where(heads, query0, 0.0).astype(LOW)
        key = with_first(mixed_ref[0, :, width : 2 * width], pick(m0_ref, seq, slice(width, 2 * width)))
        value = with_first(mixed_ref[0, :, 2 * width :], pick(m0_ref, seq, slice(2 * width, 3 * width)))
        chance_low = p0_ref[0]
        chance = chance_low.astype(F32)
        p_grad = dot_nt(grad, value)
        s_grad = (chance * (p_grad - jnp.sum(p_grad * chance, axis=-1, keepdims=True))).astype(LOW)
        dq = dot(s_grad, key)
        dq = jnp.sum(jnp.where(heads, dq, 0.0), axis=0, keepdims=True) * SCALE
        put(coef_ref, seq, dq, slice(0, width))
        put(coef_ref, seq, query0 * SCALE, slice(width, 2 * width))
        put(coef_ref, seq, own, slice(2 * width, 3 * width))
        inputs = x_ref[0]
        rows_ref[0, 0:1, :] = inputs[0:1, :].astype(F32)
        rows_ref[1] = dot(s_grad, inputs)
        rows_ref[2] = dot(chance_low, inputs)
        firsts, most = groups
        per = width // HD
        for shard, first in enumerate(firsts):
            for turn_of in range(most):
                which, head = divmod(first + turn_of, per)
                head = head if which else 0
                y_ref[shard, 0, turn_of : turn_of + 1, :] = rows_ref[which, head : head + 1, :].astype(LOW)
        from_key = (dot_nt(query, wi_ref[:, width : 2 * width]) * SCALE).astype(LOW)
        from_value = dot_nt(grad, wi_ref[:, 2 * width :]).astype(LOW)
        from_query = dot_nt(jnp.where(heads, dq, 0.0).astype(LOW), wi_ref[:, 0:width])
        from_query = jnp.sum(from_query, axis=0, keepdims=True) + hz_ref[pl.ds(seq, 1), :]
        rows = lax.broadcasted_iota(jnp.int32, (inputs.shape[0], 1), 0)
        back = dot_tn(s_grad, from_key) + dot_tn(chance_low, from_value)
        out_ref[0] = main_ref[0] + back + jnp.where(rows == 0, from_query, 0.0)
        sums_ref[0:1, :] += dq
        held = jnp.sum(chance, axis=-1, keepdims=True)
        sums_ref[1:2, :] += jnp.sum(held * grad.astype(F32), axis=0, keepdims=True)


def last_rows(g0, z0, r2, g2, slope0, wc, we, n0, r1, g1, wo, wi, p0, mixed, m0, x, main, s2, s1, s0, eb, after, shards):
    count, length, wide = mixed.shape
    width = wide // 3
    hidden = slope0.shape[1]
    chunk = 768
    chunks = hidden // chunk
    groups = shard_groups(shards, wide)

    def part(i):
        return jnp.minimum(i, chunks - 1)

    def seq(i):
        return jnp.maximum(i - chunks, 0)

    def per(*shape):
        return pl.BlockSpec((1,) + shape, lambda i: (seq(i),) + (0,) * len(shape))

    row = fixed((1, width))
    rows = fixed((count, width))
    return pl.pallas_call(
        functools.partial(last_kernel, groups=groups),
        grid=(chunks + count,),
        out_shape=(
            jax.ShapeDtypeStruct((count, length, width), F32),
            jax.ShapeDtypeStruct((count, hidden), LOW),
            jax.ShapeDtypeStruct((count, width), LOW),
            jax.ShapeDtypeStruct((count, width), LOW),
            jax.ShapeDtypeStruct((count, wide), F32),
            jax.ShapeDtypeStruct((shards, count, groups[1], width), LOW),
            jax.ShapeDtypeStruct((8, width), F32),
            jax.ShapeDtypeStruct((1, hidden), F32),
        ),
        in_specs=[
            rows, rows, fixed((count, LANES)), row,
            pl.BlockSpec((count, chunk), lambda i: (0, part(i))),
            pl.BlockSpec((chunk, width), lambda i: (part(i), 0)),
            pl.BlockSpec((width, chunk), lambda i: (0, part(i))),
            rows, fixed((count, LANES)), row,
            fixed((width, width)),
            ANYWHERE,
            per(ROW_TILE, length),
            per(length, wide),
            fixed((count, wide)),
            per(length, width),
            per(length, width),
            fixed((8, width)),
            fixed((8, width)),
            fixed((8, width)),
            pl.BlockSpec((1, chunk), lambda i: (0, part(i))),
        ]
        + [ANYWHERE] * len(after),
        out_specs=(
            per(length, width),
            pl.BlockSpec((count, chunk), lambda i: (0, part(i))),
            rows, rows,
            fixed((count, wide)),
            pl.BlockSpec((shards, 1, groups[1], width), lambda i: (0, seq(i), 0, 0)),
            fixed((8, width)),
            pl.BlockSpec((1, chunk), lambda i: (0, part(i))),
        ),
        scratch_shapes=[
            pltpu.VMEM((count, width), F32),
            pltpu.VMEM((count, width), F32),
            pltpu.VMEM((8, width), F32),
            pltpu.VMEM((8, width), F32),
            pltpu.VMEM((3, ROW_TILE, width), F32),
            pltpu.VMEM((width, wide), LOW),
            pltpu.SemaphoreType.DMA,
        ],
        compiler_params=params(60),
        cost_estimate=cost(8 * 1000**3, 36 * MIB),
        name="last_rows",
    )(g0, z0, r2, g2, slope0, wc, we, n0, r1, g1, wo, wi, p0, mixed, m0, x, main, s2, s1, s0, eb, *after)


def flip(value, bit, count):
    return lax.ppermute(value, "rows", [(i, i ^ bit) for i in range(count)])


BITS = ((1, 2), (2, 1))


def first_stage(parts, count):
    return [flip(parts[half], BITS[half][0], count) for half in range(2)]


def second_stage(sends, count):
    return [flip(sends[half], BITS[half][1], count) for half in range(2)]


def sum_low(left_ref, right_ref):
    return (left_ref[...].astype(F32) + right_ref[...].astype(F32)).astype(LOW)


def first_sum_kernel(a0, a1, b0, b1, ga0, ga1, gb0, gb1, *refs):
    sa, sb, ka, kb = refs[-4:]
    sa[...] = sum_low(a0, ga0)
    ka[...] = sum_low(a1, ga1)
    sb[...] = sum_low(b0, gb0)
    kb[...] = sum_low(b1, gb1)


def first_sum(parts, got, after):
    keep0, keep1 = parts[2:]
    rows, width = keep0.shape
    tiles = 4
    block = (rows // 2 // tiles, width)
    top = pl.BlockSpec(block, lambda i: (i, 0))
    bottom = pl.BlockSpec(block, lambda i: (i + tiles, 0))
    result = pl.pallas_call(
        first_sum_kernel,
        grid=(tiles,),
        out_shape=(jax.ShapeDtypeStruct((rows // 2, width), LOW),) * 4,
        in_specs=[top, bottom] * 4 + [ANYWHERE] * len(after),
        out_specs=(top,) * 4,
        compiler_params=params(32),
        cost_estimate=cost(rows * width, 12 * rows * width),
        name="first_sum",
    )(keep0, keep0, keep1, keep1, got[0], got[0], got[1], got[1], *after)
    return result[:2], result[2:]


def second_sum_kernel(a, b, ga, gb, *refs, rest):
    step = pl.program_id(0)
    half = a.shape[1]
    for index, out in enumerate(refs[-rest:]):

        @pl.when(step == index)
        def _():
            out[:, :half] = sum_low(a, ga)
            out[:, half:] = sum_low(b, gb)


def second_sum(keeps, got, count, after):
    rows, width = keeps[0].shape
    rest = count // 4
    block = pl.BlockSpec((rows // rest, width), lambda i: (i, 0))
    shape = (rows // rest, 2 * width)
    return pl.pallas_call(
        functools.partial(second_sum_kernel, rest=rest),
        grid=(rest,),
        out_shape=(jax.ShapeDtypeStruct(shape, LOW),) * rest,
        in_specs=[block] * 4 + [ANYWHERE] * len(after),
        out_specs=(fixed(shape),) * rest,
        compiler_params=params(32),
        cost_estimate=cost(rows * width, 12 * rows * width),
        name="second_sum",
    )(keeps[0], keeps[1], got[0], got[1], *after)


def third_stage(totals, count):
    got = [totals[0]]
    for step in range(1, count // 4):
        pairs = [(i, (i + 4 * step) % count) for i in range(count)]
        got.append(lax.ppermute(totals[step], "rows", pairs))
    return got


def third_sum(got):
    return functools.reduce(lambda left, right: left + right, [part.astype(F32) for part in got])


def places(count):
    me = lax.axis_index("rows")
    tables = []
    for first, second in BITS:
        entries = []
        for one in (first, 0):
            for two in (second, 0):
                for step in range(count // 4):
                    entries.append(((me ^ one ^ two) + 4 * step) % count)
        tables.append(jnp.stack(entries))
    return jnp.stack(tables).astype(jnp.int32)


def whole_grad(parts, count, rows=slice(None)):
    send0, send1, keep0, keep1 = (part[rows] for part in parts)
    full = jnp.concatenate(
        [jnp.concatenate([send0, send1], axis=1), jnp.concatenate([keep0, keep1], axis=1)], axis=0
    )
    return lax.psum_scatter(full.astype(F32), "rows", scatter_dimension=0, tiled=True)


def gather_rows(array, count):
    spread = jnp.broadcast_to(array[None], (count,) + array.shape)
    got = lax.all_to_all(spread, "rows", 0, 0, tiled=True)
    return got.reshape((count * array.shape[0],) + array.shape[1:])


def body(
    token_states, lengths, key_mask, cotangent, attention_in, attention_bias, attention_out, output_bias,
    gain_one, shift_one, expand_weight, expand_bias, contract_weight, contract_bias, gain_two, shift_two,
    projection, passage_table, candidates,
):
    section = lax.axis_index("section")
    is_first = section == 0
    count = lax.axis_size("rows")
    me = lax.axis_index("rows")
    tokens = token_states[0]
    seqs, length, width = tokens.shape
    rows = seqs * length

    bi = attention_bias[0]
    wi, wo, we, wc = attention_in[0], attention_out[0], expand_weight[0], contract_weight[0]
    bo, g1, c1, be, bc, g2, c2 = output_bias, gain_one, shift_one, expand_bias, contract_bias, gain_two, shift_two
    weights = (wi, bi, wo, bo, g1, c1, we, be, wc, bc, g2, c2)
    positions = jnp.arange(length)
    valid = (positions[None, :] < lengths[0][:, None]) & (key_mask[0] == 1) | (positions[None, :] == 0)
    valid = valid.astype(F32)[:, None, :]
    staged = count % 4 == 0 and width // count % ROW_TILE == 0
    cuts = count if staged else 2
    place = places(count) if staged else jnp.asarray([[0, 1], [0, 1]], jnp.int32)

    retrieved = jnp.take(passage_table, candidates, axis=0).astype(F32)
    mixed, x0 = project(token_states, wi, bi)
    message = first_rows(mixed, valid, x0, weights, projection)
    received = lax.ppermute(message, "section", [(0, 1)])
    summary_in, embedding_in = received[:, :width], received[:, width:]
    x0 = x0 + summary_in.astype(F32)
    in_bias = jnp.concatenate([bi[0], jnp.zeros_like(bi[0]), bi[1]])
    mixed0 = (dot(x0.astype(LOW), wi) + in_bias.astype(F32)).astype(LOW).astype(F32)
    chance, context, first, first_low, normal, root, x_low, chance0, early, n0, r1 = attention_forward(
        mixed, mixed0, token_states, x0, valid, wo, bo, g1, c1
    )
    match = jnp.sum(embedding_in.astype(F32)[:, None, :] * retrieved, axis=-1)
    chances = jax.nn.softmax(match, axis=-1)
    weight = TOPK * chances[:, 0]
    scal = jnp.concatenate([jnp.where(is_first, 1.0, weight), jnp.where(is_first, 0.0, 1.0)[None]]).astype(F32)
    first_flat = first_low.reshape(rows, width)
    slope, out, z_grad, feed_grad, sums_two, weight_grads, z0, r2, active0, slope0, *contract = feed_forward(
        place, scal, first_flat, first, we, be, wc, bc, g2, c2, cotangent[0], cuts
    )

    contract_got = first_stage(contract, count) if staged else None
    used_summary = jnp.where(is_first, message[:, :width], summary_in)
    early = jnp.concatenate([active0.astype(LOW), early.astype(LOW), used_summary], axis=1)
    early = gather_rows(early, count)
    expand_sum, h_grad, attended, sums_one, h0, *expand = feed_backward(
        place, feed_grad.reshape(rows, width), slope, wc, we, z_grad, normal, root, g1, first_flat, cuts
    )
    contract_send = ()
    if staged:
        contract_send, contract_keep = first_sum(contract, contract_got, (h0, early))
        contract_got = second_stage(contract_send, count)
        expand_got = first_stage(expand, count)
    mixed_grad, mg0, *rest = attention_backward(
        place, attended, wo, chance, mixed, mixed0, x_low.reshape(rows, width), context.reshape(rows, width),
        tuple(contract_send), cuts,
    )
    after = ()
    if staged:
        contract = second_sum(contract_keep, contract_got, count, (mg0,))
        contract_got = third_stage(contract, count)
        expand_send, expand_keep = first_sum(expand, expand_got, (mg0,))
        expand_got = second_stage(expand_send, count)
        rest_got = first_stage(rest, count)
        after = (contract[0], expand_send[0])
    x_main, sums_in = input_grad(mixed_grad, wi, h_grad, after)

    grad_weight = jnp.sum(weight_grads, axis=1)
    one = jnp.zeros((TOPK,), F32).at[0].set(1.0)
    grad_match = (grad_weight[:, None] * weight[:, None] * (one[None, :] - chances)).astype(LOW)
    embedding_grad = jnp.sum(grad_match.astype(F32)[:, :, None] * retrieved, axis=1).astype(LOW)
    reader_term = (h0 + dot_nt(mg0.astype(LOW), wi)).astype(LOW)
    back = lax.ppermute(jnp.concatenate([reader_term, embedding_grad], axis=1), "section", [(1, 0)])
    embedding_used = jnp.where(is_first, back[:, width:], embedding_grad)
    summary_grad = dot_nt(back[:, width:], projection) + back[:, :width].astype(F32)
    grad_zero = jnp.where(is_first, cotangent[0, :, 0, :].astype(F32) + summary_grad, 0.0)
    x_grad, hidden_zero, feed_zero, attended_zero, coefs, groups, vectors, expand_sum = last_rows(
        grad_zero, z0, r2, g2, slope0, wc, we, n0, r1, g1, wo, wi, chance0, mixed, mixed0, x_low, x_main,
        sums_two, sums_one, sums_in, expand_sum, (), count,
    )

    span = 3 * width // count
    if staged:
        expand = second_sum(expand_keep, expand_got, count, (vectors,))
        rest_send, rest_keep = first_sum(rest, rest_got, (vectors, expand[0]))
        expand_got = third_stage(expand, count)
        rest_got = second_stage(rest_send, count)
        held = (hidden_zero, feed_zero, attended_zero, coefs, groups, vectors, expand_sum, contract_got, rest_send[0])
        held = lax.optimization_barrier(held)
        hidden_zero, feed_zero, attended_zero, coefs, groups, vectors, expand_sum, contract_got, _ = held
        rest = second_sum(rest_keep, rest_got, count, ())
        rest_got = third_stage(rest, count)
        contract = third_sum(contract_got)
        expand = third_sum(expand_got)
        rest = third_sum(rest_got)
        attention_in_grad, attention_out_grad = rest[:span], rest[span:]
    else:
        contract = whole_grad(contract, count)
        expand = whole_grad(expand, count)
        attention_in_grad = whole_grad(rest, count, slice(0, 3 * width // 2))
        attention_out_grad = whole_grad(rest, count, slice(3 * width // 2, None))

    hidden = we.shape[1]
    active_all, first_all = early[:, :hidden], early[:, hidden : hidden + width]
    context_all = early[:, hidden + width : hidden + 2 * width]
    summary_all = early[:, hidden + 2 * width :]

    def shards(array):
        return jnp.swapaxes(array.reshape(array.shape[0], count, -1), 0, 1)

    most = groups.shape[2]
    spread = jnp.broadcast_to(embedding_used[None], (count,) + embedding_used.shape)
    late = jnp.concatenate(
        [
            shards(feed_zero), shards(hidden_zero), shards(attended_zero), shards(coefs.astype(LOW)), spread,
            groups.reshape(count, seqs, -1),
        ],
        axis=2,
    )
    packed = jnp.concatenate([shards(vectors).reshape(count, -1), expand_sum.reshape(count, -1)], axis=1)
    upper = packed.astype(LOW)
    lower = (packed - upper.astype(F32)).astype(LOW)
    packed = jnp.concatenate([upper, lower], axis=1)
    share = packed.shape[1]
    packed = jnp.pad(packed, ((0, 0), (0, late.shape[2] - share)))
    late = lax.all_to_all(jnp.concatenate([late, packed[:, None, :]], axis=1), "rows", 0, 0, tiled=True)
    packed = jnp.sum(late[:, seqs, :share].astype(F32).reshape(count, 2, share // 2), axis=(0, 1))
    late = late[:, :seqs].reshape(count * seqs, -1)
    ends = [width // count, (width + hidden) // count, (2 * width + hidden) // count, (5 * width + hidden) // count]
    ends.append(ends[3] + embedding_used.shape[1])
    contract = contract + dot_tn(late[:, : ends[0]], active_all)
    expand = expand + dot_tn(late[:, ends[0] : ends[1]], first_all)
    attention_out_grad = attention_out_grad + dot_tn(late[:, ends[1] : ends[2]], context_all)
    head = (span * me + jnp.arange(span)) // HD - jnp.asarray(shard_groups(count, 3 * width)[0], jnp.int32)[me]
    for one in range(most):
        part = late[:, ends[2] : ends[3]] * (head == one).astype(LOW)[None]
        attention_in_grad = attention_in_grad + dot_tn(part, late[:, ends[4] + one * width : ends[4] + (one + 1) * width])
    projection_grad = dot_tn(summary_all, late[:, ends[3] : ends[4]])
    part = width // count
    q_bias, v_bias, o_bias, gain1, shift1, c_bias, gain2, shift2 = (packed[i * part : (i + 1) * part] for i in range(8))
    e_bias = packed[8 * part :]
    return (
        out[None],
        x_grad[None],
        attention_in_grad.T[None],
        jnp.stack([q_bias, v_bias])[None],
        attention_out_grad.T[None],
        o_bias[None],
        gain1[None],
        shift1[None],
        expand.T[None],
        e_bias[None],
        contract.T[None],
        c_bias[None],
        gain2[None],
        shift2[None],
        projection_grad,
    )


def solution(mesh):
    in_specs = (
        P("section", "rows", None, None),
        P("section", "rows"),
        P("section", "rows", None),
        P("section", "rows", None, None),
        P("section", None, None),
        P("section", None, None),
        P("section", None, None),
        P("section", None),
        P("section", None),
        P("section", None),
        P("section", None, None),
        P("section", None),
        P("section", None, None),
        P("section", None),
        P("section", None),
        P("section", None),
        P(),
        P(),
        P("rows", None),
    )
    out_specs = (
        P("section", "rows", None, None),
        P("section", "rows", None, None),
        P("section", None, "rows"),
        P("section", None, "rows"),
        P("section", None, "rows"),
        P("section", "rows"),
        P("section", "rows"),
        P("section", "rows"),
        P("section", None, "rows"),
        P("section", "rows"),
        P("section", None, "rows"),
        P("section", "rows"),
        P("section", "rows"),
        P("section", "rows"),
        P(),
    )
    return jax.shard_map(body, mesh=mesh, in_specs=in_specs, out_specs=out_specs, check_vma=False)
```

```python
import functools
import math

import jax
import jax.numpy as jnp
from jax import lax
from jax.experimental import pallas as pl
from jax.experimental.pallas import tpu as pltpu
from jax.sharding import PartitionSpec as P

HD = 64
TOPK = 8
NEGATIVE = -1000000000.0
SCALE = 1.0 / math.sqrt(HD)
LANES = 128
ROW_TILE = 16
F32 = jnp.float32
LOW = jnp.bfloat16
NT = (((1,), (1,)), ((), ()))
TN = (((0,), (0,)), ((), ()))
MIB = 1 << 20


def dot(left, right):
    return jnp.dot(left, right, preferred_element_type=F32)


def dot_nt(left, right):
    return lax.dot_general(left, right, NT, preferred_element_type=F32)


def dot_tn(left, right):
    return lax.dot_general(left, right, TN, preferred_element_type=F32)


def params(limit):
    return pltpu.CompilerParams(vmem_limit_bytes=limit * MIB)


MUCH = pl.CostEstimate(flops=100 * 1000**3, bytes_accessed=50 * MIB, transcendentals=0)
LITTLE = pl.CostEstimate(flops=1, bytes_accessed=1, transcendentals=0)


ANYWHERE = pl.BlockSpec(memory_space=pl.ANY)


def fixed(shape):
    return pl.BlockSpec(shape, lambda *ids: (0,) * len(shape), pipeline_mode=pl.Buffered(1))


def norm_stats(hidden):
    mean = jnp.mean(hidden, axis=-1, keepdims=True)
    centered = hidden - mean
    root = lax.rsqrt(jnp.mean(centered * centered, axis=-1, keepdims=True) + 1e-12)
    return centered * root, root


def norm_back(grad, gain, normal, root):
    scaled = gain * grad
    mean = jnp.mean(scaled, axis=-1, keepdims=True)
    along = jnp.mean(scaled * normal, axis=-1, keepdims=True)
    return root * (scaled - mean - normal * along)


def gelu_both(u):
    phi = 0.5 + 0.5 * lax.erf(u * (1.0 / math.sqrt(2.0)))
    slope = phi + u * (jnp.exp(-0.5 * u * u) * (1.0 / math.sqrt(2.0 * math.pi)))
    return u * phi, slope


def head_rows(width):
    shape = (ROW_TILE, width)
    return lax.broadcasted_iota(jnp.int32, shape, 1) // HD == lax.broadcasted_iota(jnp.int32, shape, 0)


def pick(ref, row, columns=slice(None)):
    block = ref[:, columns]
    rows = lax.broadcasted_iota(jnp.int32, (block.shape[0], 1), 0)
    return jnp.sum(jnp.where(rows == row, block, 0.0), axis=0, keepdims=True)


def put(ref, row, value, columns=slice(None)):
    block = ref[:, columns]
    rows = lax.broadcasted_iota(jnp.int32, (block.shape[0], 1), 0)
    ref[:, columns] = jnp.where(rows == row, value, block)


def project_kernel(x_ref, w_ref, b_ref, o_ref, x0_ref):
    step = pl.program_id(0)
    bias = b_ref[...].astype(F32)
    bias = jnp.where(step == 0, bias[0:1, :], jnp.where(step == 2, bias[1:2, :], 0.0))
    for part in range(x_ref.shape[1]):
        o_ref[part] = (dot(x_ref[0, part], w_ref[...]) + bias).astype(LOW)
        x0_ref[part : part + 1, :] = x_ref[0, part, 0:1, :].astype(F32)


def project(x, weight, bias):
    _, count, length, width = x.shape
    return pl.pallas_call(
        project_kernel,
        grid=(3,),
        out_shape=(
            jax.ShapeDtypeStruct((count, length, 3 * width), LOW),
            jax.ShapeDtypeStruct((count, width), F32),
        ),
        in_specs=[
            fixed((1, count, length, width)),
            pl.BlockSpec((width, width), lambda i: (0, i)),
            fixed((2, width)),
        ],
        out_specs=(pl.BlockSpec((count, length, width), lambda i: (0, 0, i)), fixed((count, width))),
        compiler_params=params(32),
        cost_estimate=pl.CostEstimate(flops=6 * count * length * width * width, bytes_accessed=14 * MIB, transcendentals=0),
        name="project_qkv",
    )(x, weight, bias)


def first_rows_kernel(
    mixed_ref, valid_ref, x0_ref, wo_ref, bo_ref, g1_ref, c1_ref, we_ref, be_ref, wc_ref, bc_ref,
    g2_ref, c2_ref, pr_ref, out_ref, ctx_ref, first_ref, acc_ref,
):
    step = pl.program_id(0)
    count = x0_ref.shape[0]
    width = wo_ref.shape[0]
    chunks = pl.num_programs(0) - count

    @pl.when(step < count)
    def _():
        heads = head_rows(width)
        query = mixed_ref[0, 0:1, 0:width].astype(F32) * SCALE
        spread = jnp.where(heads, query, 0.0).astype(LOW)
        scores = dot_nt(spread, mixed_ref[0, :, width : 2 * width])
        scores = jnp.where(valid_ref[0] > 0, scores, NEGATIVE)
        exponent = jnp.exp(scores - jnp.max(scores, axis=-1, keepdims=True))
        chance = (exponent / jnp.sum(exponent, axis=-1, keepdims=True)).astype(LOW)
        context = dot(chance, mixed_ref[0, :, 2 * width :])
        context = jnp.sum(jnp.where(heads, context, 0.0), axis=0, keepdims=True)
        ctx_ref[pl.ds(step, 1), :] = context

    @pl.when(step == count - 1)
    def _():
        hidden = x0_ref[...] + dot(ctx_ref[0:count, :].astype(LOW), wo_ref[...]) + bo_ref[...].astype(F32)
        normal, root = norm_stats(hidden)
        first_ref[...] = normal * g1_ref[...].astype(F32) + c1_ref[...].astype(F32)

    @pl.when(step >= count)
    def _():
        u = dot(first_ref[...].astype(LOW), we_ref[...]) + be_ref[...].astype(F32)
        active, slope = gelu_both(u)
        part = dot(active.astype(LOW), wc_ref[...])

        @pl.when(step == count)
        def _():
            acc_ref[...] = part

        @pl.when(step > count)
        def _():
            acc_ref[...] += part

    @pl.when(step == pl.num_programs(0) - 1)
    def _():
        normal, root = norm_stats(first_ref[...] + acc_ref[...] + bc_ref[...].astype(F32))
        summary = (normal * g2_ref[...].astype(F32) + c2_ref[...].astype(F32)).astype(LOW)
        out_ref[:, 0:width] = summary
        out_ref[:, width:] = dot(summary, pr_ref[...]).astype(LOW)


def first_rows(mixed, valid, x0, weights, projection):
    (_, _, wo, bo, g1, c1, we, be, wc, bc, g2, c2) = weights
    count, length, wide = mixed.shape
    width, hidden = we.shape
    chunk = 768
    chunks = hidden // chunk
    proj = projection.shape[1]

    def seq(i):
        return jnp.minimum(i, count - 1)

    def part(i):
        return jnp.maximum(i - count, 0)

    row = fixed((1, width))
    return pl.pallas_call(
        first_rows_kernel,
        grid=(count + chunks,),
        out_shape=jax.ShapeDtypeStruct((count, width + proj), LOW),
        in_specs=[
            pl.BlockSpec((1, length, wide), lambda i: (seq(i), 0, 0)),
            pl.BlockSpec((1, 1, length), lambda i: (seq(i), 0, 0)),
            fixed((count, width)),
            fixed((width, width)),
            row, row, row,
            pl.BlockSpec((width, chunk), lambda i: (0, part(i))),
            pl.BlockSpec((1, chunk), lambda i: (0, part(i))),
            pl.BlockSpec((chunk, width), lambda i: (part(i), 0)),
            row, row, row,
            fixed((width, proj)),
        ],
        out_specs=fixed((count, width + proj)),
        scratch_shapes=[
            pltpu.VMEM((8, width), F32),
            pltpu.VMEM((count, width), F32),
            pltpu.VMEM((count, width), F32),
        ],
        compiler_params=params(32),
        cost_estimate=pl.CostEstimate(flops=40 * MIB, bytes_accessed=17 * MIB, transcendentals=0),
        name="first_rows_forward",
    )(mixed, valid, x0, wo, bo, g1, c1, we, be, wc, bc, g2, c2, projection)


def with_first(block, row):
    rows = lax.broadcasted_iota(jnp.int32, (ROW_TILE, 1), 0)
    top = jnp.where(rows == 0, row, block[0:ROW_TILE].astype(F32)).astype(block.dtype)
    return jnp.concatenate([top, block[ROW_TILE:]], axis=0)


def pair_of(mixed_ref, m0_ref, pair, width, seq):
    found = []
    for which in range(3):
        columns = pl.ds(which * width + pair * LANES, LANES)
        found.append(with_first(mixed_ref[0, :, columns], pick(m0_ref, seq, columns)))
    return found


def short_keys(length):
    return (length - 1) // LANES * LANES


def attention_forward_kernel(
    len_ref, mixed_ref, m0_ref, x_ref, x0_ref, valid_ref, wo_ref, bo_ref, g_ref, c_ref,
    p_ref, ctx_ref, first_ref, low_ref, normal_ref, root_ref, xlow_ref, p0_ref, early_ref, n0_ref, r0_ref,
):
    seq = pl.program_id(0)
    length, width = x_ref.shape[2:]
    valid = valid_ref[0] > 0
    lane = lax.broadcasted_iota(jnp.int32, (1, LANES), 1)
    p0_ref[0] = jnp.zeros(p0_ref.shape[1:], LOW)

    def heads(keys):
        for pair in range(width // LANES):
            query, key, value = pair_of(mixed_ref, m0_ref, pair, width, seq)
            results = []
            for half in range(2):
                mask = jnp.where(lane // HD == half, SCALE, 0.0).astype(LOW)
                scores = dot_nt(query * mask, key[:keys])
                scores = jnp.where(valid[:, :keys], scores, NEGATIVE)
                exponent = jnp.exp(scores - jnp.max(scores, axis=-1, keepdims=True))
                total = jnp.sum(exponent, axis=-1, keepdims=True)
                chance = (exponent * (1.0 / total)).astype(LOW)
                p_ref[0, 2 * pair + half, :, 0:keys] = chance
                p0_ref[0, 2 * pair + half : 2 * pair + half + 1, 0:keys] = chance[0:1, :]
                results.append(dot(chance, value[:keys]))
            ctx_ref[0, :, pl.ds(pair * LANES, LANES)] = jnp.where(lane < HD, results[0], results[1]).astype(LOW)

    short = short_keys(length)

    @pl.when(len_ref[seq] <= short)
    def _():
        heads(short)

    @pl.when(len_ref[seq] > short)
    def _():
        heads(length)

    rows = lax.broadcasted_iota(jnp.int32, (length, 1), 0)
    inputs = jnp.where(rows == 0, pick(x0_ref, seq), x_ref[0, 0].astype(F32))
    xlow_ref[0] = inputs.astype(LOW)
    hidden = inputs + dot(ctx_ref[0], wo_ref[...]) + bo_ref[...].astype(F32)
    normal, root = norm_stats(hidden)
    first = normal * g_ref[...].astype(F32) + c_ref[...].astype(F32)
    first_ref[0] = first
    low_ref[0] = first.astype(LOW)
    normal_ref[0] = normal.astype(LOW)
    root_ref[0] = jnp.broadcast_to(root, root_ref.shape[1:])
    put(early_ref, seq, first[0:1, :], slice(0, width))
    put(early_ref, seq, ctx_ref[0, 0:1, :].astype(F32), slice(width, 2 * width))
    put(n0_ref, seq, normal[0:1, :])
    put(r0_ref, seq, jnp.broadcast_to(root[0:1, :], (1, LANES)))


def attention_forward(lengths, mixed, m0, x, x0, valid, wo, bo, gain, shift):
    count, length, wide = mixed.shape
    width = wide // 3
    heads = width // HD

    def per(*shape):
        return pl.BlockSpec((1,) + shape, lambda i: (i,) + (0,) * len(shape))

    row = fixed((1, width))
    return pl.pallas_call(
        attention_forward_kernel,
        grid=(count,),
        out_shape=(
            jax.ShapeDtypeStruct((count, heads, length, length), LOW),
            jax.ShapeDtypeStruct((count, length, width), LOW),
            jax.ShapeDtypeStruct((count, length, width), F32),
            jax.ShapeDtypeStruct((count, length, width), LOW),
            jax.ShapeDtypeStruct((count, length, width), LOW),
            jax.ShapeDtypeStruct((count, length, LANES), F32),
            jax.ShapeDtypeStruct((count, length, width), LOW),
            jax.ShapeDtypeStruct((count, ROW_TILE, length), LOW),
            jax.ShapeDtypeStruct((count, 2 * width), F32),
            jax.ShapeDtypeStruct((count, width), F32),
            jax.ShapeDtypeStruct((count, LANES), F32),
        ),
        in_specs=[
            pl.BlockSpec(memory_space=pltpu.SMEM),
            per(length, wide),
            fixed((count, wide)),
            pl.BlockSpec((1, 1, length, width), lambda i: (0, i, 0, 0)),
            fixed((count, width)),
            per(1, length),
            fixed((width, width)),
            row, row, row,
        ],
        out_specs=(
            per(heads, length, length),
            per(length, width),
            per(length, width),
            per(length, width),
            per(length, width),
            per(length, LANES),
            per(length, width),
            per(ROW_TILE, length),
            fixed((count, 2 * width)),
            fixed((count, width)),
            fixed((count, LANES)),
        ),
        compiler_params=params(60),
        cost_estimate=MUCH,
        name="attention_forward",
    )(lengths, mixed, m0, x, x0, valid, wo, bo, gain, shift)


def turn(into_ref, from_ref):
    wide = from_ref.shape[1]
    tile = 384 if wide % 384 == 0 else LANES
    for column in range(0, wide, tile):
        into_ref[column : column + tile, :] = from_ref[:, column : column + tile].T


def grad_rows(place_ref, half, at_ref, right, outs, shards, start=0, size=None, offset=0):
    span = at_ref.shape[0] // shards
    size = size or span
    pitch = outs[0].shape[0] // (shards // 2)
    per = max(1, shards // 2)
    while per > 1 and per * size > 512:
        per //= 2
    for group in range(0, shards, per):
        pieces = []
        for shard in range(group, group + per):
            at = pl.multiple_of(place_ref[half, shard] * span + start, ROW_TILE)
            pieces.append(at_ref[pl.ds(at, size), :])
        left = pieces[0] if per == 1 else jnp.concatenate(pieces, axis=0)
        result = dot(left, right).astype(LOW)
        out_ref = outs[0] if group < shards // 2 else outs[1]
        for index in range(per):
            at = (group + index) % (shards // 2) * pitch + offset
            out_ref[at : at + size, :] = result[index * size : (index + 1) * size]


def cut_up(span):
    return -(-span // (2 * ROW_TILE)) * ROW_TILE


def feed_forward_kernel(
    place_ref, scal_ref, x_ref, we_ref, be_ref, wc_hbm, first_ref, bc_ref, g_ref, c_ref, cot_ref,
    slope_ref, out_ref, zg_ref, fg_ref, sums_ref, wg_ref, z0_ref, r0_ref, a0_ref, s0_ref,
    send0_ref, send1_ref, keep0_ref, keep1_ref,
    act_ref, wc_ref, feed_ref, low_ref, turned_ref, sem,
    *, chunks, tiles, shards,
):
    step = pl.program_id(0)
    length, width = first_ref.shape[1:]
    count = x_ref.shape[0] // length
    chunk = we_ref.shape[1]
    second = chunks + count + 1
    copy = pltpu.make_async_copy(wc_hbm, wc_ref, sem)

    @pl.when(step == 0)
    def _():
        copy.start()

    @pl.when(step < chunks)
    def _():
        u = dot(x_ref[...], we_ref[...]) + be_ref[...].astype(F32)
        active, slope = gelu_both(u)
        active = active.astype(LOW)
        act_ref[:, pl.ds(pl.multiple_of(step * chunk, LANES), chunk)] = active
        slope_ref[...] = slope.astype(LOW)
        for part in range(count):
            a0_ref[part : part + 1, :] = active[part * length : part * length + 1, :].astype(F32)
            s0_ref[part : part + 1, :] = slope[part * length : part * length + 1, :]

    def feed(seq):
        rows = pl.ds(pl.multiple_of(seq * length, ROW_TILE), length)
        feed_ref[lax.rem(seq, 2)] = dot(act_ref[rows, :], wc_ref[...])

    def norm(seq):
        weight = scal_ref[seq]
        keep = scal_ref[count]
        normal, root = norm_stats(first_ref[0] + feed_ref[lax.rem(seq, 2)] + bc_ref[...].astype(F32))
        gain = g_ref[...].astype(F32)
        result = normal * gain + c_ref[...].astype(F32)
        cot = cot_ref[0].astype(F32)
        out_ref[0] = weight * result
        put(wg_ref, seq, jnp.sum(cot * result, axis=0, keepdims=True))
        put(z0_ref, seq, normal[0:1, :])
        put(r0_ref, seq, jnp.broadcast_to(root[0:1, :], (1, LANES)))
        rows = lax.broadcasted_iota(jnp.int32, (length, 1), 0)
        grad = cot * jnp.where(rows == 0, weight * keep, weight)
        z_grad = norm_back(grad, gain, normal, root)
        zg_ref[0] = z_grad
        feed_grad = z_grad.astype(LOW)
        fg_ref[0] = feed_grad
        low_ref[pl.ds(pl.multiple_of(seq * length, ROW_TILE), length), :] = feed_grad
        sums_ref[0:1, :] += jnp.sum(grad * normal, axis=0, keepdims=True)
        sums_ref[1:2, :] += jnp.sum(grad, axis=0, keepdims=True)
        sums_ref[2:3, :] += jnp.sum(feed_grad.astype(F32), axis=0, keepdims=True)

    @pl.when(step == chunks)
    def _():
        copy.wait()
        sums_ref[...] = jnp.zeros(sums_ref.shape, F32)
        feed(0)

    @pl.when((step > chunks) & (step < second - 1))
    def _():
        feed(step - chunks)
        norm(step - chunks - 1)

    @pl.when(step == second - 1)
    def _():
        norm(count - 1)

    @pl.when(step == second)
    def _():
        turn(turned_ref, low_ref)

    def grads(half, send_ref, keep_ref):
        tile = send_ref.shape[1]
        columns = pl.ds(pl.multiple_of((step - second) * tile, LANES), tile)
        right = act_ref[:, columns]
        grad_rows(place_ref, half, turned_ref, right, (send_ref, keep_ref), shards)

    @pl.when((step >= second) & (step < second + tiles))
    def _():
        grads(0, send0_ref, keep0_ref)

    @pl.when(step >= second + tiles)
    def _():
        grads(1, send1_ref, keep1_ref)


def feed_forward(place, scal, x, first, we, be, wc, bc, gain, shift, cot, shards):
    count, length, width = first.shape
    rows = count * length
    hidden = we.shape[1]
    chunk = 1024
    chunks = hidden // chunk
    tile = 512
    tiles = hidden // 2 // tile
    second = chunks + count + 1

    def part(i):
        return jnp.minimum(i, chunks - 1)

    def seq(i):
        return jnp.clip(i - chunks - 1, 0, count - 1)

    def early(i):
        return (0, jnp.clip(i - second, 0, tiles - 1))

    def late(i):
        return (0, jnp.clip(i - second - tiles, 0, tiles - 1))

    def per(*shape):
        return pl.BlockSpec((1,) + shape, lambda i: (seq(i),) + (0,) * len(shape))

    row = fixed((1, width))
    cut = jax.ShapeDtypeStruct((width // 2, hidden // 2), LOW)
    block = (width // 2, tile)
    return pl.pallas_call(
        functools.partial(feed_forward_kernel, chunks=chunks, tiles=tiles, shards=shards),
        grid=(second + 2 * tiles,),
        out_shape=(
            jax.ShapeDtypeStruct((rows, hidden), LOW),
            jax.ShapeDtypeStruct((count, length, width), F32),
            jax.ShapeDtypeStruct((count, length, width), F32),
            jax.ShapeDtypeStruct((count, length, width), LOW),
            jax.ShapeDtypeStruct((8, width), F32),
            jax.ShapeDtypeStruct((count, width), F32),
            jax.ShapeDtypeStruct((count, width), F32),
            jax.ShapeDtypeStruct((count, LANES), F32),
            jax.ShapeDtypeStruct((count, hidden), F32),
            jax.ShapeDtypeStruct((count, hidden), F32),
            cut, cut, cut, cut,
        ),
        in_specs=[
            pl.BlockSpec(memory_space=pltpu.SMEM),
            pl.BlockSpec(memory_space=pltpu.SMEM),
            fixed((rows, width)),
            pl.BlockSpec((width, chunk), lambda i: (0, part(i))),
            pl.BlockSpec((1, chunk), lambda i: (0, part(i))),
            ANYWHERE,
            per(length, width),
            row, row, row,
            per(length, width),
        ],
        out_specs=(
            pl.BlockSpec((rows, chunk), lambda i: (0, part(i))),
            per(length, width),
            per(length, width),
            per(length, width),
            fixed((8, width)),
            fixed((count, width)),
            fixed((count, width)),
            fixed((count, LANES)),
            pl.BlockSpec((count, chunk), lambda i: (0, part(i))),
            pl.BlockSpec((count, chunk), lambda i: (0, part(i))),
            pl.BlockSpec(block, early),
            pl.BlockSpec(block, late),
            pl.BlockSpec(block, early),
            pl.BlockSpec(block, late),
        ),
        scratch_shapes=[
            pltpu.VMEM((rows, hidden), LOW),
            pltpu.VMEM((hidden, width), LOW),
            pltpu.VMEM((2, length, width), F32),
            pltpu.VMEM((rows, width), LOW),
            pltpu.VMEM((width, rows), LOW),
            pltpu.SemaphoreType.DMA,
        ],
        compiler_params=params(60),
        cost_estimate=MUCH,
        name="feed_forward",
    )(place, scal, x, we, be, wc, first, bc, gain, shift, cot)


def feed_backward_kernel(
    place_ref, fg_ref, slope_ref, wc_ref, we_hbm, zg_ref, normal_ref, root_ref, g_ref, x_ref,
    eb_ref, hgrad_ref, ag_ref, sums_ref, h0_ref,
    es0_ref, es1_ref, ek0_ref, ek1_ref,
    hg_ref, hidden_ref, we_ref, back_ref, sem,
    *, chunks, shards,
):
    step = pl.program_id(0)
    length, width = zg_ref.shape[1:]
    count = fg_ref.shape[0] // length
    chunk = slope_ref.shape[1]
    second = chunks + count + 1
    copy = pltpu.make_async_copy(we_hbm, we_ref, sem)

    @pl.when(step == 0)
    def _():
        copy.start()

    @pl.when(step < chunks)
    def _():
        grad = (dot_nt(fg_ref[...], wc_ref[...]) * slope_ref[...].astype(F32)).astype(LOW)
        at = pl.multiple_of(step * chunk, LANES)
        hg_ref[:, pl.ds(at, chunk)] = grad
        eb_ref[...] = jnp.sum(grad.astype(F32), axis=0, keepdims=True)
        hidden_ref[pl.ds(at, chunk), :] = grad.T

    def feed(seq):
        rows = pl.ds(pl.multiple_of(seq * length, ROW_TILE), length)
        back_ref[lax.rem(seq, 2)] = dot_nt(hg_ref[rows, :], we_ref[...])

    def norm(seq):
        grad = zg_ref[0] + back_ref[lax.rem(seq, 2)]
        normal = normal_ref[0].astype(F32)
        h_grad = norm_back(grad, g_ref[...].astype(F32), normal, root_ref[0, :, 0:1])
        hgrad_ref[0] = h_grad
        put(h0_ref, seq, h_grad[0:1, :])
        attended = h_grad.astype(LOW)
        ag_ref[0] = attended
        sums_ref[0:1, :] += jnp.sum(grad * normal, axis=0, keepdims=True)
        sums_ref[1:2, :] += jnp.sum(grad, axis=0, keepdims=True)
        sums_ref[2:3, :] += jnp.sum(attended.astype(F32), axis=0, keepdims=True)

    @pl.when(step == chunks)
    def _():
        copy.wait()
        sums_ref[...] = jnp.zeros(sums_ref.shape, F32)
        feed(0)

    @pl.when((step > chunks) & (step < second - 1))
    def _():
        feed(step - chunks)
        norm(step - chunks - 1)

    @pl.when(step == second - 1)
    def _():
        norm(count - 1)

    span = hidden_ref.shape[0] // shards
    first = cut_up(span)
    for half, outs, start, size in (
        (0, (es0_ref, ek0_ref), 0, first), (1, (es1_ref, ek1_ref), first, span - first)
    ):

        @pl.when(step == second + half)
        def _():
            grad_rows(place_ref, half, hidden_ref, x_ref[...], outs, shards, start, size)


def feed_backward(place, fg, slope, wc, we, zg, normal, root, gain, x, shards):
    count, length, width = zg.shape
    rows, hidden = slope.shape
    chunk = 1024
    chunks = hidden // chunk

    def part(i):
        return jnp.minimum(i, chunks - 1)

    def seq(i):
        return jnp.clip(i - chunks - 1, 0, count - 1)

    def per(*shape):
        return pl.BlockSpec((1,) + shape, lambda i: (seq(i),) + (0,) * len(shape))

    rows_of = [cut_up(hidden // shards), hidden // shards - cut_up(hidden // shards)] * 2
    cuts = [(shards // 2 * size, width) for size in rows_of]
    return pl.pallas_call(
        functools.partial(feed_backward_kernel, chunks=chunks, shards=shards),
        grid=(chunks + count + 3,),
        out_shape=(
            jax.ShapeDtypeStruct((1, hidden), F32),
            jax.ShapeDtypeStruct((count, length, width), F32),
            jax.ShapeDtypeStruct((count, length, width), LOW),
            jax.ShapeDtypeStruct((8, width), F32),
            jax.ShapeDtypeStruct((count, width), F32),
        )
        + tuple(jax.ShapeDtypeStruct(cut, LOW) for cut in cuts),
        in_specs=[
            pl.BlockSpec(memory_space=pltpu.SMEM),
            fixed((rows, width)),
            pl.BlockSpec((rows, chunk), lambda i: (0, part(i))),
            pl.BlockSpec((chunk, width), lambda i: (part(i), 0)),
            ANYWHERE,
            per(length, width),
            per(length, width),
            per(length, LANES),
            fixed((1, width)),
            fixed((rows, width)),
        ],
        out_specs=(
            pl.BlockSpec((1, chunk), lambda i: (0, part(i))),
            per(length, width),
            per(length, width),
            fixed((8, width)),
            fixed((count, width)),
        )
        + tuple(fixed(cut) for cut in cuts),
        scratch_shapes=[
            pltpu.VMEM((rows, hidden), LOW),
            pltpu.VMEM((hidden, rows), LOW),
            pltpu.VMEM((width, hidden), LOW),
            pltpu.VMEM((2, length, width), F32),
            pltpu.SemaphoreType.DMA,
        ],
        compiler_params=params(60),
        cost_estimate=MUCH,
        name="feed_backward",
    )(place, fg, slope, wc, we, zg, normal, root, gain, x)


def attention_backward_kernel(len_ref, ag_ref, wo_ref, p_ref, mixed_ref, m0_ref, *refs):
    mg_ref, mg0_ref, sums_ref, dctx_ref = refs[-4:]
    step = pl.program_id(0)
    width = ag_ref.shape[2]

    @pl.when(step == 0)
    def _():
        sums_ref[...] = jnp.zeros(sums_ref.shape, F32)

    dctx_ref[...] = dot_nt(ag_ref[0], wo_ref[...]).astype(LOW)
    lane = lax.broadcasted_iota(jnp.int32, (1, LANES), 1)
    length = ag_ref.shape[1]

    def heads(keys):
        for pair in range(width // LANES):
            query, key, value = pair_of(mixed_ref, m0_ref, pair, width, step)
            grad = dctx_ref[:, pl.ds(pair * LANES, LANES)]
            grads = []
            for half in range(2):
                mask = jnp.where(lane // HD == half, 1.0, 0.0).astype(LOW)
                chance_low = p_ref[0, 2 * pair + half, :, 0:keys]
                chance = chance_low.astype(F32)
                p_grad = dot_nt(grad * mask, value[:keys])
                inner = jnp.sum(p_grad * chance, axis=-1, keepdims=True)
                s_grad = (chance * (p_grad - inner)).astype(LOW)
                grads.append((dot(s_grad, key[:keys]), dot_tn(s_grad, query), dot_tn(chance_low, grad)))
            for which in range(3):
                both = jnp.where(lane < HD, grads[0][which], grads[1][which])
                if which < 2:
                    both = both * SCALE
                columns = pl.ds(which * width + pair * LANES, LANES)
                low = both.astype(LOW)
                mg_ref[0, 0 : low.shape[0], columns] = low
                if low.shape[0] < length:
                    mg_ref[0, low.shape[0] :, columns] = jnp.zeros((length - low.shape[0], LANES), LOW)
                put(mg0_ref, step, low[0:1, :].astype(F32), columns)
                if which != 1:
                    here = slice(pair * LANES, (pair + 1) * LANES)
                    sums_ref[which // 2 : which // 2 + 1, here] += jnp.sum(low.astype(F32), axis=0, keepdims=True)

    short = short_keys(length)

    @pl.when(len_ref[step] <= short)
    def _():
        heads(short)

    @pl.when(len_ref[step] > short)
    def _():
        heads(length)


def attention_backward(lengths, ag, wo, p, mixed, m0, after):
    count, length, wide = mixed.shape
    width = wide // 3
    heads = width // HD

    def per(*shape):
        return pl.BlockSpec((1,) + shape, lambda i: (i,) + (0,) * len(shape))

    return pl.pallas_call(
        attention_backward_kernel,
        grid=(count,),
        out_shape=(
            jax.ShapeDtypeStruct((count, length, wide), LOW),
            jax.ShapeDtypeStruct((count, wide), F32),
            jax.ShapeDtypeStruct((8, width), F32),
        ),
        in_specs=[
            pl.BlockSpec(memory_space=pltpu.SMEM),
            per(length, width),
            fixed((width, width)),
            per(heads, length, length),
            per(length, wide),
            fixed((count, wide)),
        ]
        + [ANYWHERE] * len(after),
        out_specs=(per(length, wide), fixed((count, wide)), fixed((8, width))),
        scratch_shapes=[pltpu.VMEM((length, width), LOW)],
        compiler_params=params(60),
        cost_estimate=MUCH,
        name="attention_backward",
    )(lengths, ag, wo, p, mixed, m0, *after)


def attention_grads_kernel(place_ref, mg_ref, ag_ref, x_ref, ctx_ref, mg0_ref, h0_ref, wi_hbm, *refs, shards):
    s0_ref, s1_ref, k0_ref, k1_ref, term_ref, turned_ref, other_ref, wi_ref, sem = refs[-9:]
    step = pl.program_id(0)
    copy = pltpu.make_async_copy(wi_hbm, wi_ref, sem)

    @pl.when(step == 0)
    def _():
        copy.start()

    @pl.when(step == 1)
    def _():
        copy.wait()
        term_ref[...] = h0_ref[...] + dot_nt(mg0_ref[...].astype(LOW), wi_ref[...])

    @pl.when(step == 0)
    def _():
        turn(turned_ref, mg_ref)
        turn(other_ref, ag_ref)

    span, other = turned_ref.shape[0] // shards, other_ref.shape[0] // shards
    first, last = cut_up(span), other - cut_up(other)
    for half, outs, in_rows, out_rows in (
        (0, (s0_ref, k0_ref), (0, first), (0, last)),
        (1, (s1_ref, k1_ref), (first, span - first), (last, other - last)),
    ):

        @pl.when(step == half)
        def _():
            grad_rows(place_ref, half, turned_ref, x_ref[...], outs, shards, *in_rows)
            grad_rows(place_ref, half, other_ref, ctx_ref[...], outs, shards, *out_rows, in_rows[1])


def attention_grads(place, mg, ag, x, ctx, mg0, h0, wi, after, shards):
    rows, wide = mg.shape
    width = wide // 3
    first = cut_up(wide // shards) + width // shards - cut_up(width // shards)
    cuts = [(shards // 2 * size, width) for size in (first, (wide + width) // shards - first)] * 2
    return pl.pallas_call(
        functools.partial(attention_grads_kernel, shards=shards),
        grid=(2,),
        out_shape=tuple(jax.ShapeDtypeStruct(cut, LOW) for cut in cuts) + (jax.ShapeDtypeStruct(h0.shape, F32),),
        in_specs=[
            pl.BlockSpec(memory_space=pltpu.SMEM),
            fixed((rows, wide)),
            fixed((rows, width)),
            fixed((rows, width)),
            fixed((rows, width)),
            fixed(mg0.shape),
            fixed(h0.shape),
            ANYWHERE,
        ]
        + [ANYWHERE] * len(after),
        out_specs=tuple(fixed(cut) for cut in cuts) + (fixed(h0.shape),),
        scratch_shapes=[
            pltpu.VMEM((wide, rows), LOW),
            pltpu.VMEM((width, rows), LOW),
            pltpu.VMEM(wi.shape, LOW),
            pltpu.SemaphoreType.DMA,
        ],
        compiler_params=params(60),
        cost_estimate=MUCH,
        name="attention_grads",
    )(place, mg, ag, x, ctx, mg0, h0, wi, *after)


def shard_groups(count, wide):
    span = wide // count
    first = [span * shard // HD for shard in range(count)]
    most = max((span * shard + span - 1) // HD - first[shard] + 1 for shard in range(count))
    return [min(one, wide // HD - most) for one in first], most


def input_grad_kernel(mg_ref, w_ref, hgrad_ref, sg_ref, p0_ref, fk_ref, fv_ref, fq_ref, *refs):
    out_ref = refs[-1]
    seq = pl.program_id(0)
    length, width = hgrad_ref.shape[1:]
    rows = lax.broadcasted_iota(jnp.int32, (length, 1), 0)
    back = dot_nt(mg_ref[0], w_ref[...]) + dot_tn(sg_ref[0], fk_ref[0]) + dot_tn(p0_ref[0], fv_ref[0])
    out_ref[0] = back + hgrad_ref[0] + jnp.where(rows == 0, pick(fq_ref, seq), 0.0)


def input_grad(mg, weight, hgrad, sg, p0, fk, fv, fq, after):
    count, length, wide = mg.shape
    width = wide // 3

    def per(*shape):
        return pl.BlockSpec((1,) + shape, lambda i: (i,) + (0,) * len(shape))

    return pl.pallas_call(
        input_grad_kernel,
        grid=(count,),
        out_shape=jax.ShapeDtypeStruct((count, length, width), F32),
        in_specs=[
            per(length, wide),
            fixed((width, wide)),
            per(length, width),
            per(ROW_TILE, length),
            per(ROW_TILE, length),
            per(ROW_TILE, width),
            per(ROW_TILE, width),
            fixed((count, width)),
        ]
        + [ANYWHERE] * len(after),
        out_specs=per(length, width),
        compiler_params=params(60),
        cost_estimate=MUCH,
        name="input_grad",
    )(mg, weight, hgrad, sg, p0, fk, fv, fq, *after)


def last_kernel(
    g0_ref, z0_ref, r2_ref, g2_ref, slope_ref, wc_ref, we_ref, n0_ref, r1_ref, g1_ref, wo_ref, wi_hbm,
    p0_ref, mixed_ref, m0_ref, x_ref, s2_ref, s1_ref, s0_ref, eb_ref, act_ref, early_ref, emb_ref, summary_ref, *refs, groups
):
    (
        sg_ref, fk_ref, fv_ref, fq_ref, send_ref,
        fg_ref, ag_ref, hg_ref, eball_ref, coef_ref, sums_ref, pack_ref,
        zg_ref, acc_ref, hz_ref, dctx_ref, rows_ref, wi_ref, sem,
    ) = refs[-19:]
    step = pl.program_id(0)
    count, width = g0_ref.shape
    chunks = pl.num_programs(0) - count
    copy = pltpu.make_async_copy(wi_hbm, wi_ref, sem)

    @pl.when(step == 0)
    def _():
        copy.start()
        grad = g0_ref[...]
        z_grad = norm_back(grad, g2_ref[...].astype(F32), z0_ref[...], r2_ref[:, 0:1])
        zg_ref[...] = z_grad
        low = z_grad.astype(LOW)
        fg_ref[...] = low
        sums_ref[0:2, :] = s0_ref[0:2, :]
        sums_ref[6:7, :] = s2_ref[0:1, :] + jnp.sum(grad * z0_ref[...], axis=0, keepdims=True)
        sums_ref[7:8, :] = s2_ref[1:2, :] + jnp.sum(grad, axis=0, keepdims=True)
        sums_ref[5:6, :] = s2_ref[2:3, :] + jnp.sum(low.astype(F32), axis=0, keepdims=True)
        acc_ref[...] = jnp.zeros(acc_ref.shape, F32)

    @pl.when(step < chunks)
    def _():
        grad = (dot_nt(fg_ref[...], wc_ref[...]) * slope_ref[...].astype(F32)).astype(LOW)
        here = pl.ds(pl.multiple_of(step * wc_ref.shape[0], LANES), wc_ref.shape[0])
        hg_ref[:, here] = grad.astype(F32)
        eball_ref[0:1, here] = eb_ref[...] + jnp.sum(grad.astype(F32), axis=0, keepdims=True)
        acc_ref[...] += dot_nt(grad, we_ref[...])

    @pl.when(step == chunks - 1)
    def _():
        grad = zg_ref[...] + acc_ref[...]
        normal = n0_ref[...]
        h_grad = norm_back(grad, g1_ref[...].astype(F32), normal, r1_ref[:, 0:1])
        hz_ref[0:count, :] = h_grad
        low = h_grad.astype(LOW)
        ag_ref[...] = low.astype(F32)
        sums_ref[3:4, :] = s1_ref[0:1, :] + jnp.sum(grad * normal, axis=0, keepdims=True)
        sums_ref[4:5, :] = s1_ref[1:2, :] + jnp.sum(grad, axis=0, keepdims=True)
        sums_ref[2:3, :] = s1_ref[2:3, :] + jnp.sum(low.astype(F32), axis=0, keepdims=True)
        dctx_ref[0:count, :] = dot_nt(low, wo_ref[...])
        copy.wait()

    @pl.when(step >= chunks)
    def _():
        seq = step - chunks
        heads = head_rows(width)
        own = dctx_ref[pl.ds(seq, 1), :]
        grad = jnp.where(heads, own, 0.0).astype(LOW)
        query0 = pick(m0_ref, seq, slice(0, width))
        query = jnp.where(heads, query0, 0.0).astype(LOW)
        key = with_first(mixed_ref[0, :, width : 2 * width], pick(m0_ref, seq, slice(width, 2 * width)))
        value = with_first(mixed_ref[0, :, 2 * width :], pick(m0_ref, seq, slice(2 * width, 3 * width)))
        chance_low = p0_ref[0]
        chance = chance_low.astype(F32)
        p_grad = dot_nt(grad, value)
        s_grad = (chance * (p_grad - jnp.sum(p_grad * chance, axis=-1, keepdims=True))).astype(LOW)
        dq = dot(s_grad, key)
        dq = jnp.sum(jnp.where(heads, dq, 0.0), axis=0, keepdims=True) * SCALE
        put(coef_ref, seq, dq, slice(0, width))
        put(coef_ref, seq, query0 * SCALE, slice(width, 2 * width))
        put(coef_ref, seq, own, slice(2 * width, 3 * width))
        inputs = x_ref[0]
        rows_ref[0, 0:1, :] = inputs[0:1, :].astype(F32)
        rows_ref[1] = dot(s_grad, inputs)
        rows_ref[2] = dot(chance_low, inputs)
        firsts, most = groups
        per = width // HD
        for shard, first in enumerate(firsts):
            for turn_of in range(most):
                which, head = divmod(first + turn_of, per)
                head = head if which else 0
                at = pl.ds(count + seq * most + turn_of, 1)
                pack_ref[shard, at, 0:width] = rows_ref[which, head : head + 1, :]
        sg_ref[0] = s_grad
        fk_ref[0] = (dot_nt(query, wi_ref[:, width : 2 * width]) * SCALE).astype(LOW)
        fv_ref[0] = dot_nt(grad, wi_ref[:, 2 * width :]).astype(LOW)
        from_query = dot_nt(jnp.where(heads, dq, 0.0).astype(LOW), wi_ref[:, 0:width])
        put(fq_ref, seq, jnp.sum(from_query, axis=0, keepdims=True) + hz_ref[pl.ds(seq, 1), :])
        sums_ref[0:1, :] += dq
        held = jnp.sum(chance, axis=-1, keepdims=True)
        sums_ref[1:2, :] += jnp.sum(held * grad.astype(F32), axis=0, keepdims=True)

    @pl.when(step == pl.num_programs(0) - 1)
    def _():
        firsts, most = groups
        shards = len(firsts)
        starts, pitch, begin = parcel(count, shards, width, eball_ref.shape[1], most, emb_ref.shape[1])
        for shard in range(shards):
            for name, source in (("feed", fg_ref), ("attended", ag_ref), ("hidden", hg_ref), ("coef", coef_ref)):
                span = source.shape[1] // shards
                piece = source[:, shard * span : (shard + 1) * span].astype(F32)
                pack_ref[shard, 0:count, starts[name] : starts[name] + span] = piece
            pack_ref[shard, 0:count, starts["emb"] : starts["emb"] + emb_ref.shape[1]] = emb_ref[...].astype(F32)
            span = width // shards
            at = starts["vectors"]
            pack_ref[shard, count : count + 8, at : at + span] = sums_ref[:, shard * span : (shard + 1) * span]
            span = eball_ref.shape[1] // shards
            for line, column in enumerate(range(0, span, LANES)):
                size = min(LANES, span - column)
                piece = eball_ref[0:1, shard * span + column : shard * span + column + size]
                pack_ref[shard, count + 8 + line : count + 9 + line, at : at + size] = piece
            send_ref[shard, 0:begin, :] = pack_ref[shard, 0:begin, :].astype(LOW)
        flat = [(act_ref, act_ref.shape[1]), (early_ref, 2 * width), (summary_ref, width)]
        for seq in range(count):
            at = 0
            for source, size in flat:
                done = 0
                while done < size:
                    line, column = divmod(at, pitch)
                    piece = min(size - done, pitch - column)
                    value = source[seq : seq + 1, done : done + piece].astype(F32)
                    where = begin + seq * 6 + line
                    pack_ref[0, where : where + 1, column : column + piece] = value
                    done += piece
                    at += piece
        early = pack_ref[0, begin : begin + 6 * count, :].astype(LOW)
        for shard in range(shards):
            send_ref[shard, begin : begin + 6 * count, :] = early


def parcel(count, shards, width, hidden, most, emb):
    starts, at = {}, 0
    for name, span in (
        ("feed", width // shards), ("attended", width // shards), ("hidden", hidden // shards),
        ("coef", 3 * width // shards), ("emb", emb),
    ):
        starts[name] = at
        at += -(-span // LANES) * LANES
    starts["vectors"] = width
    pitch = max(at, width + LANES)
    return starts, pitch, -(-(count + max(most * count, 8 + -(-hidden // shards // LANES))) // 8) * 8


def last_rows(
    g0, z0, r2, g2, slope0, wc, we, n0, r1, g1, wo, wi, p0, mixed, m0, x, s2, s1, s0, eb, act, early, emb, summary, after, shards
):
    count, length, wide = mixed.shape
    width = wide // 3
    hidden = slope0.shape[1]
    chunk = 768
    chunks = hidden // chunk
    groups = shard_groups(shards, wide)
    _, pitch, begin = parcel(count, shards, width, hidden, groups[1], emb.shape[1])
    send = (shards, begin + 6 * count, pitch)

    def part(i):
        return jnp.minimum(i, chunks - 1)

    def seq(i):
        return jnp.maximum(i - chunks, 0)

    def per(*shape):
        return pl.BlockSpec((1,) + shape, lambda i: (seq(i),) + (0,) * len(shape))

    row = fixed((1, width))
    rows = fixed((count, width))
    return pl.pallas_call(
        functools.partial(last_kernel, groups=groups),
        grid=(chunks + count,),
        out_shape=(
            jax.ShapeDtypeStruct((count, ROW_TILE, length), LOW),
            jax.ShapeDtypeStruct((count, ROW_TILE, width), LOW),
            jax.ShapeDtypeStruct((count, ROW_TILE, width), LOW),
            jax.ShapeDtypeStruct((count, width), F32),
            jax.ShapeDtypeStruct(send, LOW),
        ),
        in_specs=[
            rows, rows, fixed((count, LANES)), row,
            pl.BlockSpec((count, chunk), lambda i: (0, part(i))),
            pl.BlockSpec((chunk, width), lambda i: (part(i), 0)),
            pl.BlockSpec((width, chunk), lambda i: (0, part(i))),
            rows, fixed((count, LANES)), row,
            fixed((width, width)),
            ANYWHERE,
            per(ROW_TILE, length),
            per(length, wide),
            fixed((count, wide)),
            per(length, width),
            fixed((8, width)),
            fixed((8, width)),
            fixed((8, width)),
            pl.BlockSpec((1, chunk), lambda i: (0, part(i))),
            fixed(act.shape),
            fixed(early.shape),
            fixed(emb.shape),
            fixed(summary.shape),
        ]
        + [ANYWHERE] * len(after),
        out_specs=(
            per(ROW_TILE, length),
            per(ROW_TILE, width),
            per(ROW_TILE, width),
            rows,
            fixed(send),
        ),
        scratch_shapes=[
            pltpu.VMEM((count, width), LOW),
            pltpu.VMEM((count, width), F32),
            pltpu.VMEM((count, hidden), F32),
            pltpu.VMEM((8, hidden), F32),
            pltpu.VMEM((count, wide), F32),
            pltpu.VMEM((8, width), F32),
            pltpu.VMEM(send, F32),
            pltpu.VMEM((count, width), F32),
            pltpu.VMEM((count, width), F32),
            pltpu.VMEM((8, width), F32),
            pltpu.VMEM((8, width), F32),
            pltpu.VMEM((3, ROW_TILE, width), F32),
            pltpu.VMEM((width, wide), LOW),
            pltpu.SemaphoreType.DMA,
        ],
        compiler_params=params(60),
        cost_estimate=LITTLE,
        name="last_rows",
    )(g0, z0, r2, g2, slope0, wc, we, n0, r1, g1, wo, wi, p0, mixed, m0, x, s2, s1, s0, eb, act, early, emb, summary, *after)


def flip(value, bit, count):
    return lax.ppermute(value, "rows", [(i, i ^ bit) for i in range(count)])


BITS = ((1, 2), (2, 1))


def first_stage(parts, count):
    return [flip(parts[half], BITS[half][0], count) for half in range(2)]


def second_stage(sends, count):
    return [flip(sends[half], BITS[half][1], count) for half in range(2)]


def sum_low(left_ref, right_ref):
    return (left_ref[...].astype(F32) + right_ref[...].astype(F32)).astype(LOW)


def first_sum_kernel(a0, a1, b0, b1, ga0, ga1, gb0, gb1, *refs):
    sa, sb, ka, kb = refs[-4:]
    sa[...] = sum_low(a0, ga0)
    ka[...] = sum_low(a1, ga1)
    sb[...] = sum_low(b0, gb0)
    kb[...] = sum_low(b1, gb1)


def first_sum(parts, got, after):
    keep0, keep1 = parts[2:]
    rows, width = keep0.shape
    tiles = 4
    block = (rows // 2 // tiles, width)
    top = pl.BlockSpec(block, lambda i: (i, 0))
    bottom = pl.BlockSpec(block, lambda i: (i + tiles, 0))
    result = pl.pallas_call(
        first_sum_kernel,
        grid=(tiles,),
        out_shape=(jax.ShapeDtypeStruct((rows // 2, width), LOW),) * 4,
        in_specs=[top, bottom] * 4 + [ANYWHERE] * len(after),
        out_specs=(top,) * 4,
        compiler_params=params(60),
        cost_estimate=LITTLE,
        name="first_sum",
    )(keep0, keep0, keep1, keep1, got[0], got[0], got[1], got[1], *after)
    return result[:2], result[2:]


def second_sum_kernel(a, b, ga, gb, *refs, apart, stacked):
    step = pl.program_id(0)
    rows, half = a.shape
    left, right = sum_low(a, ga), sum_low(b, gb)
    for index, out in enumerate(refs[-2 if apart else -4 :]):

        @pl.when(step // 2 == index if apart else step == index)
        def _():
            if stacked:
                out[:rows, :] = left
                out[rows:, :] = right
            else:
                out[:, :half] = left
                out[:, half:] = right


def second_sum(keeps, got, after, apart, stacked):
    rows, width = keeps[0].shape
    tile = rows // 4
    block = pl.BlockSpec((tile, width), lambda i: (i, 0))
    wide, out_tile = (width, 2 * tile) if stacked else (2 * width, tile)
    if apart:
        shapes = (jax.ShapeDtypeStruct((2 * out_tile, wide), LOW),) * 2
        places_out = (
            pl.BlockSpec((out_tile, wide), lambda i: (jnp.minimum(i, 1), 0)),
            pl.BlockSpec((out_tile, wide), lambda i: (jnp.maximum(i - 2, 0), 0)),
        )
    else:
        shapes = (jax.ShapeDtypeStruct((out_tile, wide), LOW),) * 4
        places_out = (fixed((out_tile, wide)),) * 4
    return pl.pallas_call(
        functools.partial(second_sum_kernel, apart=apart, stacked=stacked),
        grid=(4,),
        out_shape=shapes,
        in_specs=[block] * 4 + [ANYWHERE] * len(after),
        out_specs=places_out,
        compiler_params=params(60),
        cost_estimate=LITTLE,
        name="second_sum",
    )(keeps[0], keeps[1], got[0], got[1], *after)


def third_sum_kernel(a, ga, *refs):
    for index, out in enumerate(refs[-2:]):

        @pl.when(pl.program_id(0) == index)
        def _():
            out[...] = sum_low(a, ga)


def third_sum(keep, got, after, weighs):
    rows, width = keep.shape
    block = pl.BlockSpec((rows // 2, width), lambda i: (i, 0))
    shape = (rows // 2, width)
    return pl.pallas_call(
        third_sum_kernel,
        grid=(2,),
        out_shape=(jax.ShapeDtypeStruct(shape, LOW),) * 2,
        in_specs=[block] * 2 + [ANYWHERE] * len(after),
        out_specs=(fixed(shape),) * 2,
        compiler_params=params(60),
        cost_estimate=weighs,
        name="third_sum",
    )(keep, got, *after)


def wide_sum(left, right):
    return left.astype(F32) + right.astype(F32)


def line_stage(totals, count):
    got = [totals[0]]
    for step in range(1, count // 4):
        got.append(lax.ppermute(totals[step], "rows", [(i, (i + 4 * step) % count) for i in range(count)]))
    return got


def places(count):
    me = lax.axis_index("rows")
    apart, in_order = [], []
    for first, second in BITS:
        corners = [me ^ one ^ two for one in (first, 0) for two in (second, 0)]
        apart.append(jnp.stack([corner ^ turn for corner in corners for turn in (12, 4, 8, 0)]))
        in_order.append(jnp.stack([(corner + 4 * step) % count for corner in corners for step in range(count // 4)]))
    return jnp.stack(apart).astype(jnp.int32), jnp.stack(in_order).astype(jnp.int32)


def rest_kernel(*refs):
    *got, fix_ref, in_ref, out_ref = refs
    span, other = in_ref.shape[0], out_ref.shape[0]
    first, last = cut_up(span), other - cut_up(other)
    total = got[0][...].astype(F32)
    for one in got[1:]:
        total = total + one[...].astype(F32)
    for into, start, size, at in (
        (in_ref, 0, first, 0),
        (out_ref, 0, last, first),
        (in_ref, first, span - first, first + last),
        (out_ref, last, other - last, span + last),
    ):
        add = start + (span if into is out_ref else 0)
        into[start : start + size, :] = total[at : at + size] + fix_ref[add : add + size, :]


def rest_sum(got, fix, span):
    rows, width = fix.shape
    return pl.pallas_call(
        rest_kernel,
        out_shape=(jax.ShapeDtypeStruct((span, width), F32), jax.ShapeDtypeStruct((rows - span, width), F32)),
        compiler_params=params(60),
        name="rest_sum",
    )(*got, fix)


def whole_grad(full):
    return lax.psum_scatter(full.astype(F32), "rows", scatter_dimension=0, tiled=True)


def body(
    token_states, lengths, key_mask, cotangent, attention_in, attention_bias, attention_out, output_bias,
    gain_one, shift_one, expand_weight, expand_bias, contract_weight, contract_bias, gain_two, shift_two,
    projection, passage_table, candidates,
):
    section = lax.axis_index("section")
    is_first = section == 0
    count = lax.axis_size("rows")
    me = lax.axis_index("rows")
    tokens = token_states[0]
    seqs, length, width = tokens.shape
    rows = seqs * length

    bi = attention_bias[0]
    wi, wo, we, wc = attention_in[0], attention_out[0], expand_weight[0], contract_weight[0]
    bo, g1, c1, be, bc, g2, c2 = output_bias, gain_one, shift_one, expand_bias, contract_bias, gain_two, shift_two
    weights = (wi, bi, wo, bo, g1, c1, we, be, wc, bc, g2, c2)
    positions = jnp.arange(length)
    valid = (positions[None, :] < lengths[0][:, None]) & (key_mask[0] == 1) | (positions[None, :] == 0)
    valid = valid.astype(F32)[:, None, :]
    staged = count == 16 and width // count % ROW_TILE == 0
    cuts = count if staged else 2
    place, place_line = places(count) if staged else (jnp.asarray([[0, 1], [0, 1]], jnp.int32),) * 2

    retrieved = jnp.take(passage_table, candidates, axis=0).astype(F32)
    mixed, x0 = project(token_states, wi, bi)
    message = first_rows(mixed, valid, x0, weights, projection)
    received = lax.ppermute(message, "section", [(0, 1)])
    summary_in, embedding_in = received[:, :width], received[:, width:]
    x0 = x0 + summary_in.astype(F32)
    in_bias = jnp.concatenate([bi[0], jnp.zeros_like(bi[0]), bi[1]])
    mixed0 = (dot(x0.astype(LOW), wi) + in_bias.astype(F32)).astype(LOW).astype(F32)
    chance, context, first, first_low, normal, root, x_low, chance0, early, n0, r1 = attention_forward(
        lengths[0], mixed, mixed0, token_states, x0, valid, wo, bo, g1, c1
    )
    match = jnp.sum(embedding_in.astype(F32)[:, None, :] * retrieved, axis=-1)
    chances = jax.nn.softmax(match, axis=-1)
    weight = TOPK * chances[:, 0]
    scal = jnp.concatenate([jnp.where(is_first, 1.0, weight), jnp.where(is_first, 0.0, 1.0)[None]]).astype(F32)
    first_flat = first_low.reshape(rows, width)
    slope, out, z_grad, feed_grad, sums_two, weight_grads, z0, r2, active0, slope0, *contract = feed_forward(
        place, scal, first_flat, first, we, be, wc, bc, g2, c2, cotangent[0], cuts
    )

    contract_got = first_stage(contract, count) if staged else None
    expand_sum, h_grad, attended, sums_one, h0, *expand = feed_backward(
        place, feed_grad.reshape(rows, width), slope, wc, we, z_grad, normal, root, g1, first_flat, cuts
    )
    contract_send = ()
    if staged:
        contract_send, contract_keep = first_sum(contract, contract_got, (h0,))
        contract_got = second_stage(contract_send, count)
        expand_got = first_stage(expand, count)
    mixed_grad, mg0, sums_in = attention_backward(lengths[0], attended, wo, chance, mixed, mixed0, tuple(contract_send))
    after = ()
    if staged:
        contract_send, contract_keep = second_sum(contract_keep, contract_got, (mg0,), True, False)
        contract_got = flip(contract_send, 4, count)
        expand_send, expand_keep = first_sum(expand, expand_got, (mg0,))
        expand_got = second_stage(expand_send, count)
        after = (contract_send, expand_send[0])
    *rest, reader_term = attention_grads(
        place_line, mixed_grad.reshape(rows, 3 * width), attended.reshape(rows, width), x_low.reshape(rows, width),
        context.reshape(rows, width), mg0, h0, wi, after, cuts,
    )
    rest_got = first_stage(rest, count) if staged else None

    after = (rest[0],)
    if staged:
        expand_send, expand_keep = second_sum(expand_keep, expand_got, (rest[0],), True, True)
        expand_got = flip(expand_send, 4, count)
        after = (expand_send,)
    grad_weight = jnp.sum(weight_grads, axis=1)
    one = jnp.zeros((TOPK,), F32).at[0].set(1.0)
    grad_match = (grad_weight[:, None] * weight[:, None] * (one[None, :] - chances)).astype(LOW)
    embedding_grad = jnp.sum(grad_match.astype(F32)[:, :, None] * retrieved, axis=1).astype(LOW)
    if staged:
        reader_term, _ = lax.optimization_barrier((reader_term, expand_send))
    reader_term = reader_term.astype(LOW)
    back = lax.ppermute(jnp.concatenate([reader_term, embedding_grad], axis=1), "section", [(1, 0)])
    embedding_used = jnp.where(is_first, back[:, width:], embedding_grad)
    summary_grad = dot_nt(back[:, width:], projection) + back[:, :width].astype(F32)
    grad_zero = jnp.where(is_first, cotangent[0, :, 0, :].astype(F32) + summary_grad, 0.0)
    used_summary = jnp.where(is_first, message[:, :width], summary_in)
    s_zero, from_key, from_value, from_query, parcels = last_rows(
        grad_zero, z0, r2, g2, slope0, wc, we, n0, r1, g1, wo, wi, chance0, mixed, mixed0, x_low,
        sums_two, sums_one, sums_in, expand_sum, active0, early, embedding_used, used_summary, after, count,
    )
    after = ()
    if staged:
        rest_send, rest_keep = first_sum(rest, rest_got, (parcels,))
        rest_got = second_stage(rest_send, count)
        after = (rest_send[0],)

    got = lax.all_to_all(parcels, "rows", 0, 0, tiled=True)
    if staged:
        contract_send, contract_keep = third_sum(contract_keep, contract_got, after, MUCH)
        contract_got = flip(contract_send, 8, count)
        expand_send, expand_keep = third_sum(expand_keep, expand_got, (contract_send,), LITTLE)
        expand_got = flip(expand_send, 8, count)
        rest = second_sum(rest_keep, rest_got, (expand_send,), False, True)
        rest_got = line_stage(rest, count)
        after = (rest[0],)
    x_grad = input_grad(mixed_grad, wi, h_grad, s_zero, chance0, from_key, from_value, from_query, after)
    if staged:
        got, _ = lax.optimization_barrier((got, x_grad))
    else:
        top, bottom = jnp.concatenate(contract[:2], axis=1), jnp.concatenate(contract[2:], axis=1)
        contract = whole_grad(jnp.concatenate([top, bottom], axis=0))
        expand = whole_grad(jnp.concatenate(expand, axis=0))
        inner = 3 * width // 4
        rest = [jnp.concatenate([part[cut] for part in rest]) for cut in (slice(0, inner), slice(inner, None))]
        rest = [whole_grad(part) for part in rest]
    hidden = we.shape[1]
    span = 3 * width // count
    firsts, most = shard_groups(count, 3 * width)
    starts, pitch, begin = parcel(seqs, count, width, hidden, most, embedding_used.shape[1])

    def sent(name, size):
        return got[:, :seqs, starts[name] : starts[name] + size].reshape(count * seqs, size)

    factors = got[:, begin:].reshape(count * seqs, 6 * pitch)
    active_all, first_all = factors[:, :hidden], factors[:, hidden : hidden + width]
    context_all = factors[:, hidden + width : hidden + 2 * width]
    summary_all = factors[:, hidden + 2 * width : hidden + 3 * width]
    contract_fix = dot_tn(sent("feed", width // count), active_all)
    projection_grad = dot_tn(summary_all, sent("emb", embedding_used.shape[1]))
    head = (span * me + jnp.arange(span)) // HD - jnp.asarray(firsts, jnp.int32)[me]
    chosen = (head[None, :] == jnp.arange(most)[:, None]).astype(LOW)
    coefs = (sent("coef", span)[:, None, :] * chosen[None]).reshape(count * seqs * most, span)
    groups = got[:, seqs : seqs + seqs * most, :width].reshape(count * seqs * most, width)
    fix = jnp.concatenate([dot_tn(coefs, groups), dot_tn(sent("attended", width // count), context_all)], axis=0)
    expand_fix = dot_tn(sent("hidden", hidden // count), first_all)
    at = starts["vectors"]
    packed = jnp.sum(got[:, seqs : seqs + 8, at : at + width // count].astype(F32), axis=0)
    lines = -(-hidden // count // LANES)
    e_bias = got[:, seqs + 8 : seqs + 8 + lines, at : at + LANES].astype(F32)
    e_bias = jnp.sum(e_bias, axis=0).reshape(-1)[: hidden // count]
    if staged:
        held = (contract_got, expand_got, rest_got, fix, contract_fix, expand_fix, projection_grad, packed, e_bias)
        contract_got, expand_got, rest_got, fix, contract_fix, expand_fix, projection_grad, packed, e_bias = (
            lax.optimization_barrier(held)
        )
        contract = contract_fix + wide_sum(contract_keep, contract_got)
        expand = wide_sum(expand_keep, expand_got)
        attention_in_grad, attention_out_grad = rest_sum(rest_got, fix, span)
    else:
        contract = contract + contract_fix
        attention_in_grad, attention_out_grad = rest[0] + fix[:span], rest[1] + fix[span:]
    expand = expand + expand_fix
    q_bias, v_bias, o_bias, gain1, shift1, c_bias, gain2, shift2 = (packed[i] for i in range(8))
    return (
        out[None],
        x_grad[None],
        attention_in_grad.T[None],
        jnp.stack([q_bias, v_bias])[None],
        attention_out_grad.T[None],
        o_bias[None],
        gain1[None],
        shift1[None],
        expand.T[None],
        e_bias[None],
        contract.T[None],
        c_bias[None],
        gain2[None],
        shift2[None],
        projection_grad,
    )


def solution(mesh):
    in_specs = (
        P("section", "rows", None, None),
        P("section", "rows"),
        P("section", "rows", None),
        P("section", "rows", None, None),
        P("section", None, None),
        P("section", None, None),
        P("section", None, None),
        P("section", None),
        P("section", None),
        P("section", None),
        P("section", None, None),
        P("section", None),
        P("section", None, None),
        P("section", None),
        P("section", None),
        P("section", None),
        P(),
        P(),
        P("rows", None),
    )
    out_specs = (
        P("section", "rows", None, None),
        P("section", "rows", None, None),
        P("section", None, "rows"),
        P("section", None, "rows"),
        P("section", None, "rows"),
        P("section", "rows"),
        P("section", "rows"),
        P("section", "rows"),
        P("section", None, "rows"),
        P("section", "rows"),
        P("section", None, "rows"),
        P("section", "rows"),
        P("section", "rows"),
        P("section", "rows"),
        P(),
    )
    return jax.shard_map(body, mesh=mesh, in_specs=in_specs, out_specs=out_specs, check_vma=False)
```

```python
import functools
import math

import jax
import jax.numpy as jnp
from jax import lax
from jax.experimental import pallas as pl
from jax.experimental.pallas import tpu as pltpu
from jax.sharding import PartitionSpec as P

HD = 64
TOPK = 8
NEGATIVE = -1000000000.0
SCALE = 1.0 / math.sqrt(HD)
LANES = 128
ROW_TILE = 16
F32 = jnp.float32
LOW = jnp.bfloat16
NT = (((1,), (1,)), ((), ()))
TN = (((0,), (0,)), ((), ()))
MIB = 1 << 20
BITS = ((1, 2), (2, 1))


def dot(left, right):
    return jnp.dot(left, right, preferred_element_type=F32)


def dot_nt(left, right):
    return lax.dot_general(left, right, NT, preferred_element_type=F32)


def dot_tn(left, right):
    return lax.dot_general(left, right, TN, preferred_element_type=F32)


def params(limit):
    return pltpu.CompilerParams(vmem_limit_bytes=limit * MIB)


MUCH = pl.CostEstimate(flops=100 * 1000**3, bytes_accessed=50 * MIB, transcendentals=0)
LITTLE = pl.CostEstimate(flops=1, bytes_accessed=1, transcendentals=0)


ANYWHERE = pl.BlockSpec(memory_space=pl.ANY)


def fixed(shape):
    return pl.BlockSpec(shape, lambda *ids: (0,) * len(shape), pipeline_mode=pl.Buffered(1))


def norm_stats(hidden):
    mean = jnp.mean(hidden, axis=-1, keepdims=True)
    centered = hidden - mean
    root = lax.rsqrt(jnp.mean(centered * centered, axis=-1, keepdims=True) + 1e-12)
    return centered * root, root


def norm_back(grad, gain, normal, root):
    scaled = gain * grad
    mean = jnp.mean(scaled, axis=-1, keepdims=True)
    along = jnp.mean(scaled * normal, axis=-1, keepdims=True)
    return root * (scaled - mean - normal * along)


def gelu_both(u):
    phi = 0.5 + 0.5 * lax.erf(u * (1.0 / math.sqrt(2.0)))
    slope = phi + u * (jnp.exp(-0.5 * u * u) * (1.0 / math.sqrt(2.0 * math.pi)))
    return u * phi, slope


def head_rows(width):
    shape = (ROW_TILE, width)
    return lax.broadcasted_iota(jnp.int32, shape, 1) // HD == lax.broadcasted_iota(jnp.int32, shape, 0)


def pick(ref, row, columns=slice(None)):
    block = ref[:, columns]
    rows = lax.broadcasted_iota(jnp.int32, (block.shape[0], 1), 0)
    return jnp.sum(jnp.where(rows == row, block, 0.0), axis=0, keepdims=True)


def put(ref, row, value, columns=slice(None)):
    block = ref[:, columns]
    rows = lax.broadcasted_iota(jnp.int32, (block.shape[0], 1), 0)
    ref[:, columns] = jnp.where(rows == row, value, block)


def project_kernel(x_ref, w_ref, b_ref, o_ref, x0_ref):
    step = pl.program_id(0)
    bias = b_ref[...].astype(F32)
    bias = jnp.where(step == 0, bias[0:1, :], jnp.where(step == 2, bias[1:2, :], 0.0))
    for part in range(x_ref.shape[1]):
        o_ref[part] = (dot(x_ref[0, part], w_ref[...]) + bias).astype(LOW)
        x0_ref[part : part + 1, :] = x_ref[0, part, 0:1, :].astype(F32)


def project(x, weight, bias):
    _, count, length, width = x.shape
    return pl.pallas_call(
        project_kernel,
        grid=(3,),
        out_shape=(
            jax.ShapeDtypeStruct((count, length, 3 * width), LOW),
            jax.ShapeDtypeStruct((count, width), F32),
        ),
        in_specs=[
            fixed((1, count, length, width)),
            pl.BlockSpec((width, width), lambda i: (0, i)),
            fixed((2, width)),
        ],
        out_specs=(pl.BlockSpec((count, length, width), lambda i: (0, 0, i)), fixed((count, width))),
        compiler_params=params(32),
        cost_estimate=pl.CostEstimate(flops=6 * count * length * width * width, bytes_accessed=14 * MIB, transcendentals=0),
        name="project_qkv",
    )(x, weight, bias)


def first_rows_kernel(
    mixed_ref, valid_ref, x0_ref, wo_ref, bo_ref, g1_ref, c1_ref, we_ref, be_ref, wc_ref, bc_ref,
    g2_ref, c2_ref, pr_ref, out_ref, ctx_ref, first_ref, acc_ref,
):
    step = pl.program_id(0)
    count = x0_ref.shape[0]
    width = wo_ref.shape[0]
    chunks = pl.num_programs(0) - count

    @pl.when(step < count)
    def _():
        heads = head_rows(width)
        query = mixed_ref[0, 0:1, 0:width].astype(F32) * SCALE
        spread = jnp.where(heads, query, 0.0).astype(LOW)
        scores = dot_nt(spread, mixed_ref[0, :, width : 2 * width])
        scores = jnp.where(valid_ref[0] > 0, scores, NEGATIVE)
        exponent = jnp.exp(scores - jnp.max(scores, axis=-1, keepdims=True))
        chance = (exponent / jnp.sum(exponent, axis=-1, keepdims=True)).astype(LOW)
        context = dot(chance, mixed_ref[0, :, 2 * width :])
        context = jnp.sum(jnp.where(heads, context, 0.0), axis=0, keepdims=True)
        ctx_ref[pl.ds(step, 1), :] = context

    @pl.when(step == count - 1)
    def _():
        hidden = x0_ref[...] + dot(ctx_ref[0:count, :].astype(LOW), wo_ref[...]) + bo_ref[...].astype(F32)
        normal, root = norm_stats(hidden)
        first_ref[...] = normal * g1_ref[...].astype(F32) + c1_ref[...].astype(F32)

    @pl.when(step >= count)
    def _():
        u = dot(first_ref[...].astype(LOW), we_ref[...]) + be_ref[...].astype(F32)
        active, slope = gelu_both(u)
        part = dot(active.astype(LOW), wc_ref[...])

        @pl.when(step == count)
        def _():
            acc_ref[...] = part

        @pl.when(step > count)
        def _():
            acc_ref[...] += part

    @pl.when(step == pl.num_programs(0) - 1)
    def _():
        normal, root = norm_stats(first_ref[...] + acc_ref[...] + bc_ref[...].astype(F32))
        summary = (normal * g2_ref[...].astype(F32) + c2_ref[...].astype(F32)).astype(LOW)
        out_ref[:, 0:width] = summary
        out_ref[:, width:] = dot(summary, pr_ref[...]).astype(LOW)


def first_rows(mixed, valid, x0, weights, projection):
    (_, _, wo, bo, g1, c1, we, be, wc, bc, g2, c2) = weights
    count, length, wide = mixed.shape
    width, hidden = we.shape
    chunk = 768
    chunks = hidden // chunk
    proj = projection.shape[1]

    def seq(i):
        return jnp.minimum(i, count - 1)

    def part(i):
        return jnp.maximum(i - count, 0)

    row = fixed((1, width))
    return pl.pallas_call(
        first_rows_kernel,
        grid=(count + chunks,),
        out_shape=jax.ShapeDtypeStruct((count, width + proj), LOW),
        in_specs=[
            pl.BlockSpec((1, length, wide), lambda i: (seq(i), 0, 0)),
            pl.BlockSpec((1, 1, length), lambda i: (seq(i), 0, 0)),
            fixed((count, width)),
            fixed((width, width)),
            row, row, row,
            pl.BlockSpec((width, chunk), lambda i: (0, part(i))),
            pl.BlockSpec((1, chunk), lambda i: (0, part(i))),
            pl.BlockSpec((chunk, width), lambda i: (part(i), 0)),
            row, row, row,
            fixed((width, proj)),
        ],
        out_specs=fixed((count, width + proj)),
        scratch_shapes=[
            pltpu.VMEM((8, width), F32),
            pltpu.VMEM((count, width), F32),
            pltpu.VMEM((count, width), F32),
        ],
        compiler_params=params(32),
        cost_estimate=pl.CostEstimate(flops=40 * MIB, bytes_accessed=17 * MIB, transcendentals=0),
        name="first_rows_forward",
    )(mixed, valid, x0, wo, bo, g1, c1, we, be, wc, bc, g2, c2, projection)


def with_first(block, row):
    rows = lax.broadcasted_iota(jnp.int32, (ROW_TILE, 1), 0)
    top = jnp.where(rows == 0, row, block[0:ROW_TILE].astype(F32)).astype(block.dtype)
    return jnp.concatenate([top, block[ROW_TILE:]], axis=0)


def pair_of(mixed_ref, m0_ref, pair, width, seq):
    found = []
    for which in range(3):
        columns = pl.ds(which * width + pair * LANES, LANES)
        found.append(with_first(mixed_ref[0, :, columns], pick(m0_ref, seq, columns)))
    return found


def over_lanes(value, lanes):
    parts = [value] * (lanes // LANES) + ([value[:, : lanes % LANES]] if lanes % LANES else [])
    return jnp.concatenate(parts, axis=1)


def short_keys(length):
    return (length - 1) // LANES * LANES


def attention_forward_kernel(
    len_ref, mixed_ref, m0_ref, x_ref, x0_ref, valid_ref, wo_ref, bo_ref, g_ref, c_ref,
    p_ref, ctx_ref, first_ref, low_ref, normal_ref, root_ref, xlow_ref, p0_ref, early_ref, n0_ref, r0_ref,
):
    seq = pl.program_id(0)
    length, width = x_ref.shape[2:]
    valid = valid_ref[0] > 0
    lane = lax.broadcasted_iota(jnp.int32, (1, LANES), 1)
    p0_ref[0] = jnp.zeros(p0_ref.shape[1:], LOW)

    def heads(keys):
        ones = jnp.ones((keys, LANES), LOW)
        for pair in range(width // LANES):
            query, key, value = pair_of(mixed_ref, m0_ref, pair, width, seq)
            right = jnp.concatenate([value[:keys], ones], axis=1)
            results = []
            for half in range(2):
                mask = jnp.where(lane // HD == half, SCALE, 0.0).astype(LOW)
                scores = dot_nt(query * mask, key[:keys])
                scores = jnp.where(valid[:, :keys], scores, NEGATIVE)
                exponent = jnp.exp(scores - jnp.max(scores, axis=-1, keepdims=True))
                both = dot(exponent.astype(LOW), right)
                share = 1.0 / both[:, LANES:]
                results.append(both[:, :LANES] * share)
                chance = (exponent * over_lanes(share, keys)).astype(LOW)
                p_ref[0, 2 * pair + half, :, 0:keys] = chance
                p0_ref[0, 2 * pair + half : 2 * pair + half + 1, 0:keys] = chance[0:1, :]
            ctx_ref[0, :, pl.ds(pair * LANES, LANES)] = jnp.where(lane < HD, results[0], results[1]).astype(LOW)

    short = short_keys(length)

    @pl.when(len_ref[seq] <= short)
    def _():
        heads(short)

    @pl.when(len_ref[seq] > short)
    def _():
        heads(length)

    rows = lax.broadcasted_iota(jnp.int32, (length, 1), 0)
    inputs = jnp.where(rows == 0, pick(x0_ref, seq), x_ref[0, 0].astype(F32))
    xlow_ref[0] = inputs.astype(LOW)
    hidden = inputs + dot(ctx_ref[0], wo_ref[...]) + bo_ref[...].astype(F32)
    normal, root = norm_stats(hidden)
    first = normal * g_ref[...].astype(F32) + c_ref[...].astype(F32)
    first_ref[0] = first
    low_ref[0] = first.astype(LOW)
    normal_ref[0] = normal.astype(LOW)
    root_ref[0] = jnp.broadcast_to(root, root_ref.shape[1:])
    put(early_ref, seq, first[0:1, :], slice(0, width))
    put(early_ref, seq, ctx_ref[0, 0:1, :].astype(F32), slice(width, 2 * width))
    put(n0_ref, seq, normal[0:1, :])
    put(r0_ref, seq, jnp.broadcast_to(root[0:1, :], (1, LANES)))


def attention_forward(lengths, mixed, m0, x, x0, valid, wo, bo, gain, shift):
    count, length, wide = mixed.shape
    width = wide // 3
    heads = width // HD

    def per(*shape):
        return pl.BlockSpec((1,) + shape, lambda i: (i,) + (0,) * len(shape))

    row = fixed((1, width))
    return pl.pallas_call(
        attention_forward_kernel,
        grid=(count,),
        out_shape=(
            jax.ShapeDtypeStruct((count, heads, length, length), LOW),
            jax.ShapeDtypeStruct((count, length, width), LOW),
            jax.ShapeDtypeStruct((count, length, width), F32),
            jax.ShapeDtypeStruct((count, length, width), LOW),
            jax.ShapeDtypeStruct((count, length, width), LOW),
            jax.ShapeDtypeStruct((count, length, LANES), F32),
            jax.ShapeDtypeStruct((count, length, width), LOW),
            jax.ShapeDtypeStruct((count, ROW_TILE, length), LOW),
            jax.ShapeDtypeStruct((count, 2 * width), F32),
            jax.ShapeDtypeStruct((count, width), F32),
            jax.ShapeDtypeStruct((count, LANES), F32),
        ),
        in_specs=[
            pl.BlockSpec(memory_space=pltpu.SMEM),
            per(length, wide),
            fixed((count, wide)),
            pl.BlockSpec((1, 1, length, width), lambda i: (0, i, 0, 0)),
            fixed((count, width)),
            per(1, length),
            fixed((width, width)),
            row, row, row,
        ],
        out_specs=(
            per(heads, length, length),
            per(length, width),
            per(length, width),
            per(length, width),
            per(length, width),
            per(length, LANES),
            per(length, width),
            per(ROW_TILE, length),
            fixed((count, 2 * width)),
            fixed((count, width)),
            fixed((count, LANES)),
        ),
        compiler_params=params(60),
        cost_estimate=MUCH,
        name="attention_forward",
    )(lengths, mixed, m0, x, x0, valid, wo, bo, gain, shift)


def turn(into_ref, from_ref):
    wide = from_ref.shape[1]
    tile = 384 if wide % 384 == 0 else LANES
    for column in range(0, wide, tile):
        into_ref[column : column + tile, :] = from_ref[:, column : column + tile].T


def grad_rows(me_ref, half, at_ref, right, outs, shards, line, start=0, size=None, offset=0):
    span = at_ref.shape[0] // shards
    size = size or span
    pitch = outs[0].shape[0] // (shards // 2)
    per = max(1, shards // 2)
    while per > 1 and per * size > 512:
        per //= 2
    for group in range(0, shards, per):
        pieces = []
        for shard in range(group, group + per):
            at = pl.multiple_of(shard_at(me_ref[0], half, shard, shards, line) * span + start, ROW_TILE)
            pieces.append(at_ref[pl.ds(at, size), :])
        left = pieces[0] if per == 1 else jnp.concatenate(pieces, axis=0)
        result = dot(left, right).astype(LOW)
        out_ref = outs[0] if group < shards // 2 else outs[1]
        for index in range(per):
            at = (group + index) % (shards // 2) * pitch + offset
            out_ref[at : at + size, :] = result[index * size : (index + 1) * size]


def shard_at(me, half, place, shards, line):
    if shards != 16:
        return place
    first, second = BITS[half]
    corner = me ^ (0 if place & 8 else first) ^ (0 if place & 4 else second)
    return lax.rem(corner + 4 * (place & 3), shards) if line else corner ^ (12, 4, 8, 0)[place & 3]


def cut_up(span):
    return -(-span // (2 * ROW_TILE)) * ROW_TILE


def feed_forward_kernel(
    me_ref, scal_ref, x_ref, we_ref, be_ref, wc_hbm, first_ref, bc_ref, g_ref, c_ref, cot_ref,
    slope_ref, out_ref, zg_ref, fg_ref, sums_ref, wg_ref, z0_ref, r0_ref, cot0_ref, s0_ref,
    send0_ref, send1_ref, keep0_ref, keep1_ref,
    act_ref, wc_ref, feed_ref, low_ref, turned_ref, sem,
    *, chunks, tiles, shards,
):
    step = pl.program_id(0)
    length, width = first_ref.shape[1:]
    count = x_ref.shape[0] // length
    group = first_ref.shape[0]
    groups = count // group
    chunk = we_ref.shape[1]
    second = chunks + groups + 1
    copy = pltpu.make_async_copy(wc_hbm, wc_ref, sem)

    @pl.when(step == 0)
    def _():
        copy.start()

    @pl.when(step < chunks)
    def _():
        u = dot(x_ref[...], we_ref[...]) + be_ref[...].astype(F32)
        active, slope = gelu_both(u)
        active = active.astype(LOW)
        act_ref[:, pl.ds(pl.multiple_of(step * chunk, LANES), chunk)] = active
        slope_ref[...] = slope.astype(LOW)
        for part in range(count):
            s0_ref[part : part + 1, :] = slope[part * length : part * length + 1, :]

    def feed(seq):
        rows = pl.ds(pl.multiple_of(seq * group * length, ROW_TILE), group * length)
        feed_ref[lax.rem(seq, 2)] = dot(act_ref[rows, :], wc_ref[...])

    def norms(at):
        for one in range(group):
            norm(at, one)

    def norm(at, one):
        seq = at * group + one
        weight = scal_ref[seq]
        keep = scal_ref[count]
        normal, root = norm_stats(
            first_ref[one] + feed_ref[lax.rem(at, 2), one * length : (one + 1) * length, :] + bc_ref[...].astype(F32)
        )
        gain = g_ref[...].astype(F32)
        result = normal * gain + c_ref[...].astype(F32)
        cot = cot_ref[one].astype(F32)
        out_ref[one] = weight * result
        put(wg_ref, seq, jnp.sum(cot * result, axis=0, keepdims=True))
        put(z0_ref, seq, normal[0:1, :])
        put(cot0_ref, seq, cot[0:1, :])
        put(r0_ref, seq, jnp.broadcast_to(root[0:1, :], (1, LANES)))
        rows = lax.broadcasted_iota(jnp.int32, (length, 1), 0)
        grad = cot * jnp.where(rows == 0, weight * keep, weight)
        z_grad = norm_back(grad, gain, normal, root)
        zg_ref[one] = z_grad
        feed_grad = z_grad.astype(LOW)
        fg_ref[one] = feed_grad
        low_ref[pl.ds(pl.multiple_of(seq * length, ROW_TILE), length), :] = feed_grad
        sums_ref[0:1, :] += jnp.sum(grad * normal, axis=0, keepdims=True)
        sums_ref[1:2, :] += jnp.sum(grad, axis=0, keepdims=True)
        sums_ref[2:3, :] += jnp.sum(feed_grad.astype(F32), axis=0, keepdims=True)

    @pl.when(step == chunks)
    def _():
        copy.wait()
        sums_ref[...] = jnp.zeros(sums_ref.shape, F32)
        feed(0)

    @pl.when((step > chunks) & (step < second - 1))
    def _():
        feed(step - chunks)
        norms(step - chunks - 1)

    @pl.when(step == second - 1)
    def _():
        norms(groups - 1)

    @pl.when(step == second)
    def _():
        turn(turned_ref, low_ref)

    def grads(half, send_ref, keep_ref):
        tile = send_ref.shape[1]
        columns = pl.ds(pl.multiple_of((step - second) * tile, LANES), tile)
        right = act_ref[:, columns]
        grad_rows(me_ref, half, turned_ref, right, (send_ref, keep_ref), shards, False)

    @pl.when((step >= second) & (step < second + tiles))
    def _():
        grads(0, send0_ref, keep0_ref)

    @pl.when(step >= second + tiles)
    def _():
        grads(1, send1_ref, keep1_ref)


def feed_forward(me, scal, x, first, we, be, wc, bc, gain, shift, cot, shards):
    count, length, width = first.shape
    rows = count * length
    hidden = we.shape[1]
    chunk = 1024
    chunks = hidden // chunk
    tile = 512
    tiles = hidden // 2 // tile
    second = chunks + 1 + count // (2 if count % 2 == 0 else 1)

    group = 2 if count % 2 == 0 else 1
    groups = count // group

    def part(i):
        return jnp.minimum(i, chunks - 1)

    def seq(i):
        return jnp.clip(i - chunks - 1, 0, groups - 1)

    def early(i):
        return (0, jnp.clip(i - second, 0, tiles - 1))

    def late(i):
        return (0, jnp.clip(i - second - tiles, 0, tiles - 1))

    def per(*shape):
        return pl.BlockSpec((group,) + shape, lambda i: (seq(i),) + (0,) * len(shape))

    row = fixed((1, width))
    cut = jax.ShapeDtypeStruct((width // 2, hidden // 2), LOW)
    block = (width // 2, tile)
    return pl.pallas_call(
        functools.partial(feed_forward_kernel, chunks=chunks, tiles=tiles, shards=shards),
        grid=(second + 2 * tiles,),
        out_shape=(
            jax.ShapeDtypeStruct((rows, hidden), LOW),
            jax.ShapeDtypeStruct((count, length, width), F32),
            jax.ShapeDtypeStruct((count, length, width), F32),
            jax.ShapeDtypeStruct((count, length, width), LOW),
            jax.ShapeDtypeStruct((8, width), F32),
            jax.ShapeDtypeStruct((count, width), F32),
            jax.ShapeDtypeStruct((count, width), F32),
            jax.ShapeDtypeStruct((count, LANES), F32),
            jax.ShapeDtypeStruct((count, width), F32),
            jax.ShapeDtypeStruct((count, hidden), F32),
            cut, cut, cut, cut,
        ),
        in_specs=[
            pl.BlockSpec(memory_space=pltpu.SMEM),
            pl.BlockSpec(memory_space=pltpu.SMEM),
            fixed((rows, width)),
            pl.BlockSpec((width, chunk), lambda i: (0, part(i))),
            pl.BlockSpec((1, chunk), lambda i: (0, part(i))),
            ANYWHERE,
            per(length, width),
            row, row, row,
            per(length, width),
        ],
        out_specs=(
            pl.BlockSpec((rows, chunk), lambda i: (0, part(i))),
            per(length, width),
            per(length, width),
            per(length, width),
            fixed((8, width)),
            fixed((count, width)),
            fixed((count, width)),
            fixed((count, LANES)),
            fixed((count, width)),
            pl.BlockSpec((count, chunk), lambda i: (0, part(i))),
            pl.BlockSpec(block, early),
            pl.BlockSpec(block, late),
            pl.BlockSpec(block, early),
            pl.BlockSpec(block, late),
        ),
        scratch_shapes=[
            pltpu.VMEM((rows, hidden), LOW),
            pltpu.VMEM((hidden, width), LOW),
            pltpu.VMEM((2, group * length, width), F32),
            pltpu.VMEM((rows, width), LOW),
            pltpu.VMEM((width, rows), LOW),
            pltpu.SemaphoreType.DMA,
        ],
        compiler_params=params(60),
        cost_estimate=MUCH,
        name="feed_forward",
    )(me, scal, x, we, be, wc, first, bc, gain, shift, cot)


def feed_backward_kernel(
    me_ref, fg_ref, slope_ref, wc_ref, we_hbm, zg_ref, normal_ref, root_ref, g_ref, x_ref,
    eb_ref, hgrad_ref, ag_ref, sums_ref, h0_ref,
    es0_ref, es1_ref, ek0_ref, ek1_ref,
    hg_ref, hidden_ref, we_ref, back_ref, sem,
    *, chunks, shards,
):
    step = pl.program_id(0)
    length, width = zg_ref.shape[1:]
    count = fg_ref.shape[0] // length
    group = zg_ref.shape[0]
    groups = count // group
    chunk = slope_ref.shape[1]
    second = chunks + groups + 1
    copy = pltpu.make_async_copy(we_hbm, we_ref, sem)

    @pl.when(step == 0)
    def _():
        copy.start()

    @pl.when(step < chunks)
    def _():
        grad = (dot_nt(fg_ref[...], wc_ref[...]) * slope_ref[...].astype(F32)).astype(LOW)
        at = pl.multiple_of(step * chunk, LANES)
        hg_ref[:, pl.ds(at, chunk)] = grad
        eb_ref[...] = jnp.sum(grad.astype(F32), axis=0, keepdims=True)
        hidden_ref[pl.ds(at, chunk), :] = grad.T

    def feed(seq):
        rows = pl.ds(pl.multiple_of(seq * group * length, ROW_TILE), group * length)
        back_ref[lax.rem(seq, 2)] = dot_nt(hg_ref[rows, :], we_ref[...])

    def norms(at):
        for one in range(group):
            norm(at, one)

    def norm(at, one):
        seq = at * group + one
        grad = zg_ref[one] + back_ref[lax.rem(at, 2), one * length : (one + 1) * length, :]
        normal = normal_ref[one].astype(F32)
        h_grad = norm_back(grad, g_ref[...].astype(F32), normal, root_ref[one, :, 0:1])
        hgrad_ref[one] = h_grad
        put(h0_ref, seq, h_grad[0:1, :])
        attended = h_grad.astype(LOW)
        ag_ref[one] = attended
        sums_ref[0:1, :] += jnp.sum(grad * normal, axis=0, keepdims=True)
        sums_ref[1:2, :] += jnp.sum(grad, axis=0, keepdims=True)
        sums_ref[2:3, :] += jnp.sum(attended.astype(F32), axis=0, keepdims=True)

    @pl.when(step == chunks)
    def _():
        copy.wait()
        sums_ref[...] = jnp.zeros(sums_ref.shape, F32)
        feed(0)

    @pl.when((step > chunks) & (step < second - 1))
    def _():
        feed(step - chunks)
        norms(step - chunks - 1)

    @pl.when(step == second - 1)
    def _():
        norms(groups - 1)

    span = hidden_ref.shape[0] // shards
    first = cut_up(span)
    for half, outs, start, size in (
        (0, (es0_ref, ek0_ref), 0, first), (1, (es1_ref, ek1_ref), first, span - first)
    ):

        @pl.when(step == second + half)
        def _():
            grad_rows(me_ref, half, hidden_ref, x_ref[...], outs, shards, False, start, size)


def feed_backward(me, fg, slope, wc, we, zg, normal, root, gain, x, shards):
    count, length, width = zg.shape
    rows, hidden = slope.shape
    chunk = 1024
    chunks = hidden // chunk

    group = 2 if count % 2 == 0 else 1
    groups = count // group

    def part(i):
        return jnp.minimum(i, chunks - 1)

    def seq(i):
        return jnp.clip(i - chunks - 1, 0, groups - 1)

    def per(*shape):
        return pl.BlockSpec((group,) + shape, lambda i: (seq(i),) + (0,) * len(shape))

    rows_of = [cut_up(hidden // shards), hidden // shards - cut_up(hidden // shards)] * 2
    cuts = [(shards // 2 * size, width) for size in rows_of]
    return pl.pallas_call(
        functools.partial(feed_backward_kernel, chunks=chunks, shards=shards),
        grid=(chunks + groups + 3,),
        out_shape=(
            jax.ShapeDtypeStruct((1, hidden), F32),
            jax.ShapeDtypeStruct((count, length, width), F32),
            jax.ShapeDtypeStruct((count, length, width), LOW),
            jax.ShapeDtypeStruct((8, width), F32),
            jax.ShapeDtypeStruct((count, width), F32),
        )
        + tuple(jax.ShapeDtypeStruct(cut, LOW) for cut in cuts),
        in_specs=[
            pl.BlockSpec(memory_space=pltpu.SMEM),
            fixed((rows, width)),
            pl.BlockSpec((rows, chunk), lambda i: (0, part(i))),
            pl.BlockSpec((chunk, width), lambda i: (part(i), 0)),
            ANYWHERE,
            per(length, width),
            per(length, width),
            per(length, LANES),
            fixed((1, width)),
            fixed((rows, width)),
        ],
        out_specs=(
            pl.BlockSpec((1, chunk), lambda i: (0, part(i))),
            per(length, width),
            per(length, width),
            fixed((8, width)),
            fixed((count, width)),
        )
        + tuple(fixed(cut) for cut in cuts),
        scratch_shapes=[
            pltpu.VMEM((rows, hidden), LOW),
            pltpu.VMEM((hidden, rows), LOW),
            pltpu.VMEM((width, hidden), LOW),
            pltpu.VMEM((2, group * length, width), F32),
            pltpu.SemaphoreType.DMA,
        ],
        compiler_params=params(60),
        cost_estimate=MUCH,
        name="feed_backward",
    )(me, fg, slope, wc, we, zg, normal, root, gain, x)


def attention_backward_kernel(len_ref, ag_ref, wo_ref, p_ref, mixed_ref, m0_ref, ctx_ref, *refs):
    mg_ref, mg0_ref, sums_ref, dctx_ref = refs[-4:]
    step = pl.program_id(0)
    width = ag_ref.shape[2]

    @pl.when(step == 0)
    def _():
        sums_ref[...] = jnp.zeros(sums_ref.shape, F32)

    dctx_ref[...] = dot_nt(ag_ref[0], wo_ref[...]).astype(LOW)
    lane = lax.broadcasted_iota(jnp.int32, (1, LANES), 1)
    length = ag_ref.shape[1]

    def heads(keys):
        minus = jnp.full((keys, LANES), -1.0, LOW)
        for pair in range(width // LANES):
            query, key, value = pair_of(mixed_ref, m0_ref, pair, width, step)
            here = pl.ds(pair * LANES, LANES)
            grad = dctx_ref[:, here]
            left = jnp.concatenate([grad, grad * ctx_ref[0, :, here]], axis=1)
            right = jnp.concatenate([value[:keys], minus], axis=1)
            queries, turned_s, turned_p = [], [], []
            for half in range(2):
                mask = jnp.where(lane // HD == half, 1.0, 0.0).astype(LOW)
                chance = p_ref[0, 2 * pair + half, :, 0:keys]
                less = dot_nt(left * jnp.concatenate([mask, mask], axis=1), right)
                s_grad = (chance.astype(F32) * less).astype(LOW)
                queries.append(dot(s_grad, key[:keys]))
                turned_s.append(s_grad.T)
                turned_p.append(chance.T)
            keys_grad = dot(jnp.concatenate(turned_s, axis=0), query) * SCALE
            values_grad = dot(jnp.concatenate(turned_p, axis=0), grad)
            for which, (one, two) in enumerate(
                (
                    (queries[0] * SCALE, queries[1] * SCALE),
                    (keys_grad[:keys], keys_grad[keys:]),
                    (values_grad[:keys], values_grad[keys:]),
                )
            ):
                low = jnp.where(lane < HD, one, two).astype(LOW)
                columns = pl.ds(which * width + pair * LANES, LANES)
                mg_ref[0, 0 : low.shape[0], columns] = low
                if low.shape[0] < length:
                    mg_ref[0, low.shape[0] :, columns] = jnp.zeros((length - low.shape[0], LANES), LOW)
                put(mg0_ref, step, low[0:1, :].astype(F32), columns)
                if which != 1:
                    spot = slice(pair * LANES, (pair + 1) * LANES)
                    sums_ref[which // 2 : which // 2 + 1, spot] += jnp.sum(low.astype(F32), axis=0, keepdims=True)

    short = short_keys(length)

    @pl.when(len_ref[step] <= short)
    def _():
        heads(short)

    @pl.when(len_ref[step] > short)
    def _():
        heads(length)


def attention_backward(lengths, ag, wo, p, mixed, m0, ctx, after):
    count, length, wide = mixed.shape
    width = wide // 3
    heads = width // HD

    def per(*shape):
        return pl.BlockSpec((1,) + shape, lambda i: (i,) + (0,) * len(shape))

    return pl.pallas_call(
        attention_backward_kernel,
        grid=(count,),
        out_shape=(
            jax.ShapeDtypeStruct((count, length, wide), LOW),
            jax.ShapeDtypeStruct((count, wide), F32),
            jax.ShapeDtypeStruct((8, width), F32),
        ),
        in_specs=[
            pl.BlockSpec(memory_space=pltpu.SMEM),
            per(length, width),
            fixed((width, width)),
            per(heads, length, length),
            per(length, wide),
            fixed((count, wide)),
            per(length, width),
        ]
        + [ANYWHERE] * len(after),
        out_specs=(per(length, wide), fixed((count, wide)), fixed((8, width))),
        scratch_shapes=[pltpu.VMEM((length, width), LOW)],
        compiler_params=params(60),
        cost_estimate=MUCH,
        name="attention_backward",
    )(lengths, ag, wo, p, mixed, m0, ctx, *after)


def attention_grads_kernel(me_ref, mg_ref, ag_ref, x_ref, ctx_ref, mg0_ref, h0_ref, wi_hbm, *refs, shards):
    s0_ref, s1_ref, k0_ref, k1_ref, term_ref, turned_ref, other_ref, wi_ref, sem = refs[-9:]
    step = pl.program_id(0)
    copy = pltpu.make_async_copy(wi_hbm, wi_ref, sem)

    @pl.when(step == 0)
    def _():
        copy.start()

    @pl.when(step == 1)
    def _():
        copy.wait()
        term_ref[...] = h0_ref[...] + dot_nt(mg0_ref[...].astype(LOW), wi_ref[...])

    @pl.when(step == 0)
    def _():
        turn(turned_ref, mg_ref)
        turn(other_ref, ag_ref)

    span, other = turned_ref.shape[0] // shards, other_ref.shape[0] // shards
    first, last = cut_up(span), other - cut_up(other)
    for half, outs, in_rows, out_rows in (
        (0, (s0_ref, k0_ref), (0, first), (0, last)),
        (1, (s1_ref, k1_ref), (first, span - first), (last, other - last)),
    ):

        @pl.when(step == half)
        def _():
            grad_rows(me_ref, half, turned_ref, x_ref[...], outs, shards, True, *in_rows)
            grad_rows(me_ref, half, other_ref, ctx_ref[...], outs, shards, True, *out_rows, in_rows[1])


def attention_grads(me, mg, ag, x, ctx, mg0, h0, wi, after, shards):
    rows, wide = mg.shape
    width = wide // 3
    first = cut_up(wide // shards) + width // shards - cut_up(width // shards)
    cuts = [(shards // 2 * size, width) for size in (first, (wide + width) // shards - first)] * 2
    return pl.pallas_call(
        functools.partial(attention_grads_kernel, shards=shards),
        grid=(2,),
        out_shape=tuple(jax.ShapeDtypeStruct(cut, LOW) for cut in cuts) + (jax.ShapeDtypeStruct(h0.shape, F32),),
        in_specs=[
            pl.BlockSpec(memory_space=pltpu.SMEM),
            fixed((rows, wide)),
            fixed((rows, width)),
            fixed((rows, width)),
            fixed((rows, width)),
            fixed(mg0.shape),
            fixed(h0.shape),
            ANYWHERE,
        ]
        + [ANYWHERE] * len(after),
        out_specs=tuple(fixed(cut) for cut in cuts) + (fixed(h0.shape),),
        scratch_shapes=[
            pltpu.VMEM((wide, rows), LOW),
            pltpu.VMEM((width, rows), LOW),
            pltpu.VMEM(wi.shape, LOW),
            pltpu.SemaphoreType.DMA,
        ],
        compiler_params=params(60),
        cost_estimate=MUCH,
        name="attention_grads",
    )(me, mg, ag, x, ctx, mg0, h0, wi, *after)


def shard_groups(count, wide):
    span = wide // count
    first = [span * shard // HD for shard in range(count)]
    most = max((span * shard + span - 1) // HD - first[shard] + 1 for shard in range(count))
    return [min(one, wide // HD - most) for one in first], most


def input_grad_kernel(mg_ref, w_ref, hgrad_ref, sg_ref, p0_ref, fk_ref, fv_ref, fq_ref, *refs):
    out_ref = refs[-1]
    seq = pl.program_id(0)
    length, width = hgrad_ref.shape[1:]
    rows = lax.broadcasted_iota(jnp.int32, (length, 1), 0)
    back = dot_nt(mg_ref[0], w_ref[...]) + dot_tn(sg_ref[0], fk_ref[0]) + dot_tn(p0_ref[0], fv_ref[0])
    out_ref[0] = back + hgrad_ref[0] + jnp.where(rows == 0, pick(fq_ref, seq), 0.0)


def input_grad(mg, weight, hgrad, sg, p0, fk, fv, fq, after):
    count, length, wide = mg.shape
    width = wide // 3

    def per(*shape):
        return pl.BlockSpec((1,) + shape, lambda i: (i,) + (0,) * len(shape))

    return pl.pallas_call(
        input_grad_kernel,
        grid=(count,),
        out_shape=jax.ShapeDtypeStruct((count, length, width), F32),
        in_specs=[
            per(length, wide),
            fixed((width, wide)),
            per(length, width),
            per(ROW_TILE, length),
            per(ROW_TILE, length),
            per(ROW_TILE, width),
            per(ROW_TILE, width),
            fixed((count, width)),
        ]
        + [ANYWHERE] * len(after),
        out_specs=per(length, width),
        compiler_params=params(60),
        cost_estimate=MUCH,
        name="input_grad",
    )(mg, weight, hgrad, sg, p0, fk, fv, fq, *after)


def last_kernel(
    g0_ref, z0_ref, r2_ref, g2_ref, slope_ref, wc_ref, we_ref, n0_ref, r1_ref, g1_ref, wo_ref, wi_hbm,
    p0_ref, mixed_ref, m0_ref, x_ref, s2_ref, s1_ref, s0_ref, eb_ref, early_ref, emb_ref, summary_ref, *refs, groups
):
    (
        sg_ref, fk_ref, fv_ref, fq_ref, send_ref,
        fg_ref, ag_ref, hg_ref, eball_ref, coef_ref, sums_ref, pack_ref,
        zg_ref, acc_ref, hz_ref, dctx_ref, rows_ref, wi_ref, sem,
    ) = refs[-19:]
    step = pl.program_id(0)
    count, width = g0_ref.shape
    chunks = pl.num_programs(0) - count
    copy = pltpu.make_async_copy(wi_hbm, wi_ref, sem)

    @pl.when(step == 0)
    def _():
        copy.start()
        grad = g0_ref[...]
        z_grad = norm_back(grad, g2_ref[...].astype(F32), z0_ref[...], r2_ref[:, 0:1])
        zg_ref[...] = z_grad
        low = z_grad.astype(LOW)
        fg_ref[...] = low
        sums_ref[0:2, :] = s0_ref[0:2, :]
        sums_ref[6:7, :] = s2_ref[0:1, :] + jnp.sum(grad * z0_ref[...], axis=0, keepdims=True)
        sums_ref[7:8, :] = s2_ref[1:2, :] + jnp.sum(grad, axis=0, keepdims=True)
        sums_ref[5:6, :] = s2_ref[2:3, :] + jnp.sum(low.astype(F32), axis=0, keepdims=True)
        acc_ref[...] = jnp.zeros(acc_ref.shape, F32)

    @pl.when(step < chunks)
    def _():
        grad = (dot_nt(fg_ref[...], wc_ref[...]) * slope_ref[...].astype(F32)).astype(LOW)
        here = pl.ds(pl.multiple_of(step * wc_ref.shape[0], LANES), wc_ref.shape[0])
        hg_ref[:, here] = grad.astype(F32)
        eball_ref[0:1, here] = eb_ref[...] + jnp.sum(grad.astype(F32), axis=0, keepdims=True)
        acc_ref[...] += dot_nt(grad, we_ref[...])

    @pl.when(step == chunks - 1)
    def _():
        grad = zg_ref[...] + acc_ref[...]
        normal = n0_ref[...]
        h_grad = norm_back(grad, g1_ref[...].astype(F32), normal, r1_ref[:, 0:1])
        hz_ref[0:count, :] = h_grad
        low = h_grad.astype(LOW)
        ag_ref[...] = low.astype(F32)
        sums_ref[3:4, :] = s1_ref[0:1, :] + jnp.sum(grad * normal, axis=0, keepdims=True)
        sums_ref[4:5, :] = s1_ref[1:2, :] + jnp.sum(grad, axis=0, keepdims=True)
        sums_ref[2:3, :] = s1_ref[2:3, :] + jnp.sum(low.astype(F32), axis=0, keepdims=True)
        dctx_ref[0:count, :] = dot_nt(low, wo_ref[...])
        copy.wait()

    @pl.when(step >= chunks)
    def _():
        seq = step - chunks
        heads = head_rows(width)
        own = dctx_ref[pl.ds(seq, 1), :]
        grad = jnp.where(heads, own, 0.0).astype(LOW)
        query0 = pick(m0_ref, seq, slice(0, width))
        query = jnp.where(heads, query0, 0.0).astype(LOW)
        key = with_first(mixed_ref[0, :, width : 2 * width], pick(m0_ref, seq, slice(width, 2 * width)))
        value = with_first(mixed_ref[0, :, 2 * width :], pick(m0_ref, seq, slice(2 * width, 3 * width)))
        chance_low = p0_ref[0]
        chance = chance_low.astype(F32)
        p_grad = dot_nt(grad, value)
        s_grad = (chance * (p_grad - jnp.sum(p_grad * chance, axis=-1, keepdims=True))).astype(LOW)
        dq = dot(s_grad, key)
        dq = jnp.sum(jnp.where(heads, dq, 0.0), axis=0, keepdims=True) * SCALE
        put(coef_ref, seq, dq, slice(0, width))
        put(coef_ref, seq, query0 * SCALE, slice(width, 2 * width))
        put(coef_ref, seq, own, slice(2 * width, 3 * width))
        inputs = x_ref[0]
        rows_ref[0, 0:1, :] = inputs[0:1, :].astype(F32)
        rows_ref[1] = dot(s_grad, inputs)
        rows_ref[2] = dot(chance_low, inputs)
        firsts, most = groups
        per = width // HD
        for shard, first in enumerate(firsts):
            for turn_of in range(most):
                which, head = divmod(first + turn_of, per)
                head = head if which else 0
                at = pl.ds(count + seq * most + turn_of, 1)
                pack_ref[shard, at, 0:width] = rows_ref[which, head : head + 1, :]
        sg_ref[0] = s_grad
        fk_ref[0] = (dot_nt(query, wi_ref[:, width : 2 * width]) * SCALE).astype(LOW)
        fv_ref[0] = dot_nt(grad, wi_ref[:, 2 * width :]).astype(LOW)
        from_query = dot_nt(jnp.where(heads, dq, 0.0).astype(LOW), wi_ref[:, 0:width])
        put(fq_ref, seq, jnp.sum(from_query, axis=0, keepdims=True) + hz_ref[pl.ds(seq, 1), :])
        sums_ref[0:1, :] += dq
        held = jnp.sum(chance, axis=-1, keepdims=True)
        sums_ref[1:2, :] += jnp.sum(held * grad.astype(F32), axis=0, keepdims=True)

    @pl.when(step == pl.num_programs(0) - 1)
    def _():
        firsts, most = groups
        shards = len(firsts)
        starts, pitch, begin = parcel(count, shards, width, eball_ref.shape[1], most, emb_ref.shape[1])
        for shard in range(shards):
            for name, source in (("feed", fg_ref), ("attended", ag_ref), ("hidden", hg_ref), ("coef", coef_ref)):
                span = source.shape[1] // shards
                piece = source[:, shard * span : (shard + 1) * span].astype(F32)
                pack_ref[shard, 0:count, starts[name] : starts[name] + span] = piece
            pack_ref[shard, 0:count, starts["emb"] : starts["emb"] + emb_ref.shape[1]] = emb_ref[...].astype(F32)
            span = width // shards
            at = starts["vectors"]
            pack_ref[shard, count : count + 8, at : at + span] = sums_ref[:, shard * span : (shard + 1) * span]
            span = eball_ref.shape[1] // shards
            for line, column in enumerate(range(0, span, LANES)):
                size = min(LANES, span - column)
                piece = eball_ref[0:1, shard * span + column : shard * span + column + size]
                pack_ref[shard, count + 8 + line : count + 9 + line, at : at + size] = piece
            send_ref[shard, 0:begin, 0 : pitch - LANES] = pack_ref[shard, 0:begin, 0 : pitch - LANES].astype(LOW)
            send_ref[shard, 2 * count : begin, pitch - LANES :] = jnp.zeros((begin - 2 * count, LANES), LOW)
        for seq in range(count):
            lines = [(begin + 2 * seq, 0, pitch), (begin + 2 * seq + 1, 0, pitch)]
            lines += [(2 * seq, pitch - LANES, pitch), (2 * seq + 1, pitch - LANES, pitch)]
            at = 0
            for line, column, end in lines:
                while column < end and at < 3 * width:
                    source, start = (early_ref, at) if at < 2 * width else (summary_ref, at - 2 * width)
                    size = min(end - column, (2 * width if at < 2 * width else 3 * width) - at)
                    value = source[seq : seq + 1, start : start + size].astype(F32)
                    pack_ref[0, line : line + 1, column : column + size] = value
                    column += size
                    at += size
        early = pack_ref[0, begin : begin + 2 * count, :].astype(LOW)
        spare = pack_ref[0, 0 : 2 * count, pitch - LANES :].astype(LOW)
        for shard in range(shards):
            send_ref[shard, begin : begin + 2 * count, :] = early
            send_ref[shard, 0 : 2 * count, pitch - LANES :] = spare


def parcel(count, shards, width, hidden, most, emb):
    starts, at = {}, 0
    for name, span in (
        ("feed", width // shards), ("attended", width // shards), ("hidden", hidden // shards),
        ("coef", 3 * width // shards), ("emb", emb),
    ):
        starts[name] = at
        at += -(-span // LANES) * LANES
    starts["vectors"] = width
    pitch = max(at, width + LANES) + LANES
    return starts, pitch, -(-(count + max(most * count, 8 + -(-hidden // shards // LANES))) // 8) * 8


def last_rows(
    g0, z0, r2, g2, slope0, wc, we, n0, r1, g1, wo, wi, p0, mixed, m0, x, s2, s1, s0, eb, early, emb, summary, after, shards
):
    count, length, wide = mixed.shape
    width = wide // 3
    hidden = slope0.shape[1]
    chunk = 768
    chunks = hidden // chunk
    groups = shard_groups(shards, wide)
    _, pitch, begin = parcel(count, shards, width, hidden, groups[1], emb.shape[1])
    send = (shards, begin + 2 * count, pitch)

    def part(i):
        return jnp.minimum(i, chunks - 1)

    def seq(i):
        return jnp.maximum(i - chunks, 0)

    def per(*shape):
        return pl.BlockSpec((1,) + shape, lambda i: (seq(i),) + (0,) * len(shape))

    row = fixed((1, width))
    rows = fixed((count, width))
    return pl.pallas_call(
        functools.partial(last_kernel, groups=groups),
        grid=(chunks + count,),
        out_shape=(
            jax.ShapeDtypeStruct((count, ROW_TILE, length), LOW),
            jax.ShapeDtypeStruct((count, ROW_TILE, width), LOW),
            jax.ShapeDtypeStruct((count, ROW_TILE, width), LOW),
            jax.ShapeDtypeStruct((count, width), F32),
            jax.ShapeDtypeStruct(send, LOW),
        ),
        in_specs=[
            rows, rows, fixed((count, LANES)), row,
            pl.BlockSpec((count, chunk), lambda i: (0, part(i))),
            pl.BlockSpec((chunk, width), lambda i: (part(i), 0)),
            pl.BlockSpec((width, chunk), lambda i: (0, part(i))),
            rows, fixed((count, LANES)), row,
            fixed((width, width)),
            ANYWHERE,
            per(ROW_TILE, length),
            per(length, wide),
            fixed((count, wide)),
            per(length, width),
            fixed((8, width)),
            fixed((8, width)),
            fixed((8, width)),
            pl.BlockSpec((1, chunk), lambda i: (0, part(i))),
            fixed(early.shape),
            fixed(emb.shape),
            fixed(summary.shape),
        ]
        + [ANYWHERE] * len(after),
        out_specs=(
            per(ROW_TILE, length),
            per(ROW_TILE, width),
            per(ROW_TILE, width),
            rows,
            fixed(send),
        ),
        scratch_shapes=[
            pltpu.VMEM((count, width), LOW),
            pltpu.VMEM((count, width), F32),
            pltpu.VMEM((count, hidden), F32),
            pltpu.VMEM((8, hidden), F32),
            pltpu.VMEM((count, wide), F32),
            pltpu.VMEM((8, width), F32),
            pltpu.VMEM(send, F32),
            pltpu.VMEM((count, width), F32),
            pltpu.VMEM((count, width), F32),
            pltpu.VMEM((8, width), F32),
            pltpu.VMEM((8, width), F32),
            pltpu.VMEM((3, ROW_TILE, width), F32),
            pltpu.VMEM((width, wide), LOW),
            pltpu.SemaphoreType.DMA,
        ],
        compiler_params=params(60),
        cost_estimate=LITTLE,
        name="last_rows",
    )(g0, z0, r2, g2, slope0, wc, we, n0, r1, g1, wo, wi, p0, mixed, m0, x, s2, s1, s0, eb, early, emb, summary, *after)


def flip(value, bit, count):
    return lax.ppermute(value, "rows", [(i, i ^ bit) for i in range(count)])


def first_stage(parts, count):
    return [flip(parts[half], BITS[half][0], count) for half in range(2)]


def second_stage(sends, count):
    return [flip(sends[half], BITS[half][1], count) for half in range(2)]


def sum_low(left_ref, right_ref):
    return (left_ref[...].astype(F32) + right_ref[...].astype(F32)).astype(LOW)


def first_sum_kernel(a0, a1, b0, b1, ga0, ga1, gb0, gb1, *refs):
    sa, sb, ka, kb = refs[-4:]
    sa[...] = sum_low(a0, ga0)
    ka[...] = sum_low(a1, ga1)
    sb[...] = sum_low(b0, gb0)
    kb[...] = sum_low(b1, gb1)


def first_sum(parts, got, after):
    keep0, keep1 = parts[2:]
    rows, width = keep0.shape
    tiles = 4
    block = (rows // 2 // tiles, width)
    top = pl.BlockSpec(block, lambda i: (i, 0))
    bottom = pl.BlockSpec(block, lambda i: (i + tiles, 0))
    result = pl.pallas_call(
        first_sum_kernel,
        grid=(tiles,),
        out_shape=(jax.ShapeDtypeStruct((rows // 2, width), LOW),) * 4,
        in_specs=[top, bottom] * 4 + [ANYWHERE] * len(after),
        out_specs=(top,) * 4,
        compiler_params=params(60),
        cost_estimate=LITTLE,
        name="first_sum",
    )(keep0, keep0, keep1, keep1, got[0], got[0], got[1], got[1], *after)
    return result[:2], result[2:]


def second_sum_kernel(a, b, ga, gb, *refs, apart, stacked):
    step = pl.program_id(0)
    rows, half = a.shape
    left, right = sum_low(a, ga), sum_low(b, gb)
    for index, out in enumerate(refs[-2 if apart else -4 :]):

        @pl.when(step // 2 == index if apart else step == index)
        def _():
            if stacked:
                out[:rows, :] = left
                out[rows:, :] = right
            else:
                out[:, :half] = left
                out[:, half:] = right


def second_sum(keeps, got, after, apart, stacked):
    rows, width = keeps[0].shape
    tile = rows // 4
    block = pl.BlockSpec((tile, width), lambda i: (i, 0))
    wide, out_tile = (width, 2 * tile) if stacked else (2 * width, tile)
    if apart:
        shapes = (jax.ShapeDtypeStruct((2 * out_tile, wide), LOW),) * 2
        places_out = (
            pl.BlockSpec((out_tile, wide), lambda i: (jnp.minimum(i, 1), 0)),
            pl.BlockSpec((out_tile, wide), lambda i: (jnp.maximum(i - 2, 0), 0)),
        )
    else:
        shapes = (jax.ShapeDtypeStruct((out_tile, wide), LOW),) * 4
        places_out = (fixed((out_tile, wide)),) * 4
    return pl.pallas_call(
        functools.partial(second_sum_kernel, apart=apart, stacked=stacked),
        grid=(4,),
        out_shape=shapes,
        in_specs=[block] * 4 + [ANYWHERE] * len(after),
        out_specs=places_out,
        compiler_params=params(60),
        cost_estimate=LITTLE,
        name="second_sum",
    )(keeps[0], keeps[1], got[0], got[1], *after)


def third_sum_kernel(a, ga, *refs):
    for index, out in enumerate(refs[-2:]):

        @pl.when(pl.program_id(0) == index)
        def _():
            out[...] = sum_low(a, ga)


def third_sum(keep, got, after, weighs):
    rows, width = keep.shape
    block = pl.BlockSpec((rows // 2, width), lambda i: (i, 0))
    shape = (rows // 2, width)
    return pl.pallas_call(
        third_sum_kernel,
        grid=(2,),
        out_shape=(jax.ShapeDtypeStruct(shape, LOW),) * 2,
        in_specs=[block] * 2 + [ANYWHERE] * len(after),
        out_specs=(fixed(shape),) * 2,
        compiler_params=params(60),
        cost_estimate=weighs,
        name="third_sum",
    )(keep, got, *after)


def wide_sum(left, right):
    return left.astype(F32) + right.astype(F32)


def line_stage(totals, count):
    got = [totals[0]]
    for step in range(1, count // 4):
        got.append(lax.ppermute(totals[step], "rows", [(i, (i + 4 * step) % count) for i in range(count)]))
    return got


def rest_kernel(*refs):
    *got, fix_ref, in_ref, out_ref = refs
    span, other = in_ref.shape[0], out_ref.shape[0]
    first, last = cut_up(span), other - cut_up(other)
    total = got[0][...].astype(F32)
    for one in got[1:]:
        total = total + one[...].astype(F32)
    for into, start, size, at in (
        (in_ref, 0, first, 0),
        (out_ref, 0, last, first),
        (in_ref, first, span - first, first + last),
        (out_ref, last, other - last, span + last),
    ):
        add = start + (span if into is out_ref else 0)
        into[start : start + size, :] = total[at : at + size] + fix_ref[add : add + size, :]


def rest_sum(got, fix, span):
    rows, width = fix.shape
    return pl.pallas_call(
        rest_kernel,
        out_shape=(jax.ShapeDtypeStruct((span, width), F32), jax.ShapeDtypeStruct((rows - span, width), F32)),
        compiler_params=params(60),
        name="rest_sum",
    )(*got, fix)


def whole_grad(full):
    return lax.psum_scatter(full.astype(F32), "rows", scatter_dimension=0, tiled=True)


def body(
    token_states, lengths, key_mask, cotangent, attention_in, attention_bias, attention_out, output_bias,
    gain_one, shift_one, expand_weight, expand_bias, contract_weight, contract_bias, gain_two, shift_two,
    projection, passage_table, candidates,
):
    section = lax.axis_index("section")
    is_first = section == 0
    count = lax.axis_size("rows")
    me = lax.axis_index("rows")
    tokens = token_states[0]
    seqs, length, width = tokens.shape
    rows = seqs * length

    bi = attention_bias[0]
    wi, wo, we, wc = attention_in[0], attention_out[0], expand_weight[0], contract_weight[0]
    bo, g1, c1, be, bc, g2, c2 = output_bias, gain_one, shift_one, expand_bias, contract_bias, gain_two, shift_two
    weights = (wi, bi, wo, bo, g1, c1, we, be, wc, bc, g2, c2)
    positions = jnp.arange(length)
    valid = (positions[None, :] < lengths[0][:, None]) & (key_mask[0] == 1) | (positions[None, :] == 0)
    valid = valid.astype(F32)[:, None, :]
    staged = count == 16 and width // count % ROW_TILE == 0
    cuts = count if staged else 2
    place = me.reshape(1).astype(jnp.int32)

    retrieved = jnp.take(passage_table, candidates, axis=0).astype(F32)
    mixed, x0 = project(token_states, wi, bi)
    message = first_rows(mixed, valid, x0, weights, projection)
    received = lax.ppermute(message, "section", [(0, 1)])
    summary_in, embedding_in = received[:, :width], received[:, width:]
    x0 = x0 + summary_in.astype(F32)
    in_bias = jnp.concatenate([bi[0], jnp.zeros_like(bi[0]), bi[1]])
    mixed0 = (dot(x0.astype(LOW), wi) + in_bias.astype(F32)).astype(LOW).astype(F32)
    chance, context, first, first_low, normal, root, x_low, chance0, early, n0, r1 = attention_forward(
        lengths[0], mixed, mixed0, token_states, x0, valid, wo, bo, g1, c1
    )
    match = jnp.sum(embedding_in.astype(F32)[:, None, :] * retrieved, axis=-1)
    chances = jax.nn.softmax(match, axis=-1)
    weight = TOPK * chances[:, 0]
    scal = jnp.concatenate([jnp.where(is_first, 1.0, weight), jnp.where(is_first, 0.0, 1.0)[None]]).astype(F32)
    first_flat = first_low.reshape(rows, width)
    slope, out, z_grad, feed_grad, sums_two, weight_grads, z0, r2, cot0, slope0, *contract = feed_forward(
        place, scal, first_flat, first, we, be, wc, bc, g2, c2, cotangent[0], cuts
    )

    contract_got = first_stage(contract, count) if staged else None
    expand_sum, h_grad, attended, sums_one, h0, *expand = feed_backward(
        place, feed_grad.reshape(rows, width), slope, wc, we, z_grad, normal, root, g1, first_flat, cuts
    )
    contract_send = ()
    if staged:
        contract_send, contract_keep = first_sum(contract, contract_got, (h0,))
        contract_got = second_stage(contract_send, count)
        expand_got = first_stage(expand, count)
    mixed_grad, mg0, sums_in = attention_backward(
        lengths[0], attended, wo, chance, mixed, mixed0, context, tuple(contract_send)
    )
    after = ()
    if staged:
        expand_send, expand_keep = first_sum(expand, expand_got, (mg0,))
        expand_got = second_stage(expand_send, count)
        after = (expand_send[0],)
    *rest, reader_term = attention_grads(
        place, mixed_grad.reshape(rows, 3 * width), attended.reshape(rows, width), x_low.reshape(rows, width),
        context.reshape(rows, width), mg0, h0, wi, after, cuts,
    )
    rest_got = first_stage(rest, count) if staged else None

    after = (rest[0],)
    if staged:
        contract_send, contract_keep = second_sum(contract_keep, contract_got, (rest[0],), True, False)
        contract_got = flip(contract_send, 4, count)
        expand_send, expand_keep = second_sum(expand_keep, expand_got, (contract_send,), True, True)
        expand_got = flip(expand_send, 4, count)
        after = (expand_send, contract_send)
    grad_weight = jnp.sum(weight_grads, axis=1)
    one = jnp.zeros((TOPK,), F32).at[0].set(1.0)
    grad_match = (grad_weight[:, None] * weight[:, None] * (one[None, :] - chances)).astype(LOW)
    embedding_grad = jnp.sum(grad_match.astype(F32)[:, :, None] * retrieved, axis=1).astype(LOW)
    if staged:
        reader_term, _ = lax.optimization_barrier((reader_term, expand_send))
    reader_term = reader_term.astype(LOW)
    back = lax.ppermute(jnp.concatenate([reader_term, embedding_grad], axis=1), "section", [(1, 0)])
    embedding_used = jnp.where(is_first, back[:, width:], embedding_grad)
    summary_grad = dot_nt(back[:, width:], projection) + back[:, :width].astype(F32)
    grad_zero = jnp.where(is_first, cot0 + summary_grad, 0.0)
    used_summary = jnp.where(is_first, message[:, :width], summary_in)
    s_zero, from_key, from_value, from_query, parcels = last_rows(
        grad_zero, z0, r2, g2, slope0, wc, we, n0, r1, g1, wo, wi, chance0, mixed, mixed0, x_low,
        sums_two, sums_one, sums_in, expand_sum, early, embedding_used, used_summary, after, count,
    )
    after = ()
    if staged:
        rest_send, rest_keep = first_sum(rest, rest_got, (parcels,))
        rest_got = second_stage(rest_send, count)
        after = (rest_send[0],)

    got = lax.all_to_all(parcels, "rows", 0, 0, tiled=True)
    if staged:
        contract_send, contract_keep = third_sum(contract_keep, contract_got, after, MUCH)
        contract_got = flip(contract_send, 8, count)
        expand_send, expand_keep = third_sum(expand_keep, expand_got, (contract_send,), LITTLE)
        expand_got = flip(expand_send, 8, count)
        after = (expand_send,)
    x_grad = input_grad(mixed_grad, wi, h_grad, s_zero, chance0, from_key, from_value, from_query, after)
    if staged:
        rest = second_sum(rest_keep, rest_got, (x_grad,), False, True)
        rest_got = line_stage(rest, count)
        got, me, _ = lax.optimization_barrier((got, me, rest))
    else:
        top, bottom = jnp.concatenate(contract[:2], axis=1), jnp.concatenate(contract[2:], axis=1)
        contract = whole_grad(jnp.concatenate([top, bottom], axis=0))
        expand = whole_grad(jnp.concatenate(expand, axis=0))
        inner = 3 * width // 4
        rest = [jnp.concatenate([part[cut] for part in rest]) for cut in (slice(0, inner), slice(inner, None))]
        rest = [whole_grad(part) for part in rest]
    hidden = we.shape[1]
    span = 3 * width // count
    firsts, most = shard_groups(count, 3 * width)
    starts, pitch, begin = parcel(seqs, count, width, hidden, most, embedding_used.shape[1])

    def sent(name, size):
        return got[:, :seqs, starts[name] : starts[name] + size].reshape(count * seqs, size)

    factors = jnp.concatenate(
        [
            got[:, begin : begin + 2 * seqs].reshape(count * seqs, 2 * pitch),
            got[:, : 2 * seqs, pitch - LANES :].reshape(count * seqs, 2 * LANES),
        ],
        axis=1,
    )
    first_all, context_all, summary_all = (factors[:, i * width : (i + 1) * width] for i in range(3))
    active_all = gelu_both(dot(first_all, we) + be.astype(F32))[0].astype(LOW)
    contract_fix = dot_tn(sent("feed", width // count), active_all)
    projection_grad = dot_tn(summary_all, sent("emb", embedding_used.shape[1]))
    head = (span * me + jnp.arange(span)) // HD - jnp.asarray(firsts, jnp.int32)[me]
    chosen = (head[None, :] == jnp.arange(most)[:, None]).astype(LOW)
    coefs = (sent("coef", span)[:, None, :] * chosen[None]).reshape(count * seqs * most, span)
    groups = got[:, seqs : seqs + seqs * most, :width].reshape(count * seqs * most, width)
    fix = jnp.concatenate([dot_tn(coefs, groups), dot_tn(sent("attended", width // count), context_all)], axis=0)
    expand_fix = dot_tn(sent("hidden", hidden // count), first_all)
    at = starts["vectors"]
    packed = jnp.sum(got[:, seqs : seqs + 8, at : at + width // count].astype(F32), axis=0)
    lines = -(-hidden // count // LANES)
    e_bias = got[:, seqs + 8 : seqs + 8 + lines, at : at + LANES].astype(F32)
    e_bias = jnp.sum(e_bias, axis=0).reshape(-1)[: hidden // count]
    if staged:
        held = (contract_got, expand_got, rest_got, fix, contract_fix, expand_fix, projection_grad, packed, e_bias)
        contract_got, expand_got, rest_got, fix, contract_fix, expand_fix, projection_grad, packed, e_bias = (
            lax.optimization_barrier(held)
        )
        contract = contract_fix + wide_sum(contract_keep, contract_got)
        expand = wide_sum(expand_keep, expand_got)
        attention_in_grad, attention_out_grad = rest_sum(rest_got, fix, span)
    else:
        contract = contract + contract_fix
        attention_in_grad, attention_out_grad = rest[0] + fix[:span], rest[1] + fix[span:]
    expand = expand + expand_fix
    q_bias, v_bias, o_bias, gain1, shift1, c_bias, gain2, shift2 = (packed[i] for i in range(8))
    return (
        out[None],
        x_grad[None],
        attention_in_grad.T[None],
        jnp.stack([q_bias, v_bias])[None],
        attention_out_grad.T[None],
        o_bias[None],
        gain1[None],
        shift1[None],
        expand.T[None],
        e_bias[None],
        contract.T[None],
        c_bias[None],
        gain2[None],
        shift2[None],
        projection_grad,
    )


def solution(mesh):
    in_specs = (
        P("section", "rows", None, None),
        P("section", "rows"),
        P("section", "rows", None),
        P("section", "rows", None, None),
        P("section", None, None),
        P("section", None, None),
        P("section", None, None),
        P("section", None),
        P("section", None),
        P("section", None),
        P("section", None, None),
        P("section", None),
        P("section", None, None),
        P("section", None),
        P("section", None),
        P("section", None),
        P(),
        P(),
        P("rows", None),
    )
    out_specs = (
        P("section", "rows", None, None),
        P("section", "rows", None, None),
        P("section", None, "rows"),
        P("section", None, "rows"),
        P("section", None, "rows"),
        P("section", "rows"),
        P("section", "rows"),
        P("section", "rows"),
        P("section", None, "rows"),
        P("section", "rows"),
        P("section", None, "rows"),
        P("section", "rows"),
        P("section", "rows"),
        P("section", "rows"),
        P(),
    )
    return jax.shard_map(body, mesh=mesh, in_specs=in_specs, out_specs=out_specs, check_vma=False)
```

```python
import functools
import math

import jax
import jax.numpy as jnp
from jax import lax
from jax.experimental import pallas as pl
from jax.experimental.pallas import tpu as pltpu
from jax.sharding import PartitionSpec as P

HD = 64
TOPK = 8
NEGATIVE = -1000000000.0
SCALE = 1.0 / math.sqrt(HD)
LANES = 128
ROW_TILE = 16
F32 = jnp.float32
LOW = jnp.bfloat16
NT = (((1,), (1,)), ((), ()))
TN = (((0,), (0,)), ((), ()))
MIB = 1 << 20
BITS = ((1, 2), (2, 1))


def dot(left, right):
    return jnp.dot(left, right, preferred_element_type=F32)


def dot_nt(left, right):
    return lax.dot_general(left, right, NT, preferred_element_type=F32)


def dot_tn(left, right):
    return lax.dot_general(left, right, TN, preferred_element_type=F32)


def params(limit):
    return pltpu.CompilerParams(vmem_limit_bytes=limit * MIB)


MUCH = pl.CostEstimate(flops=100 * 1000**3, bytes_accessed=50 * MIB, transcendentals=0)
LITTLE = pl.CostEstimate(flops=1, bytes_accessed=1, transcendentals=0)


ANYWHERE = pl.BlockSpec(memory_space=pl.ANY)


def fixed(shape):
    return pl.BlockSpec(shape, lambda *ids: (0,) * len(shape), pipeline_mode=pl.Buffered(1))


def norm_stats(hidden):
    mean = jnp.mean(hidden, axis=-1, keepdims=True)
    centered = hidden - mean
    root = lax.rsqrt(jnp.mean(centered * centered, axis=-1, keepdims=True) + 1e-12)
    return centered * root, root


def norm_back(grad, gain, normal, root):
    scaled = gain * grad
    mean = jnp.mean(scaled, axis=-1, keepdims=True)
    along = jnp.mean(scaled * normal, axis=-1, keepdims=True)
    return root * (scaled - mean - normal * along)


def gelu_both(u):
    phi = 0.5 + 0.5 * lax.erf(u * (1.0 / math.sqrt(2.0)))
    slope = phi + u * (jnp.exp(-0.5 * u * u) * (1.0 / math.sqrt(2.0 * math.pi)))
    return u * phi, slope


def head_rows(width):
    shape = (ROW_TILE, width)
    return lax.broadcasted_iota(jnp.int32, shape, 1) // HD == lax.broadcasted_iota(jnp.int32, shape, 0)


def pick(ref, row, columns=slice(None)):
    block = ref[:, columns]
    rows = lax.broadcasted_iota(jnp.int32, (block.shape[0], 1), 0)
    return jnp.sum(jnp.where(rows == row, block, 0.0), axis=0, keepdims=True)


def put(ref, row, value, columns=slice(None)):
    block = ref[:, columns]
    rows = lax.broadcasted_iota(jnp.int32, (block.shape[0], 1), 0)
    ref[:, columns] = jnp.where(rows == row, value, block)


def project_kernel(x_ref, w_ref, b_ref, o_ref, x0_ref):
    step = pl.program_id(0)
    bias = b_ref[...].astype(F32)
    bias = jnp.where(step == 0, bias[0:1, :], jnp.where(step == 2, bias[1:2, :], 0.0))
    for part in range(x_ref.shape[1]):
        o_ref[part] = (dot(x_ref[0, part], w_ref[...]) + bias).astype(LOW)
        x0_ref[part : part + 1, :] = x_ref[0, part, 0:1, :].astype(F32)


def project(x, weight, bias):
    _, count, length, width = x.shape
    return pl.pallas_call(
        project_kernel,
        grid=(3,),
        out_shape=(
            jax.ShapeDtypeStruct((count, length, 3 * width), LOW),
            jax.ShapeDtypeStruct((count, width), F32),
        ),
        in_specs=[
            fixed((1, count, length, width)),
            pl.BlockSpec((width, width), lambda i: (0, i)),
            fixed((2, width)),
        ],
        out_specs=(pl.BlockSpec((count, length, width), lambda i: (0, 0, i)), fixed((count, width))),
        compiler_params=params(32),
        cost_estimate=pl.CostEstimate(flops=6 * count * length * width * width, bytes_accessed=14 * MIB, transcendentals=0),
        name="project_qkv",
    )(x, weight, bias)


def first_rows_kernel(
    mixed_ref, valid_ref, x0_ref, wo_ref, bo_ref, g1_ref, c1_ref, we_ref, be_ref, wc_ref, bc_ref,
    g2_ref, c2_ref, pr_ref, out_ref, ctx_ref, first_ref, acc_ref,
):
    step = pl.program_id(0)
    count = x0_ref.shape[0]
    width = wo_ref.shape[0]
    chunks = pl.num_programs(0) - count

    @pl.when(step < count)
    def _():
        heads = head_rows(width)
        query = mixed_ref[0, 0:1, 0:width].astype(F32) * SCALE
        spread = jnp.where(heads, query, 0.0).astype(LOW)
        scores = dot_nt(spread, mixed_ref[0, :, width : 2 * width])
        scores = jnp.where(valid_ref[0] > 0, scores, NEGATIVE)
        exponent = jnp.exp(scores - jnp.max(scores, axis=-1, keepdims=True))
        chance = (exponent / jnp.sum(exponent, axis=-1, keepdims=True)).astype(LOW)
        context = dot(chance, mixed_ref[0, :, 2 * width :])
        context = jnp.sum(jnp.where(heads, context, 0.0), axis=0, keepdims=True)
        ctx_ref[pl.ds(step, 1), :] = context

    @pl.when(step == count - 1)
    def _():
        hidden = x0_ref[...] + dot(ctx_ref[0:count, :].astype(LOW), wo_ref[...]) + bo_ref[...].astype(F32)
        normal, root = norm_stats(hidden)
        first_ref[...] = normal * g1_ref[...].astype(F32) + c1_ref[...].astype(F32)

    @pl.when(step >= count)
    def _():
        u = dot(first_ref[...].astype(LOW), we_ref[...]) + be_ref[...].astype(F32)
        active, slope = gelu_both(u)
        part = dot(active.astype(LOW), wc_ref[...])

        @pl.when(step == count)
        def _():
            acc_ref[...] = part

        @pl.when(step > count)
        def _():
            acc_ref[...] += part

    @pl.when(step == pl.num_programs(0) - 1)
    def _():
        normal, root = norm_stats(first_ref[...] + acc_ref[...] + bc_ref[...].astype(F32))
        summary = (normal * g2_ref[...].astype(F32) + c2_ref[...].astype(F32)).astype(LOW)
        out_ref[:, 0:width] = summary
        out_ref[:, width:] = dot(summary, pr_ref[...]).astype(LOW)


def first_rows(mixed, valid, x0, weights, projection):
    (_, _, wo, bo, g1, c1, we, be, wc, bc, g2, c2) = weights
    count, length, wide = mixed.shape
    width, hidden = we.shape
    chunk = 768
    chunks = hidden // chunk
    proj = projection.shape[1]

    def seq(i):
        return jnp.minimum(i, count - 1)

    def part(i):
        return jnp.maximum(i - count, 0)

    row = fixed((1, width))
    return pl.pallas_call(
        first_rows_kernel,
        grid=(count + chunks,),
        out_shape=jax.ShapeDtypeStruct((count, width + proj), LOW),
        in_specs=[
            pl.BlockSpec((1, length, wide), lambda i: (seq(i), 0, 0)),
            pl.BlockSpec((1, 1, length), lambda i: (seq(i), 0, 0)),
            fixed((count, width)),
            fixed((width, width)),
            row, row, row,
            pl.BlockSpec((width, chunk), lambda i: (0, part(i))),
            pl.BlockSpec((1, chunk), lambda i: (0, part(i))),
            pl.BlockSpec((chunk, width), lambda i: (part(i), 0)),
            row, row, row,
            fixed((width, proj)),
        ],
        out_specs=fixed((count, width + proj)),
        scratch_shapes=[
            pltpu.VMEM((8, width), F32),
            pltpu.VMEM((count, width), F32),
            pltpu.VMEM((count, width), F32),
        ],
        compiler_params=params(32),
        cost_estimate=pl.CostEstimate(flops=40 * MIB, bytes_accessed=17 * MIB, transcendentals=0),
        name="first_rows_forward",
    )(mixed, valid, x0, wo, bo, g1, c1, we, be, wc, bc, g2, c2, projection)


def with_first(block, row):
    rows = lax.broadcasted_iota(jnp.int32, (ROW_TILE, 1), 0)
    top = jnp.where(rows == 0, row, block[0:ROW_TILE].astype(F32)).astype(block.dtype)
    return jnp.concatenate([top, block[ROW_TILE:]], axis=0)


def pair_of(mixed_ref, m0_ref, pair, width, seq):
    found = []
    for which in range(3):
        columns = pl.ds(which * width + pair * LANES, LANES)
        found.append(with_first(mixed_ref[0, :, columns], pick(m0_ref, seq, columns)))
    return found


def over_lanes(value, lanes):
    parts = [value] * (lanes // LANES) + ([value[:, : lanes % LANES]] if lanes % LANES else [])
    return jnp.concatenate(parts, axis=1)


def short_keys(length):
    return (length - 1) // LANES * LANES


def attention_forward_kernel(
    len_ref, mixed_ref, m0_ref, x_ref, x0_ref, valid_ref, wo_ref, bo_ref, g_ref, c_ref,
    p_ref, ctx_ref, first_ref, low_ref, normal_ref, root_ref, xlow_ref, p0_ref, early_ref, n0_ref, r0_ref,
):
    seq = pl.program_id(0)
    length, width = x_ref.shape[2:]
    valid = valid_ref[0] > 0
    lane = lax.broadcasted_iota(jnp.int32, (1, LANES), 1)
    p0_ref[0] = jnp.zeros(p0_ref.shape[1:], LOW)

    def heads(keys):
        ones = jnp.ones((keys, LANES), LOW)
        for pair in range(width // LANES):
            query, key, value = pair_of(mixed_ref, m0_ref, pair, width, seq)
            right = jnp.concatenate([value[:keys], ones], axis=1)
            results = []
            for half in range(2):
                mask = jnp.where(lane // HD == half, SCALE, 0.0).astype(LOW)
                scores = dot_nt(query * mask, key[:keys])
                scores = jnp.where(valid[:, :keys], scores, NEGATIVE)
                exponent = jnp.exp(scores - jnp.max(scores, axis=-1, keepdims=True))
                both = dot(exponent.astype(LOW), right)
                share = 1.0 / both[:, LANES:]
                results.append(both[:, :LANES] * share)
                chance = (exponent * over_lanes(share, keys)).astype(LOW)
                p_ref[0, 2 * pair + half, :, 0:keys] = chance
                p0_ref[0, 2 * pair + half : 2 * pair + half + 1, 0:keys] = chance[0:1, :]
            ctx_ref[0, :, pl.ds(pair * LANES, LANES)] = jnp.where(lane < HD, results[0], results[1]).astype(LOW)

    short = short_keys(length)

    @pl.when(len_ref[seq] <= short)
    def _():
        heads(short)

    @pl.when(len_ref[seq] > short)
    def _():
        heads(length)

    rows = lax.broadcasted_iota(jnp.int32, (length, 1), 0)
    inputs = jnp.where(rows == 0, pick(x0_ref, seq), x_ref[0, 0].astype(F32))
    xlow_ref[0] = inputs.astype(LOW)
    hidden = inputs + dot(ctx_ref[0], wo_ref[...]) + bo_ref[...].astype(F32)
    normal, root = norm_stats(hidden)
    first = normal * g_ref[...].astype(F32) + c_ref[...].astype(F32)
    first_ref[0] = first
    low_ref[0] = first.astype(LOW)
    normal_ref[0] = normal.astype(LOW)
    root_ref[0] = jnp.broadcast_to(root, root_ref.shape[1:])
    put(early_ref, seq, first[0:1, :], slice(0, width))
    put(early_ref, seq, ctx_ref[0, 0:1, :].astype(F32), slice(width, 2 * width))
    put(n0_ref, seq, normal[0:1, :])
    put(r0_ref, seq, jnp.broadcast_to(root[0:1, :], (1, LANES)))


def attention_forward(lengths, mixed, m0, x, x0, valid, wo, bo, gain, shift):
    count, length, wide = mixed.shape
    width = wide // 3
    heads = width // HD

    def per(*shape):
        return pl.BlockSpec((1,) + shape, lambda i: (i,) + (0,) * len(shape))

    row = fixed((1, width))
    return pl.pallas_call(
        attention_forward_kernel,
        grid=(count,),
        out_shape=(
            jax.ShapeDtypeStruct((count, heads, length, length), LOW),
            jax.ShapeDtypeStruct((count, length, width), LOW),
            jax.ShapeDtypeStruct((count, length, width), F32),
            jax.ShapeDtypeStruct((count, length, width), LOW),
            jax.ShapeDtypeStruct((count, length, width), LOW),
            jax.ShapeDtypeStruct((count, length, LANES), F32),
            jax.ShapeDtypeStruct((count, length, width), LOW),
            jax.ShapeDtypeStruct((count, ROW_TILE, length), LOW),
            jax.ShapeDtypeStruct((count, 2 * width), F32),
            jax.ShapeDtypeStruct((count, width), F32),
            jax.ShapeDtypeStruct((count, LANES), F32),
        ),
        in_specs=[
            pl.BlockSpec(memory_space=pltpu.SMEM),
            per(length, wide),
            fixed((count, wide)),
            pl.BlockSpec((1, 1, length, width), lambda i: (0, i, 0, 0)),
            fixed((count, width)),
            per(1, length),
            fixed((width, width)),
            row, row, row,
        ],
        out_specs=(
            per(heads, length, length),
            per(length, width),
            per(length, width),
            per(length, width),
            per(length, width),
            per(length, LANES),
            per(length, width),
            per(ROW_TILE, length),
            fixed((count, 2 * width)),
            fixed((count, width)),
            fixed((count, LANES)),
        ),
        compiler_params=params(60),
        cost_estimate=MUCH,
        name="attention_forward",
    )(lengths, mixed, m0, x, x0, valid, wo, bo, gain, shift)


def turn(into_ref, from_ref):
    wide = from_ref.shape[1]
    tile = 384 if wide % 384 == 0 else LANES
    for column in range(0, wide, tile):
        into_ref[column : column + tile, :] = from_ref[:, column : column + tile].T


def grad_rows(me_ref, half, at_ref, right, outs, shards, line, start=0, size=None, offset=0):
    span = at_ref.shape[0] // shards
    size = size or span
    pitch = outs[0].shape[0] // (shards // 2)
    per = max(1, shards // 2)
    while per > 1 and per * size > 512:
        per //= 2
    for group in range(0, shards, per):
        pieces = []
        for shard in range(group, group + per):
            at = pl.multiple_of(shard_at(me_ref[0], half, shard, shards, line) * span + start, ROW_TILE)
            pieces.append(at_ref[pl.ds(at, size), :])
        left = pieces[0] if per == 1 else jnp.concatenate(pieces, axis=0)
        result = dot(left, right).astype(LOW)
        out_ref = outs[0] if group < shards // 2 else outs[1]
        for index in range(per):
            at = (group + index) % (shards // 2) * pitch + offset
            out_ref[at : at + size, :] = result[index * size : (index + 1) * size]


def shard_at(me, half, place, shards, line):
    if shards != 16:
        return place
    first, second = BITS[half]
    corner = me ^ (0 if place & 8 else first) ^ (0 if place & 4 else second)
    return lax.rem(corner + 4 * (place & 3), shards) if line else corner ^ (12, 4, 8, 0)[place & 3]


def cut_up(span):
    return -(-span // (2 * ROW_TILE)) * ROW_TILE


def feed_forward_kernel(
    me_ref, scal_ref, x_ref, we_ref, be_ref, wc_hbm, first_ref, bc_ref, g_ref, c_ref, cot_ref,
    slope_ref, out_ref, zg_ref, fg_ref, sums_ref, wg_ref, z0_ref, r0_ref, cot0_ref, s0_ref,
    send0_ref, send1_ref, keep0_ref, keep1_ref,
    act_ref, wc_ref, feed_ref, low_ref, turned_ref, sem,
    *, chunks, tiles, shards,
):
    step = pl.program_id(0)
    length, width = first_ref.shape[1:]
    count = x_ref.shape[0] // length
    group = first_ref.shape[0]
    groups = count // group
    chunk = we_ref.shape[1]
    second = chunks + groups + 1
    copy = pltpu.make_async_copy(wc_hbm, wc_ref, sem)

    @pl.when(step == 0)
    def _():
        copy.start()

    @pl.when(step < chunks)
    def _():
        u = dot(x_ref[...], we_ref[...]) + be_ref[...].astype(F32)
        active, slope = gelu_both(u)
        active = active.astype(LOW)
        act_ref[:, pl.ds(pl.multiple_of(step * chunk, LANES), chunk)] = active
        slope_ref[...] = slope.astype(LOW)
        for part in range(count):
            s0_ref[part : part + 1, :] = slope[part * length : part * length + 1, :]

    def feed(seq):
        rows = pl.ds(pl.multiple_of(seq * group * length, ROW_TILE), group * length)
        feed_ref[lax.rem(seq, 2)] = dot(act_ref[rows, :], wc_ref[...])

    def norms(at):
        for one in range(group):
            norm(at, one)

    def norm(at, one):
        seq = at * group + one
        weight = scal_ref[seq]
        keep = scal_ref[count]
        normal, root = norm_stats(
            first_ref[one] + feed_ref[lax.rem(at, 2), one * length : (one + 1) * length, :] + bc_ref[...].astype(F32)
        )
        gain = g_ref[...].astype(F32)
        result = normal * gain + c_ref[...].astype(F32)
        cot = cot_ref[one].astype(F32)
        out_ref[one] = weight * result
        put(wg_ref, seq, jnp.sum(cot * result, axis=0, keepdims=True))
        put(z0_ref, seq, normal[0:1, :])
        put(cot0_ref, seq, cot[0:1, :])
        put(r0_ref, seq, jnp.broadcast_to(root[0:1, :], (1, LANES)))
        rows = lax.broadcasted_iota(jnp.int32, (length, 1), 0)
        grad = cot * jnp.where(rows == 0, weight * keep, weight)
        z_grad = norm_back(grad, gain, normal, root)
        zg_ref[one] = z_grad
        feed_grad = z_grad.astype(LOW)
        fg_ref[one] = feed_grad
        low_ref[pl.ds(pl.multiple_of(seq * length, ROW_TILE), length), :] = feed_grad
        sums_ref[0:1, :] += jnp.sum(grad * normal, axis=0, keepdims=True)
        sums_ref[1:2, :] += jnp.sum(grad, axis=0, keepdims=True)
        sums_ref[2:3, :] += jnp.sum(feed_grad.astype(F32), axis=0, keepdims=True)

    @pl.when(step == chunks)
    def _():
        copy.wait()
        sums_ref[...] = jnp.zeros(sums_ref.shape, F32)
        feed(0)

    @pl.when((step > chunks) & (step < second - 1))
    def _():
        feed(step - chunks)
        norms(step - chunks - 1)

    @pl.when(step == second - 1)
    def _():
        norms(groups - 1)

    @pl.when(step == second)
    def _():
        turn(turned_ref, low_ref)

    def grads(half, send_ref, keep_ref):
        tile = send_ref.shape[1]
        columns = pl.ds(pl.multiple_of((step - second) * tile, LANES), tile)
        right = act_ref[:, columns]
        grad_rows(me_ref, half, turned_ref, right, (send_ref, keep_ref), shards, False)

    @pl.when((step >= second) & (step < second + tiles))
    def _():
        grads(0, send0_ref, keep0_ref)

    @pl.when(step >= second + tiles)
    def _():
        grads(1, send1_ref, keep1_ref)


def feed_forward(me, scal, x, first, we, be, wc, bc, gain, shift, cot, shards):
    count, length, width = first.shape
    rows = count * length
    hidden = we.shape[1]
    chunk = 1024
    chunks = hidden // chunk
    tile = 512
    tiles = hidden // 2 // tile
    second = chunks + 1 + count // (2 if count % 2 == 0 else 1)

    group = 2 if count % 2 == 0 else 1
    groups = count // group

    def part(i):
        return jnp.minimum(i, chunks - 1)

    def seq(i):
        return jnp.clip(i - chunks - 1, 0, groups - 1)

    def early(i):
        return (0, jnp.clip(i - second, 0, tiles - 1))

    def late(i):
        return (0, jnp.clip(i - second - tiles, 0, tiles - 1))

    def per(*shape):
        return pl.BlockSpec((group,) + shape, lambda i: (seq(i),) + (0,) * len(shape))

    row = fixed((1, width))
    cut = jax.ShapeDtypeStruct((width // 2, hidden // 2), LOW)
    block = (width // 2, tile)
    return pl.pallas_call(
        functools.partial(feed_forward_kernel, chunks=chunks, tiles=tiles, shards=shards),
        grid=(second + 2 * tiles,),
        out_shape=(
            jax.ShapeDtypeStruct((rows, hidden), LOW),
            jax.ShapeDtypeStruct((count, length, width), F32),
            jax.ShapeDtypeStruct((count, length, width), F32),
            jax.ShapeDtypeStruct((count, length, width), LOW),
            jax.ShapeDtypeStruct((8, width), F32),
            jax.ShapeDtypeStruct((count, width), F32),
            jax.ShapeDtypeStruct((count, width), F32),
            jax.ShapeDtypeStruct((count, LANES), F32),
            jax.ShapeDtypeStruct((count, width), F32),
            jax.ShapeDtypeStruct((count, hidden), F32),
            cut, cut, cut, cut,
        ),
        in_specs=[
            pl.BlockSpec(memory_space=pltpu.SMEM),
            pl.BlockSpec(memory_space=pltpu.SMEM),
            fixed((rows, width)),
            pl.BlockSpec((width, chunk), lambda i: (0, part(i))),
            pl.BlockSpec((1, chunk), lambda i: (0, part(i))),
            ANYWHERE,
            per(length, width),
            row, row, row,
            per(length, width),
        ],
        out_specs=(
            pl.BlockSpec((rows, chunk), lambda i: (0, part(i))),
            per(length, width),
            per(length, width),
            per(length, width),
            fixed((8, width)),
            fixed((count, width)),
            fixed((count, width)),
            fixed((count, LANES)),
            fixed((count, width)),
            pl.BlockSpec((count, chunk), lambda i: (0, part(i))),
            pl.BlockSpec(block, early),
            pl.BlockSpec(block, late),
            pl.BlockSpec(block, early),
            pl.BlockSpec(block, late),
        ),
        scratch_shapes=[
            pltpu.VMEM((rows, hidden), LOW),
            pltpu.VMEM((hidden, width), LOW),
            pltpu.VMEM((2, group * length, width), F32),
            pltpu.VMEM((rows, width), LOW),
            pltpu.VMEM((width, rows), LOW),
            pltpu.SemaphoreType.DMA,
        ],
        compiler_params=params(60),
        cost_estimate=MUCH,
        name="feed_forward",
    )(me, scal, x, we, be, wc, first, bc, gain, shift, cot)


def feed_backward_kernel(
    me_ref, fg_ref, slope_ref, wc_ref, we_hbm, zg_ref, normal_ref, root_ref, g_ref, x_ref,
    eb_ref, hgrad_ref, ag_ref, sums_ref, h0_ref,
    es0_ref, es1_ref, ek0_ref, ek1_ref,
    hg_ref, hidden_ref, we_ref, back_ref, sem,
    *, chunks, shards,
):
    step = pl.program_id(0)
    length, width = zg_ref.shape[1:]
    count = fg_ref.shape[0] // length
    group = zg_ref.shape[0]
    groups = count // group
    chunk = slope_ref.shape[1]
    second = chunks + groups + 1
    copy = pltpu.make_async_copy(we_hbm, we_ref, sem)

    @pl.when(step == 0)
    def _():
        copy.start()

    @pl.when(step < chunks)
    def _():
        grad = (dot_nt(fg_ref[...], wc_ref[...]) * slope_ref[...].astype(F32)).astype(LOW)
        at = pl.multiple_of(step * chunk, LANES)
        hg_ref[:, pl.ds(at, chunk)] = grad
        eb_ref[...] = jnp.sum(grad.astype(F32), axis=0, keepdims=True)
        hidden_ref[pl.ds(at, chunk), :] = grad.T

    def feed(seq):
        rows = pl.ds(pl.multiple_of(seq * group * length, ROW_TILE), group * length)
        back_ref[lax.rem(seq, 2)] = dot_nt(hg_ref[rows, :], we_ref[...])

    def norms(at):
        for one in range(group):
            norm(at, one)

    def norm(at, one):
        seq = at * group + one
        grad = zg_ref[one] + back_ref[lax.rem(at, 2), one * length : (one + 1) * length, :]
        normal = normal_ref[one].astype(F32)
        h_grad = norm_back(grad, g_ref[...].astype(F32), normal, root_ref[one, :, 0:1])
        hgrad_ref[one] = h_grad
        put(h0_ref, seq, h_grad[0:1, :])
        attended = h_grad.astype(LOW)
        ag_ref[one] = attended
        sums_ref[0:1, :] += jnp.sum(grad * normal, axis=0, keepdims=True)
        sums_ref[1:2, :] += jnp.sum(grad, axis=0, keepdims=True)
        sums_ref[2:3, :] += jnp.sum(attended.astype(F32), axis=0, keepdims=True)

    @pl.when(step == chunks)
    def _():
        copy.wait()
        sums_ref[...] = jnp.zeros(sums_ref.shape, F32)
        feed(0)

    @pl.when((step > chunks) & (step < second - 1))
    def _():
        feed(step - chunks)
        norms(step - chunks - 1)

    @pl.when(step == second - 1)
    def _():
        norms(groups - 1)

    span = hidden_ref.shape[0] // shards
    first = cut_up(span)
    for half, outs, start, size in (
        (0, (es0_ref, ek0_ref), 0, first), (1, (es1_ref, ek1_ref), first, span - first)
    ):

        @pl.when(step == second + half)
        def _():
            grad_rows(me_ref, half, hidden_ref, x_ref[...], outs, shards, False, start, size)


def feed_backward(me, fg, slope, wc, we, zg, normal, root, gain, x, shards):
    count, length, width = zg.shape
    rows, hidden = slope.shape
    chunk = 1024
    chunks = hidden // chunk

    group = 2 if count % 2 == 0 else 1
    groups = count // group

    def part(i):
        return jnp.minimum(i, chunks - 1)

    def seq(i):
        return jnp.clip(i - chunks - 1, 0, groups - 1)

    def per(*shape):
        return pl.BlockSpec((group,) + shape, lambda i: (seq(i),) + (0,) * len(shape))

    rows_of = [cut_up(hidden // shards), hidden // shards - cut_up(hidden // shards)] * 2
    cuts = [(shards // 2 * size, width) for size in rows_of]
    return pl.pallas_call(
        functools.partial(feed_backward_kernel, chunks=chunks, shards=shards),
        grid=(chunks + groups + 3,),
        out_shape=(
            jax.ShapeDtypeStruct((1, hidden), F32),
            jax.ShapeDtypeStruct((count, length, width), F32),
            jax.ShapeDtypeStruct((count, length, width), LOW),
            jax.ShapeDtypeStruct((8, width), F32),
            jax.ShapeDtypeStruct((count, width), F32),
        )
        + tuple(jax.ShapeDtypeStruct(cut, LOW) for cut in cuts),
        in_specs=[
            pl.BlockSpec(memory_space=pltpu.SMEM),
            fixed((rows, width)),
            pl.BlockSpec((rows, chunk), lambda i: (0, part(i))),
            pl.BlockSpec((chunk, width), lambda i: (part(i), 0)),
            ANYWHERE,
            per(length, width),
            per(length, width),
            per(length, LANES),
            fixed((1, width)),
            fixed((rows, width)),
        ],
        out_specs=(
            pl.BlockSpec((1, chunk), lambda i: (0, part(i))),
            per(length, width),
            per(length, width),
            fixed((8, width)),
            fixed((count, width)),
        )
        + tuple(fixed(cut) for cut in cuts),
        scratch_shapes=[
            pltpu.VMEM((rows, hidden), LOW),
            pltpu.VMEM((hidden, rows), LOW),
            pltpu.VMEM((width, hidden), LOW),
            pltpu.VMEM((2, group * length, width), F32),
            pltpu.SemaphoreType.DMA,
        ],
        compiler_params=params(60),
        cost_estimate=MUCH,
        name="feed_backward",
    )(me, fg, slope, wc, we, zg, normal, root, gain, x)


def attention_backward_kernel(len_ref, ag_ref, wo_ref, p_ref, mixed_ref, m0_ref, ctx_ref, *refs):
    mg_ref, mg0_ref, sums_ref, dctx_ref = refs[-4:]
    step = pl.program_id(0)
    width = ag_ref.shape[2]

    @pl.when(step == 0)
    def _():
        sums_ref[...] = jnp.zeros(sums_ref.shape, F32)

    dctx_ref[...] = dot_nt(ag_ref[0], wo_ref[...]).astype(LOW)
    lane = lax.broadcasted_iota(jnp.int32, (1, LANES), 1)
    length = ag_ref.shape[1]

    def heads(keys):
        minus = jnp.full((keys, LANES), -1.0, LOW)
        for pair in range(width // LANES):
            query, key, value = pair_of(mixed_ref, m0_ref, pair, width, step)
            here = pl.ds(pair * LANES, LANES)
            grad = dctx_ref[:, here]
            left = jnp.concatenate([grad, grad * ctx_ref[0, :, here]], axis=1)
            right = jnp.concatenate([value[:keys], minus], axis=1)
            queries, turned_s, turned_p = [], [], []
            for half in range(2):
                mask = jnp.where(lane // HD == half, 1.0, 0.0).astype(LOW)
                chance = p_ref[0, 2 * pair + half, :, 0:keys]
                less = dot_nt(left * jnp.concatenate([mask, mask], axis=1), right)
                s_grad = (chance.astype(F32) * less).astype(LOW)
                queries.append(dot(s_grad, key[:keys]))
                turned_s.append(s_grad.T)
                turned_p.append(chance.T)
            keys_grad = dot(jnp.concatenate(turned_s, axis=0), query) * SCALE
            values_grad = dot(jnp.concatenate(turned_p, axis=0), grad)
            for which, (one, two) in enumerate(
                (
                    (queries[0] * SCALE, queries[1] * SCALE),
                    (keys_grad[:keys], keys_grad[keys:]),
                    (values_grad[:keys], values_grad[keys:]),
                )
            ):
                low = jnp.where(lane < HD, one, two).astype(LOW)
                columns = pl.ds(which * width + pair * LANES, LANES)
                mg_ref[0, 0 : low.shape[0], columns] = low
                if low.shape[0] < length:
                    mg_ref[0, low.shape[0] :, columns] = jnp.zeros((length - low.shape[0], LANES), LOW)
                put(mg0_ref, step, low[0:1, :].astype(F32), columns)
                if which != 1:
                    spot = slice(pair * LANES, (pair + 1) * LANES)
                    sums_ref[which // 2 : which // 2 + 1, spot] += jnp.sum(low.astype(F32), axis=0, keepdims=True)

    short = short_keys(length)

    @pl.when(len_ref[step] <= short)
    def _():
        heads(short)

    @pl.when(len_ref[step] > short)
    def _():
        heads(length)


def attention_backward(lengths, ag, wo, p, mixed, m0, ctx, after):
    count, length, wide = mixed.shape
    width = wide // 3
    heads = width // HD

    def per(*shape):
        return pl.BlockSpec((1,) + shape, lambda i: (i,) + (0,) * len(shape))

    return pl.pallas_call(
        attention_backward_kernel,
        grid=(count,),
        out_shape=(
            jax.ShapeDtypeStruct((count, length, wide), LOW),
            jax.ShapeDtypeStruct((count, wide), F32),
            jax.ShapeDtypeStruct((8, width), F32),
        ),
        in_specs=[
            pl.BlockSpec(memory_space=pltpu.SMEM),
            per(length, width),
            fixed((width, width)),
            per(heads, length, length),
            per(length, wide),
            fixed((count, wide)),
            per(length, width),
        ]
        + [ANYWHERE] * len(after),
        out_specs=(per(length, wide), fixed((count, wide)), fixed((8, width))),
        scratch_shapes=[pltpu.VMEM((length, width), LOW)],
        compiler_params=params(60),
        cost_estimate=MUCH,
        name="attention_backward",
    )(lengths, ag, wo, p, mixed, m0, ctx, *after)


def attention_grads_kernel(me_ref, mg_ref, ag_ref, x_ref, ctx_ref, mg0_ref, h0_ref, wi_hbm, *refs, shards):
    s0_ref, s1_ref, k0_ref, k1_ref, term_ref, turned_ref, other_ref, wi_ref, sem = refs[-9:]
    step = pl.program_id(0)
    copy = pltpu.make_async_copy(wi_hbm, wi_ref, sem)

    @pl.when(step == 0)
    def _():
        copy.start()

    @pl.when(step == 1)
    def _():
        copy.wait()
        term_ref[...] = h0_ref[...] + dot_nt(mg0_ref[...].astype(LOW), wi_ref[...])

    @pl.when(step == 0)
    def _():
        turn(turned_ref, mg_ref)
        turn(other_ref, ag_ref)

    span, other = turned_ref.shape[0] // shards, other_ref.shape[0] // shards
    first, last = cut_up(span), other - cut_up(other)
    for half, outs, in_rows, out_rows in (
        (0, (s0_ref, k0_ref), (0, first), (0, last)),
        (1, (s1_ref, k1_ref), (first, span - first), (last, other - last)),
    ):

        @pl.when(step == half)
        def _():
            grad_rows(me_ref, half, turned_ref, x_ref[...], outs, shards, True, *in_rows)
            grad_rows(me_ref, half, other_ref, ctx_ref[...], outs, shards, True, *out_rows, in_rows[1])


def attention_grads(me, mg, ag, x, ctx, mg0, h0, wi, after, shards):
    rows, wide = mg.shape
    width = wide // 3
    first = cut_up(wide // shards) + width // shards - cut_up(width // shards)
    cuts = [(shards // 2 * size, width) for size in (first, (wide + width) // shards - first)] * 2
    return pl.pallas_call(
        functools.partial(attention_grads_kernel, shards=shards),
        grid=(2,),
        out_shape=tuple(jax.ShapeDtypeStruct(cut, LOW) for cut in cuts) + (jax.ShapeDtypeStruct(h0.shape, F32),),
        in_specs=[
            pl.BlockSpec(memory_space=pltpu.SMEM),
            fixed((rows, wide)),
            fixed((rows, width)),
            fixed((rows, width)),
            fixed((rows, width)),
            fixed(mg0.shape),
            fixed(h0.shape),
            ANYWHERE,
        ]
        + [ANYWHERE] * len(after),
        out_specs=tuple(fixed(cut) for cut in cuts) + (fixed(h0.shape),),
        scratch_shapes=[
            pltpu.VMEM((wide, rows), LOW),
            pltpu.VMEM((width, rows), LOW),
            pltpu.VMEM(wi.shape, LOW),
            pltpu.SemaphoreType.DMA,
        ],
        compiler_params=params(60),
        cost_estimate=MUCH,
        name="attention_grads",
    )(me, mg, ag, x, ctx, mg0, h0, wi, *after)


def shard_groups(count, wide):
    span = wide // count
    first = [span * shard // HD for shard in range(count)]
    most = max((span * shard + span - 1) // HD - first[shard] + 1 for shard in range(count))
    return [min(one, wide // HD - most) for one in first], most


def input_grad_kernel(mg_ref, w_ref, hgrad_ref, sg_ref, p0_ref, fk_ref, fv_ref, fq_ref, *refs):
    out_ref = refs[-1]
    seq = pl.program_id(0)
    length, width = hgrad_ref.shape[1:]
    rows = lax.broadcasted_iota(jnp.int32, (length, 1), 0)
    back = dot_nt(mg_ref[0], w_ref[...]) + dot_tn(sg_ref[0], fk_ref[0]) + dot_tn(p0_ref[0], fv_ref[0])
    out_ref[0] = back + hgrad_ref[0] + jnp.where(rows == 0, pick(fq_ref, seq), 0.0)


def input_grad(mg, weight, hgrad, sg, p0, fk, fv, fq, after):
    count, length, wide = mg.shape
    width = wide // 3

    def per(*shape):
        return pl.BlockSpec((1,) + shape, lambda i: (i,) + (0,) * len(shape))

    return pl.pallas_call(
        input_grad_kernel,
        grid=(count,),
        out_shape=jax.ShapeDtypeStruct((count, length, width), F32),
        in_specs=[
            per(length, wide),
            fixed((width, wide)),
            per(length, width),
            per(ROW_TILE, length),
            per(ROW_TILE, length),
            per(ROW_TILE, width),
            per(ROW_TILE, width),
            fixed((count, width)),
        ]
        + [ANYWHERE] * len(after),
        out_specs=per(length, width),
        compiler_params=params(60),
        cost_estimate=MUCH,
        name="input_grad",
    )(mg, weight, hgrad, sg, p0, fk, fv, fq, *after)


def last_kernel(
    g0_ref, z0_ref, r2_ref, g2_ref, slope_ref, wc_ref, we_ref, n0_ref, r1_ref, g1_ref, wo_ref, wi_hbm,
    p0_ref, mixed_ref, m0_ref, x_ref, s2_ref, s1_ref, s0_ref, eb_ref, early_ref, emb_ref, summary_ref, *refs, groups
):
    (
        sg_ref, fk_ref, fv_ref, fq_ref, send_ref,
        fg_ref, ag_ref, hg_ref, eball_ref, coef_ref, sums_ref, pack_ref,
        zg_ref, acc_ref, hz_ref, dctx_ref, rows_ref, wi_ref, sem,
    ) = refs[-19:]
    step = pl.program_id(0)
    count, width = g0_ref.shape
    chunks = pl.num_programs(0) - count
    copy = pltpu.make_async_copy(wi_hbm, wi_ref, sem)

    @pl.when(step == 0)
    def _():
        copy.start()
        grad = g0_ref[...]
        z_grad = norm_back(grad, g2_ref[...].astype(F32), z0_ref[...], r2_ref[:, 0:1])
        zg_ref[...] = z_grad
        low = z_grad.astype(LOW)
        fg_ref[...] = low
        sums_ref[0:2, :] = s0_ref[0:2, :]
        sums_ref[6:7, :] = s2_ref[0:1, :] + jnp.sum(grad * z0_ref[...], axis=0, keepdims=True)
        sums_ref[7:8, :] = s2_ref[1:2, :] + jnp.sum(grad, axis=0, keepdims=True)
        sums_ref[5:6, :] = s2_ref[2:3, :] + jnp.sum(low.astype(F32), axis=0, keepdims=True)
        acc_ref[...] = jnp.zeros(acc_ref.shape, F32)

    @pl.when(step < chunks)
    def _():
        grad = (dot_nt(fg_ref[...], wc_ref[...]) * slope_ref[...].astype(F32)).astype(LOW)
        here = pl.ds(pl.multiple_of(step * wc_ref.shape[0], LANES), wc_ref.shape[0])
        hg_ref[:, here] = grad.astype(F32)
        eball_ref[0:1, here] = eb_ref[...] + jnp.sum(grad.astype(F32), axis=0, keepdims=True)
        acc_ref[...] += dot_nt(grad, we_ref[...])

    @pl.when(step == chunks - 1)
    def _():
        grad = zg_ref[...] + acc_ref[...]
        normal = n0_ref[...]
        h_grad = norm_back(grad, g1_ref[...].astype(F32), normal, r1_ref[:, 0:1])
        hz_ref[0:count, :] = h_grad
        low = h_grad.astype(LOW)
        ag_ref[...] = low.astype(F32)
        sums_ref[3:4, :] = s1_ref[0:1, :] + jnp.sum(grad * normal, axis=0, keepdims=True)
        sums_ref[4:5, :] = s1_ref[1:2, :] + jnp.sum(grad, axis=0, keepdims=True)
        sums_ref[2:3, :] = s1_ref[2:3, :] + jnp.sum(low.astype(F32), axis=0, keepdims=True)
        context_grad = dot_nt(low, wo_ref[...])
        dctx_ref[0:count, :] = context_grad
        copy.wait()
        heads = head_rows(width)
        spread_q = [jnp.where(heads, m0_ref[one : one + 1, 0:width], 0.0).astype(LOW) for one in range(count)]
        spread_v = [jnp.where(heads, context_grad[one : one + 1, :], 0.0).astype(LOW) for one in range(count)]
        from_key = dot_nt(jnp.concatenate(spread_q, axis=0), wi_ref[:, width : 2 * width]) * SCALE
        from_value = dot_nt(jnp.concatenate(spread_v, axis=0), wi_ref[:, 2 * width :])
        for one in range(count):
            fk_ref[one] = from_key[one * ROW_TILE : (one + 1) * ROW_TILE].astype(LOW)
            fv_ref[one] = from_value[one * ROW_TILE : (one + 1) * ROW_TILE].astype(LOW)

    @pl.when(step >= chunks)
    def _():
        seq = step - chunks
        heads = head_rows(width)
        own = dctx_ref[pl.ds(seq, 1), :]
        grad = jnp.where(heads, own, 0.0).astype(LOW)
        query0 = pick(m0_ref, seq, slice(0, width))
        key = with_first(mixed_ref[0, :, width : 2 * width], pick(m0_ref, seq, slice(width, 2 * width)))
        value = with_first(mixed_ref[0, :, 2 * width :], pick(m0_ref, seq, slice(2 * width, 3 * width)))
        chance_low = p0_ref[0]
        chance = chance_low.astype(F32)
        p_grad = dot_nt(grad, value)
        s_grad = (chance * (p_grad - jnp.sum(p_grad * chance, axis=-1, keepdims=True))).astype(LOW)
        dq = dot(s_grad, key)
        dq = jnp.sum(jnp.where(heads, dq, 0.0), axis=0, keepdims=True) * SCALE
        put(coef_ref, seq, dq, slice(0, width))
        put(coef_ref, seq, query0 * SCALE, slice(width, 2 * width))
        put(coef_ref, seq, own, slice(2 * width, 3 * width))
        inputs = x_ref[0]
        rows_ref[0, 0:1, :] = inputs[0:1, :].astype(F32)
        both = dot(jnp.concatenate([s_grad, chance_low], axis=0), inputs)
        rows_ref[1] = both[0:ROW_TILE]
        rows_ref[2] = both[ROW_TILE:]
        firsts, most = groups
        per = width // HD
        for shard, first in enumerate(firsts):
            for turn_of in range(most):
                which, head = divmod(first + turn_of, per)
                head = head if which else 0
                at = pl.ds(count + seq * most + turn_of, 1)
                pack_ref[shard, at, 0:width] = rows_ref[which, head : head + 1, :]
        sg_ref[0] = s_grad
        sums_ref[0:1, :] += dq
        held = jnp.sum(chance, axis=-1, keepdims=True)
        sums_ref[1:2, :] += jnp.sum(held * grad.astype(F32), axis=0, keepdims=True)

    @pl.when(step == pl.num_programs(0) - 1)
    def _():
        fq_ref[...] = dot_nt(coef_ref[:, 0:width].astype(LOW), wi_ref[:, 0:width]) + hz_ref[0:count, :]
        firsts, most = groups
        shards = len(firsts)
        starts, pitch, begin = parcel(count, shards, width, eball_ref.shape[1], most, emb_ref.shape[1])
        for shard in range(shards):
            for name, source in (("feed", fg_ref), ("attended", ag_ref), ("hidden", hg_ref), ("coef", coef_ref)):
                span = source.shape[1] // shards
                piece = source[:, shard * span : (shard + 1) * span].astype(F32)
                pack_ref[shard, 0:count, starts[name] : starts[name] + span] = piece
            pack_ref[shard, 0:count, starts["emb"] : starts["emb"] + emb_ref.shape[1]] = emb_ref[...].astype(F32)
            span = width // shards
            at = starts["vectors"]
            pack_ref[shard, count : count + 8, at : at + span] = sums_ref[:, shard * span : (shard + 1) * span]
            span = eball_ref.shape[1] // shards
            for line, column in enumerate(range(0, span, LANES)):
                size = min(LANES, span - column)
                piece = eball_ref[0:1, shard * span + column : shard * span + column + size]
                pack_ref[shard, count + 8 + line : count + 9 + line, at : at + size] = piece
            send_ref[shard, 0:begin, 0 : pitch - LANES] = pack_ref[shard, 0:begin, 0 : pitch - LANES].astype(LOW)
            send_ref[shard, 2 * count : begin, pitch - LANES :] = jnp.zeros((begin - 2 * count, LANES), LOW)
        for seq in range(count):
            lines = [(begin + 2 * seq, 0, pitch), (begin + 2 * seq + 1, 0, pitch)]
            lines += [(2 * seq, pitch - LANES, pitch), (2 * seq + 1, pitch - LANES, pitch)]
            at = 0
            for line, column, end in lines:
                while column < end and at < 3 * width:
                    source, start = (early_ref, at) if at < 2 * width else (summary_ref, at - 2 * width)
                    size = min(end - column, (2 * width if at < 2 * width else 3 * width) - at)
                    value = source[seq : seq + 1, start : start + size].astype(F32)
                    pack_ref[0, line : line + 1, column : column + size] = value
                    column += size
                    at += size
        early = pack_ref[0, begin : begin + 2 * count, :].astype(LOW)
        spare = pack_ref[0, 0 : 2 * count, pitch - LANES :].astype(LOW)
        for shard in range(shards):
            send_ref[shard, begin : begin + 2 * count, :] = early
            send_ref[shard, 0 : 2 * count, pitch - LANES :] = spare


def parcel(count, shards, width, hidden, most, emb):
    starts, at = {}, 0
    for name, span in (
        ("feed", width // shards), ("attended", width // shards), ("hidden", hidden // shards),
        ("coef", 3 * width // shards), ("emb", emb),
    ):
        starts[name] = at
        at += -(-span // LANES) * LANES
    starts["vectors"] = width
    pitch = max(at, width + LANES) + LANES
    return starts, pitch, -(-(count + max(most * count, 8 + -(-hidden // shards // LANES))) // 8) * 8


def last_rows(
    g0, z0, r2, g2, slope0, wc, we, n0, r1, g1, wo, wi, p0, mixed, m0, x, s2, s1, s0, eb, early, emb, summary, after, shards
):
    count, length, wide = mixed.shape
    width = wide // 3
    hidden = slope0.shape[1]
    chunk = 768
    chunks = hidden // chunk
    groups = shard_groups(shards, wide)
    _, pitch, begin = parcel(count, shards, width, hidden, groups[1], emb.shape[1])
    send = (shards, begin + 2 * count, pitch)

    def part(i):
        return jnp.minimum(i, chunks - 1)

    def seq(i):
        return jnp.maximum(i - chunks, 0)

    def per(*shape):
        return pl.BlockSpec((1,) + shape, lambda i: (seq(i),) + (0,) * len(shape))

    row = fixed((1, width))
    rows = fixed((count, width))
    return pl.pallas_call(
        functools.partial(last_kernel, groups=groups),
        grid=(chunks + count,),
        out_shape=(
            jax.ShapeDtypeStruct((count, ROW_TILE, length), LOW),
            jax.ShapeDtypeStruct((count, ROW_TILE, width), LOW),
            jax.ShapeDtypeStruct((count, ROW_TILE, width), LOW),
            jax.ShapeDtypeStruct((count, width), F32),
            jax.ShapeDtypeStruct(send, LOW),
        ),
        in_specs=[
            rows, rows, fixed((count, LANES)), row,
            pl.BlockSpec((count, chunk), lambda i: (0, part(i))),
            pl.BlockSpec((chunk, width), lambda i: (part(i), 0)),
            pl.BlockSpec((width, chunk), lambda i: (0, part(i))),
            rows, fixed((count, LANES)), row,
            fixed((width, width)),
            ANYWHERE,
            per(ROW_TILE, length),
            per(length, wide),
            fixed((count, wide)),
            per(length, width),
            fixed((8, width)),
            fixed((8, width)),
            fixed((8, width)),
            pl.BlockSpec((1, chunk), lambda i: (0, part(i))),
            fixed(early.shape),
            fixed(emb.shape),
            fixed(summary.shape),
        ]
        + [ANYWHERE] * len(after),
        out_specs=(
            per(ROW_TILE, length),
            fixed((count, ROW_TILE, width)),
            fixed((count, ROW_TILE, width)),
            rows,
            fixed(send),
        ),
        scratch_shapes=[
            pltpu.VMEM((count, width), LOW),
            pltpu.VMEM((count, width), F32),
            pltpu.VMEM((count, hidden), F32),
            pltpu.VMEM((8, hidden), F32),
            pltpu.VMEM((count, wide), F32),
            pltpu.VMEM((8, width), F32),
            pltpu.VMEM(send, F32),
            pltpu.VMEM((count, width), F32),
            pltpu.VMEM((count, width), F32),
            pltpu.VMEM((8, width), F32),
            pltpu.VMEM((8, width), F32),
            pltpu.VMEM((3, ROW_TILE, width), F32),
            pltpu.VMEM((width, wide), LOW),
            pltpu.SemaphoreType.DMA,
        ],
        compiler_params=params(60),
        cost_estimate=LITTLE,
        name="last_rows",
    )(g0, z0, r2, g2, slope0, wc, we, n0, r1, g1, wo, wi, p0, mixed, m0, x, s2, s1, s0, eb, early, emb, summary, *after)


def flip(value, bit, count):
    return lax.ppermute(value, "rows", [(i, i ^ bit) for i in range(count)])


def first_stage(parts, count):
    return [flip(parts[half], BITS[half][0], count) for half in range(2)]


def second_stage(sends, count):
    return [flip(sends[half], BITS[half][1], count) for half in range(2)]


def sum_low(left_ref, right_ref):
    return (left_ref[...].astype(F32) + right_ref[...].astype(F32)).astype(LOW)


def first_sum_kernel(a0, a1, b0, b1, ga0, ga1, gb0, gb1, *refs):
    sa, sb, ka, kb = refs[-4:]
    sa[...] = sum_low(a0, ga0)
    ka[...] = sum_low(a1, ga1)
    sb[...] = sum_low(b0, gb0)
    kb[...] = sum_low(b1, gb1)


def first_sum(parts, got, after):
    keep0, keep1 = parts[2:]
    rows, width = keep0.shape
    tiles = 4
    block = (rows // 2 // tiles, width)
    top = pl.BlockSpec(block, lambda i: (i, 0))
    bottom = pl.BlockSpec(block, lambda i: (i + tiles, 0))
    result = pl.pallas_call(
        first_sum_kernel,
        grid=(tiles,),
        out_shape=(jax.ShapeDtypeStruct((rows // 2, width), LOW),) * 4,
        in_specs=[top, bottom] * 4 + [ANYWHERE] * len(after),
        out_specs=(top,) * 4,
        compiler_params=params(60),
        cost_estimate=LITTLE,
        name="first_sum",
    )(keep0, keep0, keep1, keep1, got[0], got[0], got[1], got[1], *after)
    return result[:2], result[2:]


def second_sum_kernel(*refs, jobs):
    step = pl.program_id(0)
    outs = list(refs[-sum(job[0] for job in jobs) :])
    for index, (count, stacked) in enumerate(jobs):
        a, b, ga, gb = refs[4 * index : 4 * index + 4]
        rows, half = a.shape
        left, right = sum_low(a, ga), sum_low(b, gb)
        for number in range(count):
            out = outs.pop(0)

            @pl.when(step * count // 4 == number)
            def _():
                if stacked:
                    out[:rows, :] = left
                    out[rows:, :] = right
                else:
                    out[:, :half] = left
                    out[:, half:] = right


def second_sum(buckets, after):
    arrays, blocks, shapes, places_out = [], [], [], []
    for keeps, got, number, stacked in buckets:
        rows, width = keeps[0].shape
        tile = rows // 4
        arrays += [*keeps, *got]
        blocks += [pl.BlockSpec((tile, width), lambda i: (i, 0))] * 4
        wide, out_tile = (width, 2 * tile) if stacked else (2 * width, tile)
        shapes += [jax.ShapeDtypeStruct((4 // number * out_tile, wide), LOW)] * number
        if number == 4:
            places_out += [fixed((out_tile, wide))] * 4
        else:
            places_out += [
                pl.BlockSpec((out_tile, wide), lambda i: (jnp.minimum(i, 1), 0)),
                pl.BlockSpec((out_tile, wide), lambda i: (jnp.maximum(i - 2, 0), 0)),
            ]
    return pl.pallas_call(
        functools.partial(second_sum_kernel, jobs=tuple(bucket[2:] for bucket in buckets)),
        grid=(4,),
        out_shape=tuple(shapes),
        in_specs=blocks + [ANYWHERE] * len(after),
        out_specs=tuple(places_out),
        compiler_params=params(60),
        cost_estimate=LITTLE,
        name="second_sum",
    )(*arrays, *after)


def third_sum_kernel(*refs, jobs):
    outs = refs[-2 * jobs :]
    for job in range(jobs):
        a, ga = refs[2 * job : 2 * job + 2]
        for index, out in enumerate(outs[2 * job : 2 * job + 2]):

            @pl.when(pl.program_id(0) == index)
            def _():
                out[...] = sum_low(a, ga)


def third_sum(buckets, after):
    arrays, blocks, shapes = [], [], []
    for keep, got in buckets:
        rows, width = keep.shape
        arrays += [keep, got]
        blocks += [pl.BlockSpec((rows // 2, width), lambda i: (i, 0))] * 2
        shapes += [(rows // 2, width)] * 2
    return pl.pallas_call(
        functools.partial(third_sum_kernel, jobs=len(buckets)),
        grid=(2,),
        out_shape=tuple(jax.ShapeDtypeStruct(shape, LOW) for shape in shapes),
        in_specs=blocks + [ANYWHERE] * len(after),
        out_specs=tuple(fixed(shape) for shape in shapes),
        compiler_params=params(60),
        cost_estimate=MUCH,
        name="third_sum",
    )(*arrays, *after)


def wide_sum(left, right):
    return left.astype(F32) + right.astype(F32)


def line_stage(totals, count):
    got = [totals[0]]
    for step in range(1, count // 4):
        got.append(lax.ppermute(totals[step], "rows", [(i, (i + 4 * step) % count) for i in range(count)]))
    return got


def rest_kernel(*refs, parts):
    got, fix_ref = refs[:parts], refs[parts]
    in_ref, out_ref = refs[-2:]
    span, other = in_ref.shape[0], out_ref.shape[0]
    first, last = cut_up(span), other - cut_up(other)
    total = got[0][...].astype(F32)
    for one in got[1:]:
        total = total + one[...].astype(F32)
    for into, start, size, at in (
        (in_ref, 0, first, 0),
        (out_ref, 0, last, first),
        (in_ref, first, span - first, first + last),
        (out_ref, last, other - last, span + last),
    ):
        add = start + (span if into is out_ref else 0)
        into[start : start + size, :] = total[at : at + size] + fix_ref[add : add + size, :]


def rest_sum(got, fix, span, after):
    rows, width = fix.shape
    return pl.pallas_call(
        functools.partial(rest_kernel, parts=len(got)),
        out_shape=(jax.ShapeDtypeStruct((span, width), F32), jax.ShapeDtypeStruct((rows - span, width), F32)),
        in_specs=[pl.BlockSpec(memory_space=pltpu.VMEM)] * (len(got) + 1) + [ANYWHERE] * len(after),
        compiler_params=params(60),
        name="rest_sum",
    )(*got, fix, *after)


def whole_grad(full):
    return lax.psum_scatter(full.astype(F32), "rows", scatter_dimension=0, tiled=True)


def body(
    token_states, lengths, key_mask, cotangent, attention_in, attention_bias, attention_out, output_bias,
    gain_one, shift_one, expand_weight, expand_bias, contract_weight, contract_bias, gain_two, shift_two,
    projection, passage_table, candidates,
):
    section = lax.axis_index("section")
    is_first = section == 0
    count = lax.axis_size("rows")
    me = lax.axis_index("rows")
    tokens = token_states[0]
    seqs, length, width = tokens.shape
    rows = seqs * length

    bi = attention_bias[0]
    wi, wo, we, wc = attention_in[0], attention_out[0], expand_weight[0], contract_weight[0]
    bo, g1, c1, be, bc, g2, c2 = output_bias, gain_one, shift_one, expand_bias, contract_bias, gain_two, shift_two
    weights = (wi, bi, wo, bo, g1, c1, we, be, wc, bc, g2, c2)
    positions = jnp.arange(length)
    valid = (positions[None, :] < lengths[0][:, None]) & (key_mask[0] == 1) | (positions[None, :] == 0)
    valid = valid.astype(F32)[:, None, :]
    staged = count == 16 and width // count % ROW_TILE == 0
    cuts = count if staged else 2
    place = me.reshape(1).astype(jnp.int32)

    retrieved = jnp.take(passage_table, candidates, axis=0).astype(F32)
    mixed, x0 = project(token_states, wi, bi)
    message = first_rows(mixed, valid, x0, weights, projection)
    received = lax.ppermute(message, "section", [(0, 1)])
    summary_in, embedding_in = received[:, :width], received[:, width:]
    x0 = x0 + summary_in.astype(F32)
    in_bias = jnp.concatenate([bi[0], jnp.zeros_like(bi[0]), bi[1]])
    mixed0 = (dot(x0.astype(LOW), wi) + in_bias.astype(F32)).astype(LOW).astype(F32)
    chance, context, first, first_low, normal, root, x_low, chance0, early, n0, r1 = attention_forward(
        lengths[0], mixed, mixed0, token_states, x0, valid, wo, bo, g1, c1
    )
    match = jnp.sum(embedding_in.astype(F32)[:, None, :] * retrieved, axis=-1)
    chances = jax.nn.softmax(match, axis=-1)
    weight = TOPK * chances[:, 0]
    scal = jnp.concatenate([jnp.where(is_first, 1.0, weight), jnp.where(is_first, 0.0, 1.0)[None]]).astype(F32)
    first_flat = first_low.reshape(rows, width)
    slope, out, z_grad, feed_grad, sums_two, weight_grads, z0, r2, cot0, slope0, *contract = feed_forward(
        place, scal, first_flat, first, we, be, wc, bc, g2, c2, cotangent[0], cuts
    )

    contract_got = first_stage(contract, count) if staged else None
    expand_sum, h_grad, attended, sums_one, h0, *expand = feed_backward(
        place, feed_grad.reshape(rows, width), slope, wc, we, z_grad, normal, root, g1, first_flat, cuts
    )
    contract_send = ()
    if staged:
        contract_send, contract_keep = first_sum(contract, contract_got, (h0,))
        contract_got = second_stage(contract_send, count)
        expand_got = first_stage(expand, count)
    mixed_grad, mg0, sums_in = attention_backward(
        lengths[0], attended, wo, chance, mixed, mixed0, context, tuple(contract_send)
    )
    after = ()
    if staged:
        expand_send, expand_keep = first_sum(expand, expand_got, (mg0,))
        expand_got = second_stage(expand_send, count)
        after = (expand_send[0],)
    *rest, reader_term = attention_grads(
        place, mixed_grad.reshape(rows, 3 * width), attended.reshape(rows, width), x_low.reshape(rows, width),
        context.reshape(rows, width), mg0, h0, wi, after, cuts,
    )
    rest_got = first_stage(rest, count) if staged else None

    after = (rest[0],)
    if staged:
        contract_send, contract_keep, expand_send, expand_keep = second_sum(
            ((contract_keep, contract_got, 2, False), (expand_keep, expand_got, 2, True)), (rest[0],)
        )
        contract_got = flip(contract_send, 4, count)
        expand_got = flip(expand_send, 4, count)
        after = (expand_send, contract_send)
    grad_weight = jnp.sum(weight_grads, axis=1)
    one = jnp.zeros((TOPK,), F32).at[0].set(1.0)
    grad_match = (grad_weight[:, None] * weight[:, None] * (one[None, :] - chances)).astype(LOW)
    embedding_grad = jnp.sum(grad_match.astype(F32)[:, :, None] * retrieved, axis=1).astype(LOW)
    if staged:
        reader_term, _ = lax.optimization_barrier((reader_term, expand_send))
    reader_term = reader_term.astype(LOW)
    back = lax.ppermute(jnp.concatenate([reader_term, embedding_grad], axis=1), "section", [(1, 0)])
    embedding_used = jnp.where(is_first, back[:, width:], embedding_grad)
    summary_grad = dot_nt(back[:, width:], projection) + back[:, :width].astype(F32)
    grad_zero = jnp.where(is_first, cot0 + summary_grad, 0.0)
    used_summary = jnp.where(is_first, message[:, :width], summary_in)
    s_zero, from_key, from_value, from_query, parcels = last_rows(
        grad_zero, z0, r2, g2, slope0, wc, we, n0, r1, g1, wo, wi, chance0, mixed, mixed0, x_low,
        sums_two, sums_one, sums_in, expand_sum, early, embedding_used, used_summary, after, count,
    )
    after = ()
    if staged:
        rest_send, rest_keep = first_sum(rest, rest_got, (parcels,))
        rest_got = second_stage(rest_send, count)
        after = (rest_send[0],)

    got = lax.all_to_all(parcels, "rows", 0, 0, tiled=True)
    if staged:
        contract_send, contract_keep, expand_send, expand_keep = third_sum(
            ((contract_keep, contract_got), (expand_keep, expand_got)), after
        )
        contract_got = flip(contract_send, 8, count)
        expand_got = flip(expand_send, 8, count)
        after = (expand_send,)
    x_grad = input_grad(mixed_grad, wi, h_grad, s_zero, chance0, from_key, from_value, from_query, after)
    if staged:
        rest = second_sum(((rest_keep, rest_got, 4, True),), (x_grad,))
        rest_got = line_stage(rest, count)
        got, me, _ = lax.optimization_barrier((got, me, rest))
    else:
        top, bottom = jnp.concatenate(contract[:2], axis=1), jnp.concatenate(contract[2:], axis=1)
        contract = whole_grad(jnp.concatenate([top, bottom], axis=0))
        expand = whole_grad(jnp.concatenate(expand, axis=0))
        inner = 3 * width // 4
        rest = [jnp.concatenate([part[cut] for part in rest]) for cut in (slice(0, inner), slice(inner, None))]
        rest = [whole_grad(part) for part in rest]
    hidden = we.shape[1]
    span = 3 * width // count
    firsts, most = shard_groups(count, 3 * width)
    starts, pitch, begin = parcel(seqs, count, width, hidden, most, embedding_used.shape[1])

    def sent(name, size):
        return got[:, :seqs, starts[name] : starts[name] + size].reshape(count * seqs, size)

    factors = jnp.concatenate(
        [
            got[:, begin : begin + 2 * seqs].reshape(count * seqs, 2 * pitch),
            got[:, : 2 * seqs, pitch - LANES :].reshape(count * seqs, 2 * LANES),
        ],
        axis=1,
    )
    first_all, context_all, summary_all = (factors[:, i * width : (i + 1) * width] for i in range(3))
    active_all = gelu_both(dot(first_all, we) + be.astype(F32))[0].astype(LOW)
    contract_fix = dot_tn(sent("feed", width // count), active_all)
    projection_grad = dot_tn(summary_all, sent("emb", embedding_used.shape[1]))
    head = (span * me + jnp.arange(span)) // HD - jnp.asarray(firsts, jnp.int32)[me]
    chosen = (head[None, :] == jnp.arange(most)[:, None]).astype(LOW)
    coefs = (sent("coef", span)[:, None, :] * chosen[None]).reshape(count * seqs * most, span)
    groups = got[:, seqs : seqs + seqs * most, :width].reshape(count * seqs * most, width)
    fix = jnp.concatenate([dot_tn(coefs, groups), dot_tn(sent("attended", width // count), context_all)], axis=0)
    expand_fix = dot_tn(sent("hidden", hidden // count), first_all)
    at = starts["vectors"]
    packed = jnp.sum(got[:, seqs : seqs + 8, at : at + width // count].astype(F32), axis=0)
    lines = -(-hidden // count // LANES)
    e_bias = got[:, seqs + 8 : seqs + 8 + lines, at : at + LANES].astype(F32)
    e_bias = jnp.sum(e_bias, axis=0).reshape(-1)[: hidden // count]
    if staged:
        held = (contract_got, expand_got, fix, contract_fix, expand_fix, projection_grad, packed, e_bias)
        contract_got, expand_got, fix, contract_fix, expand_fix, projection_grad, packed, e_bias = (
            lax.optimization_barrier(held)
        )
        contract = contract_fix + wide_sum(contract_keep, contract_got)
        expand = wide_sum(expand_keep, expand_got) + expand_fix
        attention_in_grad, attention_out_grad = rest_sum(rest_got, fix, span, (contract, expand))
    else:
        contract = contract + contract_fix
        attention_in_grad, attention_out_grad = rest[0] + fix[:span], rest[1] + fix[span:]
        expand = expand + expand_fix
    q_bias, v_bias, o_bias, gain1, shift1, c_bias, gain2, shift2 = (packed[i] for i in range(8))
    return (
        out[None],
        x_grad[None],
        attention_in_grad.T[None],
        jnp.stack([q_bias, v_bias])[None],
        attention_out_grad.T[None],
        o_bias[None],
        gain1[None],
        shift1[None],
        expand.T[None],
        e_bias[None],
        contract.T[None],
        c_bias[None],
        gain2[None],
        shift2[None],
        projection_grad,
    )


def solution(mesh):
    in_specs = (
        P("section", "rows", None, None),
        P("section", "rows"),
        P("section", "rows", None),
        P("section", "rows", None, None),
        P("section", None, None),
        P("section", None, None),
        P("section", None, None),
        P("section", None),
        P("section", None),
        P("section", None),
        P("section", None, None),
        P("section", None),
        P("section", None, None),
        P("section", None),
        P("section", None),
        P("section", None),
        P(),
        P(),
        P("rows", None),
    )
    out_specs = (
        P("section", "rows", None, None),
        P("section", "rows", None, None),
        P("section", None, "rows"),
        P("section", None, "rows"),
        P("section", None, "rows"),
        P("section", "rows"),
        P("section", "rows"),
        P("section", "rows"),
        P("section", None, "rows"),
        P("section", "rows"),
        P("section", None, "rows"),
        P("section", "rows"),
        P("section", "rows"),
        P("section", "rows"),
        P(),
    )
    return jax.shard_map(body, mesh=mesh, in_specs=in_specs, out_specs=out_specs, check_vma=False)
```

```python
import functools
import math

import jax
import jax.numpy as jnp
from jax import lax
from jax.experimental import pallas as pl
from jax.experimental.pallas import tpu as pltpu
from jax.sharding import PartitionSpec as P

HD = 64
TOPK = 8
NEGATIVE = -1000000000.0
SCALE = 1.0 / math.sqrt(HD)
LANES = 128
ROW_TILE = 16
F32 = jnp.float32
LOW = jnp.bfloat16
NT = (((1,), (1,)), ((), ()))
TN = (((0,), (0,)), ((), ()))
MIB = 1 << 20
BITS = ((1, 2), (2, 1))


def dot(left, right):
    return jnp.dot(left, right, preferred_element_type=F32)


def dot_nt(left, right):
    return lax.dot_general(left, right, NT, preferred_element_type=F32)


def dot_tn(left, right):
    return lax.dot_general(left, right, TN, preferred_element_type=F32)


def params(limit):
    return pltpu.CompilerParams(vmem_limit_bytes=limit * MIB)


MUCH = pl.CostEstimate(flops=100 * 1000**3, bytes_accessed=50 * MIB, transcendentals=0)
LITTLE = pl.CostEstimate(flops=1, bytes_accessed=1, transcendentals=0)


ANYWHERE = pl.BlockSpec(memory_space=pl.ANY)


def fixed(shape):
    return pl.BlockSpec(shape, lambda *ids: (0,) * len(shape), pipeline_mode=pl.Buffered(1))


def norm_stats(hidden):
    mean = jnp.mean(hidden, axis=-1, keepdims=True)
    centered = hidden - mean
    root = lax.rsqrt(jnp.mean(centered * centered, axis=-1, keepdims=True) + 1e-12)
    return centered * root, root


def norm_back(grad, gain, normal, root):
    scaled = gain * grad
    mean = jnp.mean(scaled, axis=-1, keepdims=True)
    along = jnp.mean(scaled * normal, axis=-1, keepdims=True)
    return root * (scaled - mean - normal * along)


def gelu_both(u):
    phi = 0.5 + 0.5 * lax.erf(u * (1.0 / math.sqrt(2.0)))
    slope = phi + u * (jnp.exp(-0.5 * u * u) * (1.0 / math.sqrt(2.0 * math.pi)))
    return u * phi, slope


def head_rows(width):
    shape = (ROW_TILE, width)
    return lax.broadcasted_iota(jnp.int32, shape, 1) // HD == lax.broadcasted_iota(jnp.int32, shape, 0)


def pick(ref, row, columns=slice(None)):
    block = ref[:, columns]
    rows = lax.broadcasted_iota(jnp.int32, (block.shape[0], 1), 0)
    return jnp.sum(jnp.where(rows == row, block, 0.0), axis=0, keepdims=True)


def put(ref, row, value, columns=slice(None)):
    block = ref[:, columns]
    rows = lax.broadcasted_iota(jnp.int32, (block.shape[0], 1), 0)
    ref[:, columns] = jnp.where(rows == row, value, block)


def project_kernel(x_ref, w_ref, b_ref, o_ref, x0_ref):
    step = pl.program_id(0)
    bias = b_ref[...].astype(F32)
    bias = jnp.where(step == 0, bias[0:1, :], jnp.where(step == 2, bias[1:2, :], 0.0))
    for part in range(x_ref.shape[1]):
        o_ref[part] = (dot(x_ref[0, part], w_ref[...]) + bias).astype(LOW)
        x0_ref[part : part + 1, :] = x_ref[0, part, 0:1, :].astype(F32)


def project(x, weight, bias):
    _, count, length, width = x.shape
    return pl.pallas_call(
        project_kernel,
        grid=(3,),
        out_shape=(
            jax.ShapeDtypeStruct((count, length, 3 * width), LOW),
            jax.ShapeDtypeStruct((count, width), F32),
        ),
        in_specs=[
            fixed((1, count, length, width)),
            pl.BlockSpec((width, width), lambda i: (0, i)),
            fixed((2, width)),
        ],
        out_specs=(pl.BlockSpec((count, length, width), lambda i: (0, 0, i)), fixed((count, width))),
        compiler_params=params(32),
        cost_estimate=pl.CostEstimate(flops=6 * count * length * width * width, bytes_accessed=14 * MIB, transcendentals=0),
        name="project_qkv",
    )(x, weight, bias)


def first_rows_kernel(
    mixed_ref, valid_ref, x0_ref, wo_ref, bo_ref, g1_ref, c1_ref, we_ref, be_ref, wc_ref, bc_ref,
    g2_ref, c2_ref, pr_ref, out_ref, ctx_ref, first_ref, acc_ref,
):
    step = pl.program_id(0)
    count = x0_ref.shape[0]
    width = wo_ref.shape[0]
    chunks = pl.num_programs(0) - count

    @pl.when(step < count)
    def _():
        heads = head_rows(width)
        query = mixed_ref[0, 0:1, 0:width].astype(F32) * SCALE
        spread = jnp.where(heads, query, 0.0).astype(LOW)
        scores = dot_nt(spread, mixed_ref[0, :, width : 2 * width])
        scores = jnp.where(valid_ref[0] > 0, scores, NEGATIVE)
        exponent = jnp.exp(scores - jnp.max(scores, axis=-1, keepdims=True))
        chance = (exponent / jnp.sum(exponent, axis=-1, keepdims=True)).astype(LOW)
        context = dot(chance, mixed_ref[0, :, 2 * width :])
        context = jnp.sum(jnp.where(heads, context, 0.0), axis=0, keepdims=True)
        ctx_ref[pl.ds(step, 1), :] = context

    @pl.when(step == count - 1)
    def _():
        hidden = x0_ref[...] + dot(ctx_ref[0:count, :].astype(LOW), wo_ref[...]) + bo_ref[...].astype(F32)
        normal, root = norm_stats(hidden)
        first_ref[...] = normal * g1_ref[...].astype(F32) + c1_ref[...].astype(F32)

    @pl.when(step >= count)
    def _():
        u = dot(first_ref[...].astype(LOW), we_ref[...]) + be_ref[...].astype(F32)
        active, slope = gelu_both(u)
        part = dot(active.astype(LOW), wc_ref[...])

        @pl.when(step == count)
        def _():
            acc_ref[...] = part

        @pl.when(step > count)
        def _():
            acc_ref[...] += part

    @pl.when(step == pl.num_programs(0) - 1)
    def _():
        normal, root = norm_stats(first_ref[...] + acc_ref[...] + bc_ref[...].astype(F32))
        summary = (normal * g2_ref[...].astype(F32) + c2_ref[...].astype(F32)).astype(LOW)
        out_ref[:, 0:width] = summary
        out_ref[:, width:] = dot(summary, pr_ref[...]).astype(LOW)


def first_rows(mixed, valid, x0, weights, projection):
    (_, _, wo, bo, g1, c1, we, be, wc, bc, g2, c2) = weights
    count, length, wide = mixed.shape
    width, hidden = we.shape
    chunk = 768
    chunks = hidden // chunk
    proj = projection.shape[1]

    def seq(i):
        return jnp.minimum(i, count - 1)

    def part(i):
        return jnp.maximum(i - count, 0)

    row = fixed((1, width))
    return pl.pallas_call(
        first_rows_kernel,
        grid=(count + chunks,),
        out_shape=jax.ShapeDtypeStruct((count, width + proj), LOW),
        in_specs=[
            pl.BlockSpec((1, length, wide), lambda i: (seq(i), 0, 0)),
            pl.BlockSpec((1, 1, length), lambda i: (seq(i), 0, 0)),
            fixed((count, width)),
            fixed((width, width)),
            row, row, row,
            pl.BlockSpec((width, chunk), lambda i: (0, part(i))),
            pl.BlockSpec((1, chunk), lambda i: (0, part(i))),
            pl.BlockSpec((chunk, width), lambda i: (part(i), 0)),
            row, row, row,
            fixed((width, proj)),
        ],
        out_specs=fixed((count, width + proj)),
        scratch_shapes=[
            pltpu.VMEM((8, width), F32),
            pltpu.VMEM((count, width), F32),
            pltpu.VMEM((count, width), F32),
        ],
        compiler_params=params(32),
        cost_estimate=pl.CostEstimate(flops=40 * MIB, bytes_accessed=17 * MIB, transcendentals=0),
        name="first_rows_forward",
    )(mixed, valid, x0, wo, bo, g1, c1, we, be, wc, bc, g2, c2, projection)


def with_first(block, row):
    rows = lax.broadcasted_iota(jnp.int32, (ROW_TILE, 1), 0)
    top = jnp.where(rows == 0, row, block[0:ROW_TILE].astype(F32)).astype(block.dtype)
    return jnp.concatenate([top, block[ROW_TILE:]], axis=0)


def pair_of(mixed_ref, m0_ref, pair, width, seq):
    found = []
    for which in range(3):
        columns = pl.ds(which * width + pair * LANES, LANES)
        found.append(with_first(mixed_ref[0, :, columns], pick(m0_ref, seq, columns)))
    return found


def over_lanes(value, lanes):
    parts = [value] * (lanes // LANES) + ([value[:, : lanes % LANES]] if lanes % LANES else [])
    return jnp.concatenate(parts, axis=1)


def short_keys(length):
    return (length - 1) // LANES * LANES


def attention_forward_kernel(
    len_ref, mixed_ref, m0_ref, x_ref, x0_ref, valid_ref, wo_ref, bo_ref, g_ref, c_ref,
    p_ref, ctx_ref, first_ref, low_ref, normal_ref, root_ref, xlow_ref, p0_ref, early_ref, n0_ref, r0_ref,
):
    seq = pl.program_id(0)
    length, width = x_ref.shape[2:]
    valid = valid_ref[0] > 0
    lane = lax.broadcasted_iota(jnp.int32, (1, LANES), 1)
    p0_ref[0] = jnp.zeros(p0_ref.shape[1:], LOW)

    def heads(keys):
        ones = jnp.ones((keys, LANES), LOW)
        for pair in range(width // LANES):
            query, key, value = pair_of(mixed_ref, m0_ref, pair, width, seq)
            right = jnp.concatenate([value[:keys], ones], axis=1)
            results = []
            for half in range(2):
                mask = jnp.where(lane // HD == half, SCALE, 0.0).astype(LOW)
                scores = dot_nt(query * mask, key[:keys])
                scores = jnp.where(valid[:, :keys], scores, NEGATIVE)
                exponent = jnp.exp(scores - jnp.max(scores, axis=-1, keepdims=True))
                both = dot(exponent.astype(LOW), right)
                share = 1.0 / both[:, LANES:]
                results.append(both[:, :LANES] * share)
                chance = (exponent * over_lanes(share, keys)).astype(LOW)
                p_ref[0, 2 * pair + half, :, 0:keys] = chance
                p0_ref[0, 2 * pair + half : 2 * pair + half + 1, 0:keys] = chance[0:1, :]
            ctx_ref[0, :, pl.ds(pair * LANES, LANES)] = jnp.where(lane < HD, results[0], results[1]).astype(LOW)

    short = short_keys(length)

    @pl.when(len_ref[seq] <= short)
    def _():
        heads(short)

    @pl.when(len_ref[seq] > short)
    def _():
        heads(length)

    rows = lax.broadcasted_iota(jnp.int32, (length, 1), 0)
    inputs = jnp.where(rows == 0, pick(x0_ref, seq), x_ref[0, 0].astype(F32))
    xlow_ref[0] = inputs.astype(LOW)
    hidden = inputs + dot(ctx_ref[0], wo_ref[...]) + bo_ref[...].astype(F32)
    normal, root = norm_stats(hidden)
    first = normal * g_ref[...].astype(F32) + c_ref[...].astype(F32)
    first_ref[0] = first
    low_ref[0] = first.astype(LOW)
    normal_ref[0] = normal.astype(LOW)
    root_ref[0] = jnp.broadcast_to(root, root_ref.shape[1:])
    put(early_ref, seq, first[0:1, :], slice(0, width))
    put(early_ref, seq, ctx_ref[0, 0:1, :].astype(F32), slice(width, 2 * width))
    put(n0_ref, seq, normal[0:1, :])
    put(r0_ref, seq, jnp.broadcast_to(root[0:1, :], (1, LANES)))


def attention_forward(lengths, mixed, m0, x, x0, valid, wo, bo, gain, shift):
    count, length, wide = mixed.shape
    width = wide // 3
    heads = width // HD

    def per(*shape):
        return pl.BlockSpec((1,) + shape, lambda i: (i,) + (0,) * len(shape))

    row = fixed((1, width))
    return pl.pallas_call(
        attention_forward_kernel,
        grid=(count,),
        out_shape=(
            jax.ShapeDtypeStruct((count, heads, length, length), LOW),
            jax.ShapeDtypeStruct((count, length, width), LOW),
            jax.ShapeDtypeStruct((count, length, width), F32),
            jax.ShapeDtypeStruct((count, length, width), LOW),
            jax.ShapeDtypeStruct((count, length, width), LOW),
            jax.ShapeDtypeStruct((count, length, LANES), F32),
            jax.ShapeDtypeStruct((count, length, width), LOW),
            jax.ShapeDtypeStruct((count, ROW_TILE, length), LOW),
            jax.ShapeDtypeStruct((count, 2 * width), F32),
            jax.ShapeDtypeStruct((count, width), F32),
            jax.ShapeDtypeStruct((count, LANES), F32),
        ),
        in_specs=[
            pl.BlockSpec(memory_space=pltpu.SMEM),
            per(length, wide),
            fixed((count, wide)),
            pl.BlockSpec((1, 1, length, width), lambda i: (0, i, 0, 0)),
            fixed((count, width)),
            per(1, length),
            fixed((width, width)),
            row, row, row,
        ],
        out_specs=(
            per(heads, length, length),
            per(length, width),
            per(length, width),
            per(length, width),
            per(length, width),
            per(length, LANES),
            per(length, width),
            per(ROW_TILE, length),
            fixed((count, 2 * width)),
            fixed((count, width)),
            fixed((count, LANES)),
        ),
        compiler_params=params(60),
        cost_estimate=MUCH,
        name="attention_forward",
    )(lengths, mixed, m0, x, x0, valid, wo, bo, gain, shift)


def turn(into_ref, from_ref):
    wide = from_ref.shape[1]
    tile = 384 if wide % 384 == 0 else LANES
    for column in range(0, wide, tile):
        into_ref[column : column + tile, :] = from_ref[:, column : column + tile].T


def grad_rows(me_ref, half, at_ref, right, outs, shards, line, start=0, size=None, offset=0):
    span = at_ref.shape[0] // shards
    size = size or span
    pitch = outs[0].shape[0] // (shards // 2)
    per = max(1, shards // 2)
    while per > 1 and per * size > 512:
        per //= 2
    for group in range(0, shards, per):
        pieces = []
        for shard in range(group, group + per):
            at = pl.multiple_of(shard_at(me_ref[0], half, shard, shards, line) * span + start, ROW_TILE)
            pieces.append(at_ref[pl.ds(at, size), :])
        left = pieces[0] if per == 1 else jnp.concatenate(pieces, axis=0)
        result = dot(left, right).astype(LOW)
        out_ref = outs[0] if group < shards // 2 else outs[1]
        for index in range(per):
            at = (group + index) % (shards // 2) * pitch + offset
            out_ref[at : at + size, :] = result[index * size : (index + 1) * size]


def shard_at(me, half, place, shards, line):
    if shards != 16:
        return place
    first, second = BITS[half]
    corner = me ^ (0 if place & 8 else first) ^ (0 if place & 4 else second)
    return lax.rem(corner + 4 * (place & 3), shards) if line else corner ^ (12, 4, 8, 0)[place & 3]


def cut_up(span):
    return -(-span // (2 * ROW_TILE)) * ROW_TILE


def feed_forward_kernel(
    me_ref, scal_ref, x_ref, we_ref, be_ref, wc_hbm, first_ref, bc_ref, g_ref, c_ref, cot_ref,
    slope_ref, out_ref, zg_ref, fg_ref, sums_ref, wg_ref, z0_ref, r0_ref, cot0_ref, s0_ref,
    send0_ref, send1_ref, keep0_ref, keep1_ref,
    act_ref, wc_ref, feed_ref, low_ref, turned_ref, sem,
    *, chunks, tiles, shards,
):
    step = pl.program_id(0)
    length, width = first_ref.shape[1:]
    count = x_ref.shape[0] // length
    group = first_ref.shape[0]
    groups = count // group
    chunk = we_ref.shape[1]
    second = chunks + groups + 1
    copy = pltpu.make_async_copy(wc_hbm, wc_ref, sem)

    @pl.when(step == 0)
    def _():
        copy.start()

    @pl.when(step < chunks)
    def _():
        u = dot(x_ref[...], we_ref[...]) + be_ref[...].astype(F32)
        active, slope = gelu_both(u)
        active = active.astype(LOW)
        act_ref[:, pl.ds(pl.multiple_of(step * chunk, LANES), chunk)] = active
        slope_ref[...] = slope.astype(LOW)
        for part in range(count):
            s0_ref[part : part + 1, :] = slope[part * length : part * length + 1, :]

    def feed(seq):
        rows = pl.ds(pl.multiple_of(seq * group * length, ROW_TILE), group * length)
        feed_ref[lax.rem(seq, 2)] = dot(act_ref[rows, :], wc_ref[...])

    def norms(at):
        for one in range(group):
            norm(at, one)

    def norm(at, one):
        seq = at * group + one
        weight = scal_ref[seq]
        keep = scal_ref[count]
        normal, root = norm_stats(
            first_ref[one] + feed_ref[lax.rem(at, 2), one * length : (one + 1) * length, :] + bc_ref[...].astype(F32)
        )
        gain = g_ref[...].astype(F32)
        result = normal * gain + c_ref[...].astype(F32)
        cot = cot_ref[one].astype(F32)
        out_ref[one] = weight * result
        put(wg_ref, seq, jnp.sum(cot * result, axis=0, keepdims=True))
        put(z0_ref, seq, normal[0:1, :])
        put(cot0_ref, seq, cot[0:1, :])
        put(r0_ref, seq, jnp.broadcast_to(root[0:1, :], (1, LANES)))
        rows = lax.broadcasted_iota(jnp.int32, (length, 1), 0)
        grad = cot * jnp.where(rows == 0, weight * keep, weight)
        z_grad = norm_back(grad, gain, normal, root)
        zg_ref[one] = z_grad
        feed_grad = z_grad.astype(LOW)
        fg_ref[one] = feed_grad
        low_ref[pl.ds(pl.multiple_of(seq * length, ROW_TILE), length), :] = feed_grad
        sums_ref[0:1, :] += jnp.sum(grad * normal, axis=0, keepdims=True)
        sums_ref[1:2, :] += jnp.sum(grad, axis=0, keepdims=True)
        sums_ref[2:3, :] += jnp.sum(feed_grad.astype(F32), axis=0, keepdims=True)

    @pl.when(step == chunks)
    def _():
        copy.wait()
        sums_ref[...] = jnp.zeros(sums_ref.shape, F32)
        feed(0)

    @pl.when((step > chunks) & (step < second - 1))
    def _():
        feed(step - chunks)
        norms(step - chunks - 1)

    @pl.when(step == second - 1)
    def _():
        norms(groups - 1)

    @pl.when(step == second)
    def _():
        turn(turned_ref, low_ref)

    def grads(half, send_ref, keep_ref):
        tile = send_ref.shape[1]
        columns = pl.ds(pl.multiple_of((step - second) * tile, LANES), tile)
        right = act_ref[:, columns]
        grad_rows(me_ref, half, turned_ref, right, (send_ref, keep_ref), shards, False)

    @pl.when((step >= second) & (step < second + tiles))
    def _():
        grads(0, send0_ref, keep0_ref)

    @pl.when(step >= second + tiles)
    def _():
        grads(1, send1_ref, keep1_ref)


def feed_forward(me, scal, x, first, we, be, wc, bc, gain, shift, cot, shards):
    count, length, width = first.shape
    rows = count * length
    hidden = we.shape[1]
    chunk = 1024
    chunks = hidden // chunk
    tile = 512
    tiles = hidden // 2 // tile
    second = chunks + 1 + count // (2 if count % 2 == 0 else 1)

    group = 2 if count % 2 == 0 else 1
    groups = count // group

    def part(i):
        return jnp.minimum(i, chunks - 1)

    def seq(i):
        return jnp.clip(i - chunks - 1, 0, groups - 1)

    def early(i):
        return (0, jnp.clip(i - second, 0, tiles - 1))

    def late(i):
        return (0, jnp.clip(i - second - tiles, 0, tiles - 1))

    def per(*shape):
        return pl.BlockSpec((group,) + shape, lambda i: (seq(i),) + (0,) * len(shape))

    row = fixed((1, width))
    cut = jax.ShapeDtypeStruct((width // 2, hidden // 2), LOW)
    block = (width // 2, tile)
    return pl.pallas_call(
        functools.partial(feed_forward_kernel, chunks=chunks, tiles=tiles, shards=shards),
        grid=(second + 2 * tiles,),
        out_shape=(
            jax.ShapeDtypeStruct((rows, hidden), LOW),
            jax.ShapeDtypeStruct((count, length, width), F32),
            jax.ShapeDtypeStruct((count, length, width), F32),
            jax.ShapeDtypeStruct((count, length, width), LOW),
            jax.ShapeDtypeStruct((8, width), F32),
            jax.ShapeDtypeStruct((count, width), F32),
            jax.ShapeDtypeStruct((count, width), F32),
            jax.ShapeDtypeStruct((count, LANES), F32),
            jax.ShapeDtypeStruct((count, width), F32),
            jax.ShapeDtypeStruct((count, hidden), F32),
            cut, cut, cut, cut,
        ),
        in_specs=[
            pl.BlockSpec(memory_space=pltpu.SMEM),
            pl.BlockSpec(memory_space=pltpu.SMEM),
            fixed((rows, width)),
            pl.BlockSpec((width, chunk), lambda i: (0, part(i))),
            pl.BlockSpec((1, chunk), lambda i: (0, part(i))),
            ANYWHERE,
            per(length, width),
            row, row, row,
            per(length, width),
        ],
        out_specs=(
            pl.BlockSpec((rows, chunk), lambda i: (0, part(i))),
            per(length, width),
            per(length, width),
            per(length, width),
            fixed((8, width)),
            fixed((count, width)),
            fixed((count, width)),
            fixed((count, LANES)),
            fixed((count, width)),
            pl.BlockSpec((count, chunk), lambda i: (0, part(i))),
            pl.BlockSpec(block, early),
            pl.BlockSpec(block, late),
            pl.BlockSpec(block, early),
            pl.BlockSpec(block, late),
        ),
        scratch_shapes=[
            pltpu.VMEM((rows, hidden), LOW),
            pltpu.VMEM((hidden, width), LOW),
            pltpu.VMEM((2, group * length, width), F32),
            pltpu.VMEM((rows, width), LOW),
            pltpu.VMEM((width, rows), LOW),
            pltpu.SemaphoreType.DMA,
        ],
        compiler_params=params(60),
        cost_estimate=MUCH,
        name="feed_forward",
    )(me, scal, x, we, be, wc, first, bc, gain, shift, cot)


def feed_backward_kernel(
    me_ref, fg_ref, slope_ref, wc_ref, we_hbm, zg_ref, normal_ref, root_ref, g_ref, x_ref,
    eb_ref, hgrad_ref, ag_ref, sums_ref, h0_ref,
    es0_ref, es1_ref, ek0_ref, ek1_ref,
    hg_ref, hidden_ref, we_ref, back_ref, sem,
    *, chunks, shards,
):
    step = pl.program_id(0)
    length, width = zg_ref.shape[1:]
    count = fg_ref.shape[0] // length
    group = zg_ref.shape[0]
    groups = count // group
    chunk = slope_ref.shape[1]
    second = chunks + groups + 1
    copy = pltpu.make_async_copy(we_hbm, we_ref, sem)

    @pl.when(step == 0)
    def _():
        copy.start()

    @pl.when(step < chunks)
    def _():
        grad = (dot_nt(fg_ref[...], wc_ref[...]) * slope_ref[...].astype(F32)).astype(LOW)
        at = pl.multiple_of(step * chunk, LANES)
        hg_ref[:, pl.ds(at, chunk)] = grad
        eb_ref[...] = jnp.sum(grad.astype(F32), axis=0, keepdims=True)
        hidden_ref[pl.ds(at, chunk), :] = grad.T

    def feed(seq):
        rows = pl.ds(pl.multiple_of(seq * group * length, ROW_TILE), group * length)
        back_ref[lax.rem(seq, 2)] = dot_nt(hg_ref[rows, :], we_ref[...])

    def norms(at):
        for one in range(group):
            norm(at, one)

    def norm(at, one):
        seq = at * group + one
        grad = zg_ref[one] + back_ref[lax.rem(at, 2), one * length : (one + 1) * length, :]
        normal = normal_ref[one].astype(F32)
        h_grad = norm_back(grad, g_ref[...].astype(F32), normal, root_ref[one, :, 0:1])
        hgrad_ref[one] = h_grad
        put(h0_ref, seq, h_grad[0:1, :])
        attended = h_grad.astype(LOW)
        ag_ref[one] = attended
        sums_ref[0:1, :] += jnp.sum(grad * normal, axis=0, keepdims=True)
        sums_ref[1:2, :] += jnp.sum(grad, axis=0, keepdims=True)
        sums_ref[2:3, :] += jnp.sum(attended.astype(F32), axis=0, keepdims=True)

    @pl.when(step == chunks)
    def _():
        copy.wait()
        sums_ref[...] = jnp.zeros(sums_ref.shape, F32)
        feed(0)

    @pl.when((step > chunks) & (step < second - 1))
    def _():
        feed(step - chunks)
        norms(step - chunks - 1)

    @pl.when(step == second - 1)
    def _():
        norms(groups - 1)

    span = hidden_ref.shape[0] // shards
    first = cut_up(span)
    for half, outs, start, size in (
        (0, (es0_ref, ek0_ref), 0, first), (1, (es1_ref, ek1_ref), first, span - first)
    ):

        @pl.when(step == second + half)
        def _():
            grad_rows(me_ref, half, hidden_ref, x_ref[...], outs, shards, False, start, size)


def feed_backward(me, fg, slope, wc, we, zg, normal, root, gain, x, shards):
    count, length, width = zg.shape
    rows, hidden = slope.shape
    chunk = 1024
    chunks = hidden // chunk

    group = 2 if count % 2 == 0 else 1
    groups = count // group

    def part(i):
        return jnp.minimum(i, chunks - 1)

    def seq(i):
        return jnp.clip(i - chunks - 1, 0, groups - 1)

    def per(*shape):
        return pl.BlockSpec((group,) + shape, lambda i: (seq(i),) + (0,) * len(shape))

    rows_of = [cut_up(hidden // shards), hidden // shards - cut_up(hidden // shards)] * 2
    cuts = [(shards // 2 * size, width) for size in rows_of]
    return pl.pallas_call(
        functools.partial(feed_backward_kernel, chunks=chunks, shards=shards),
        grid=(chunks + groups + 3,),
        out_shape=(
            jax.ShapeDtypeStruct((1, hidden), F32),
            jax.ShapeDtypeStruct((count, length, width), F32),
            jax.ShapeDtypeStruct((count, length, width), LOW),
            jax.ShapeDtypeStruct((8, width), F32),
            jax.ShapeDtypeStruct((count, width), F32),
        )
        + tuple(jax.ShapeDtypeStruct(cut, LOW) for cut in cuts),
        in_specs=[
            pl.BlockSpec(memory_space=pltpu.SMEM),
            fixed((rows, width)),
            pl.BlockSpec((rows, chunk), lambda i: (0, part(i))),
            pl.BlockSpec((chunk, width), lambda i: (part(i), 0)),
            ANYWHERE,
            per(length, width),
            per(length, width),
            per(length, LANES),
            fixed((1, width)),
            fixed((rows, width)),
        ],
        out_specs=(
            pl.BlockSpec((1, chunk), lambda i: (0, part(i))),
            per(length, width),
            per(length, width),
            fixed((8, width)),
            fixed((count, width)),
        )
        + tuple(fixed(cut) for cut in cuts),
        scratch_shapes=[
            pltpu.VMEM((rows, hidden), LOW),
            pltpu.VMEM((hidden, rows), LOW),
            pltpu.VMEM((width, hidden), LOW),
            pltpu.VMEM((2, group * length, width), F32),
            pltpu.SemaphoreType.DMA,
        ],
        compiler_params=params(60),
        cost_estimate=MUCH,
        name="feed_backward",
    )(me, fg, slope, wc, we, zg, normal, root, gain, x)


def attention_backward_kernel(len_ref, ag_ref, wo_ref, p_ref, mixed_ref, m0_ref, ctx_ref, *refs):
    mg_ref, mg0_ref, sums_ref, dctx_ref = refs[-4:]
    step = pl.program_id(0)
    width = ag_ref.shape[2]

    @pl.when(step == 0)
    def _():
        sums_ref[...] = jnp.zeros(sums_ref.shape, F32)

    dctx_ref[...] = dot_nt(ag_ref[0], wo_ref[...]).astype(LOW)
    lane = lax.broadcasted_iota(jnp.int32, (1, LANES), 1)
    length = ag_ref.shape[1]

    def heads(keys):
        minus = jnp.full((keys, LANES), -1.0, LOW)
        for pair in range(width // LANES):
            query, key, value = pair_of(mixed_ref, m0_ref, pair, width, step)
            here = pl.ds(pair * LANES, LANES)
            grad = dctx_ref[:, here]
            left = jnp.concatenate([grad, grad * ctx_ref[0, :, here]], axis=1)
            right = jnp.concatenate([value[:keys], minus], axis=1)
            queries, turned_s, turned_p = [], [], []
            for half in range(2):
                mask = jnp.where(lane // HD == half, 1.0, 0.0).astype(LOW)
                chance = p_ref[0, 2 * pair + half, :, 0:keys]
                less = dot_nt(left * jnp.concatenate([mask, mask], axis=1), right)
                s_grad = (chance.astype(F32) * less).astype(LOW)
                queries.append(dot(s_grad, key[:keys]))
                turned_s.append(s_grad.T)
                turned_p.append(chance.T)
            keys_grad = dot(jnp.concatenate(turned_s, axis=0), query) * SCALE
            values_grad = dot(jnp.concatenate(turned_p, axis=0), grad)
            for which, (one, two) in enumerate(
                (
                    (queries[0] * SCALE, queries[1] * SCALE),
                    (keys_grad[:keys], keys_grad[keys:]),
                    (values_grad[:keys], values_grad[keys:]),
                )
            ):
                low = jnp.where(lane < HD, one, two).astype(LOW)
                columns = pl.ds(which * width + pair * LANES, LANES)
                mg_ref[0, 0 : low.shape[0], columns] = low
                if low.shape[0] < length:
                    mg_ref[0, low.shape[0] :, columns] = jnp.zeros((length - low.shape[0], LANES), LOW)
                put(mg0_ref, step, low[0:1, :].astype(F32), columns)
                if which != 1:
                    spot = slice(pair * LANES, (pair + 1) * LANES)
                    sums_ref[which // 2 : which // 2 + 1, spot] += jnp.sum(low.astype(F32), axis=0, keepdims=True)

    short = short_keys(length)

    @pl.when(len_ref[step] <= short)
    def _():
        heads(short)

    @pl.when(len_ref[step] > short)
    def _():
        heads(length)


def attention_backward(lengths, ag, wo, p, mixed, m0, ctx, after):
    count, length, wide = mixed.shape
    width = wide // 3
    heads = width // HD

    def per(*shape):
        return pl.BlockSpec((1,) + shape, lambda i: (i,) + (0,) * len(shape))

    return pl.pallas_call(
        attention_backward_kernel,
        grid=(count,),
        out_shape=(
            jax.ShapeDtypeStruct((count, length, wide), LOW),
            jax.ShapeDtypeStruct((count, wide), F32),
            jax.ShapeDtypeStruct((8, width), F32),
        ),
        in_specs=[
            pl.BlockSpec(memory_space=pltpu.SMEM),
            per(length, width),
            fixed((width, width)),
            per(heads, length, length),
            per(length, wide),
            fixed((count, wide)),
            per(length, width),
        ]
        + [ANYWHERE] * len(after),
        out_specs=(per(length, wide), fixed((count, wide)), fixed((8, width))),
        scratch_shapes=[pltpu.VMEM((length, width), LOW)],
        compiler_params=params(60),
        cost_estimate=MUCH,
        name="attention_backward",
    )(lengths, ag, wo, p, mixed, m0, ctx, *after)


def attention_grads_kernel(me_ref, mg_ref, ag_ref, x_ref, ctx_ref, mg0_ref, h0_ref, wi_hbm, *refs, shards):
    s0_ref, s1_ref, k0_ref, k1_ref, term_ref, turned_ref, other_ref, wi_ref, sem = refs[-9:]
    step = pl.program_id(0)
    copy = pltpu.make_async_copy(wi_hbm, wi_ref, sem)

    @pl.when(step == 0)
    def _():
        copy.start()

    @pl.when(step == 1)
    def _():
        copy.wait()
        term_ref[...] = h0_ref[...] + dot_nt(mg0_ref[...].astype(LOW), wi_ref[...])

    @pl.when(step == 0)
    def _():
        turn(turned_ref, mg_ref)
        turn(other_ref, ag_ref)

    span, other = turned_ref.shape[0] // shards, other_ref.shape[0] // shards
    first, last = cut_up(span), other - cut_up(other)
    for half, outs, in_rows, out_rows in (
        (0, (s0_ref, k0_ref), (0, first), (0, last)),
        (1, (s1_ref, k1_ref), (first, span - first), (last, other - last)),
    ):

        @pl.when(step == half)
        def _():
            grad_rows(me_ref, half, turned_ref, x_ref[...], outs, shards, True, *in_rows)
            grad_rows(me_ref, half, other_ref, ctx_ref[...], outs, shards, True, *out_rows, in_rows[1])


def attention_grads(me, mg, ag, x, ctx, mg0, h0, wi, after, shards):
    rows, wide = mg.shape
    width = wide // 3
    first = cut_up(wide // shards) + width // shards - cut_up(width // shards)
    cuts = [(shards // 2 * size, width) for size in (first, (wide + width) // shards - first)] * 2
    return pl.pallas_call(
        functools.partial(attention_grads_kernel, shards=shards),
        grid=(2,),
        out_shape=tuple(jax.ShapeDtypeStruct(cut, LOW) for cut in cuts) + (jax.ShapeDtypeStruct(h0.shape, F32),),
        in_specs=[
            pl.BlockSpec(memory_space=pltpu.SMEM),
            fixed((rows, wide)),
            fixed((rows, width)),
            fixed((rows, width)),
            fixed((rows, width)),
            fixed(mg0.shape),
            fixed(h0.shape),
            ANYWHERE,
        ]
        + [ANYWHERE] * len(after),
        out_specs=tuple(fixed(cut) for cut in cuts) + (fixed(h0.shape),),
        scratch_shapes=[
            pltpu.VMEM((wide, rows), LOW),
            pltpu.VMEM((width, rows), LOW),
            pltpu.VMEM(wi.shape, LOW),
            pltpu.SemaphoreType.DMA,
        ],
        compiler_params=params(60),
        cost_estimate=MUCH,
        name="attention_grads",
    )(me, mg, ag, x, ctx, mg0, h0, wi, *after)


def shard_groups(count, wide):
    span = wide // count
    first = [span * shard // HD for shard in range(count)]
    most = max((span * shard + span - 1) // HD - first[shard] + 1 for shard in range(count))
    return [min(one, wide // HD - most) for one in first], most


def input_grad_kernel(mg_ref, w_ref, hgrad_ref, sg_ref, p0_ref, fk_ref, fv_ref, fq_ref, *refs):
    out_ref = refs[-1]
    seq = pl.program_id(0)
    length, width = hgrad_ref.shape[1:]
    rows = lax.broadcasted_iota(jnp.int32, (length, 1), 0)
    back = dot_nt(mg_ref[0], w_ref[...]) + dot_tn(sg_ref[0], fk_ref[0]) + dot_tn(p0_ref[0], fv_ref[0])
    out_ref[0] = back + hgrad_ref[0] + jnp.where(rows == 0, pick(fq_ref, seq), 0.0)


def input_grad(mg, weight, hgrad, sg, p0, fk, fv, fq, after):
    count, length, wide = mg.shape
    width = wide // 3

    def per(*shape):
        return pl.BlockSpec((1,) + shape, lambda i: (i,) + (0,) * len(shape))

    return pl.pallas_call(
        input_grad_kernel,
        grid=(count,),
        out_shape=jax.ShapeDtypeStruct((count, length, width), F32),
        in_specs=[
            per(length, wide),
            fixed((width, wide)),
            per(length, width),
            per(ROW_TILE, length),
            per(ROW_TILE, length),
            per(ROW_TILE, width),
            per(ROW_TILE, width),
            fixed((count, width)),
        ]
        + [ANYWHERE] * len(after),
        out_specs=per(length, width),
        compiler_params=params(60),
        cost_estimate=MUCH,
        name="input_grad",
    )(mg, weight, hgrad, sg, p0, fk, fv, fq, *after)


def last_kernel(
    g0_ref, z0_ref, r2_ref, g2_ref, slope_ref, wc_ref, we_ref, n0_ref, r1_ref, g1_ref, wo_ref, wi_hbm,
    p0_ref, mixed_ref, m0_ref, x_ref, s2_ref, s1_ref, s0_ref, eb_ref, early_ref, emb_ref, summary_ref, *refs, groups
):
    (
        sg_ref, fk_ref, fv_ref, fq_ref, send_ref,
        fg_ref, ag_ref, hg_ref, eball_ref, coef_ref, sums_ref, pack_ref,
        zg_ref, acc_ref, hz_ref, dctx_ref, rows_ref, wi_ref, sem,
    ) = refs[-19:]
    step = pl.program_id(0)
    count, width = g0_ref.shape
    chunks = pl.num_programs(0) - count
    copy = pltpu.make_async_copy(wi_hbm, wi_ref, sem)

    @pl.when(step == 0)
    def _():
        copy.start()
        grad = g0_ref[...]
        z_grad = norm_back(grad, g2_ref[...].astype(F32), z0_ref[...], r2_ref[:, 0:1])
        zg_ref[...] = z_grad
        low = z_grad.astype(LOW)
        fg_ref[...] = low
        sums_ref[0:2, :] = s0_ref[0:2, :]
        sums_ref[6:7, :] = s2_ref[0:1, :] + jnp.sum(grad * z0_ref[...], axis=0, keepdims=True)
        sums_ref[7:8, :] = s2_ref[1:2, :] + jnp.sum(grad, axis=0, keepdims=True)
        sums_ref[5:6, :] = s2_ref[2:3, :] + jnp.sum(low.astype(F32), axis=0, keepdims=True)
        acc_ref[...] = jnp.zeros(acc_ref.shape, F32)

    @pl.when(step < chunks)
    def _():
        grad = (dot_nt(fg_ref[...], wc_ref[...]) * slope_ref[...].astype(F32)).astype(LOW)
        here = pl.ds(pl.multiple_of(step * wc_ref.shape[0], LANES), wc_ref.shape[0])
        hg_ref[:, here] = grad.astype(F32)
        eball_ref[0:1, here] = eb_ref[...] + jnp.sum(grad.astype(F32), axis=0, keepdims=True)
        acc_ref[...] += dot_nt(grad, we_ref[...])

    @pl.when(step == chunks - 1)
    def _():
        grad = zg_ref[...] + acc_ref[...]
        normal = n0_ref[...]
        h_grad = norm_back(grad, g1_ref[...].astype(F32), normal, r1_ref[:, 0:1])
        hz_ref[0:count, :] = h_grad
        low = h_grad.astype(LOW)
        ag_ref[...] = low.astype(F32)
        sums_ref[3:4, :] = s1_ref[0:1, :] + jnp.sum(grad * normal, axis=0, keepdims=True)
        sums_ref[4:5, :] = s1_ref[1:2, :] + jnp.sum(grad, axis=0, keepdims=True)
        sums_ref[2:3, :] = s1_ref[2:3, :] + jnp.sum(low.astype(F32), axis=0, keepdims=True)
        context_grad = dot_nt(low, wo_ref[...])
        dctx_ref[0:count, :] = context_grad
        copy.wait()
        heads = head_rows(width)
        spread_q = [jnp.where(heads, m0_ref[one : one + 1, 0:width], 0.0).astype(LOW) for one in range(count)]
        spread_v = [jnp.where(heads, context_grad[one : one + 1, :], 0.0).astype(LOW) for one in range(count)]
        from_key = dot_nt(jnp.concatenate(spread_q, axis=0), wi_ref[:, width : 2 * width]) * SCALE
        from_value = dot_nt(jnp.concatenate(spread_v, axis=0), wi_ref[:, 2 * width :])
        for one in range(count):
            fk_ref[one] = from_key[one * ROW_TILE : (one + 1) * ROW_TILE].astype(LOW)
            fv_ref[one] = from_value[one * ROW_TILE : (one + 1) * ROW_TILE].astype(LOW)

    @pl.when(step >= chunks)
    def _():
        seq = step - chunks
        heads = head_rows(width)
        own = dctx_ref[pl.ds(seq, 1), :]
        grad = jnp.where(heads, own, 0.0).astype(LOW)
        query0 = pick(m0_ref, seq, slice(0, width))
        key = with_first(mixed_ref[0, :, width : 2 * width], pick(m0_ref, seq, slice(width, 2 * width)))
        value = with_first(mixed_ref[0, :, 2 * width :], pick(m0_ref, seq, slice(2 * width, 3 * width)))
        chance_low = p0_ref[0]
        chance = chance_low.astype(F32)
        p_grad = dot_nt(grad, value)
        s_grad = (chance * (p_grad - jnp.sum(p_grad * chance, axis=-1, keepdims=True))).astype(LOW)
        dq = dot(s_grad, key)
        dq = jnp.sum(jnp.where(heads, dq, 0.0), axis=0, keepdims=True) * SCALE
        put(coef_ref, seq, dq, slice(0, width))
        put(coef_ref, seq, query0 * SCALE, slice(width, 2 * width))
        put(coef_ref, seq, own, slice(2 * width, 3 * width))
        inputs = x_ref[0]
        rows_ref[0, 0:1, :] = inputs[0:1, :].astype(F32)
        both = dot(jnp.concatenate([s_grad, chance_low], axis=0), inputs)
        rows_ref[1] = both[0:ROW_TILE]
        rows_ref[2] = both[ROW_TILE:]
        firsts, most = groups
        per = width // HD
        for shard, first in enumerate(firsts):
            for turn_of in range(most):
                which, head = divmod(first + turn_of, per)
                head = head if which else 0
                at = pl.ds(count + seq * most + turn_of, 1)
                pack_ref[shard, at, 0:width] = rows_ref[which, head : head + 1, :]
        sg_ref[0] = s_grad
        sums_ref[0:1, :] += dq
        held = jnp.sum(chance, axis=-1, keepdims=True)
        sums_ref[1:2, :] += jnp.sum(held * grad.astype(F32), axis=0, keepdims=True)

    @pl.when(step == pl.num_programs(0) - 1)
    def _():
        fq_ref[...] = dot_nt(coef_ref[:, 0:width].astype(LOW), wi_ref[:, 0:width]) + hz_ref[0:count, :]
        firsts, most = groups
        shards = len(firsts)
        starts, pitch, begin = parcel(count, shards, width, eball_ref.shape[1], most, emb_ref.shape[1])
        for shard in range(shards):
            for name, source in (("feed", fg_ref), ("attended", ag_ref), ("hidden", hg_ref), ("coef", coef_ref)):
                span = source.shape[1] // shards
                piece = source[:, shard * span : (shard + 1) * span].astype(F32)
                pack_ref[shard, 0:count, starts[name] : starts[name] + span] = piece
            pack_ref[shard, 0:count, starts["emb"] : starts["emb"] + emb_ref.shape[1]] = emb_ref[...].astype(F32)
            span = width // shards
            at = starts["vectors"]
            pack_ref[shard, count : count + 8, at : at + span] = sums_ref[:, shard * span : (shard + 1) * span]
            span = eball_ref.shape[1] // shards
            for line, column in enumerate(range(0, span, LANES)):
                size = min(LANES, span - column)
                piece = eball_ref[0:1, shard * span + column : shard * span + column + size]
                pack_ref[shard, count + 8 + line : count + 9 + line, at : at + size] = piece
            send_ref[shard, 0:begin, 0 : pitch - LANES] = pack_ref[shard, 0:begin, 0 : pitch - LANES].astype(LOW)
            send_ref[shard, 2 * count : begin, pitch - LANES :] = jnp.zeros((begin - 2 * count, LANES), LOW)
        for seq in range(count):
            lines = [(begin + 2 * seq, 0, pitch), (begin + 2 * seq + 1, 0, pitch)]
            lines += [(2 * seq, pitch - LANES, pitch), (2 * seq + 1, pitch - LANES, pitch)]
            at = 0
            for line, column, end in lines:
                while column < end and at < 3 * width:
                    source, start = (early_ref, at) if at < 2 * width else (summary_ref, at - 2 * width)
                    size = min(end - column, (2 * width if at < 2 * width else 3 * width) - at)
                    value = source[seq : seq + 1, start : start + size].astype(F32)
                    pack_ref[0, line : line + 1, column : column + size] = value
                    column += size
                    at += size
        early = pack_ref[0, begin : begin + 2 * count, :].astype(LOW)
        spare = pack_ref[0, 0 : 2 * count, pitch - LANES :].astype(LOW)
        for shard in range(shards):
            send_ref[shard, begin : begin + 2 * count, :] = early
            send_ref[shard, 0 : 2 * count, pitch - LANES :] = spare


def parcel(count, shards, width, hidden, most, emb):
    starts, at = {}, 0
    for name, span in (
        ("feed", width // shards), ("attended", width // shards), ("hidden", hidden // shards),
        ("coef", 3 * width // shards), ("emb", emb),
    ):
        starts[name] = at
        at += -(-span // LANES) * LANES
    starts["vectors"] = width
    pitch = max(at, width + LANES) + LANES
    return starts, pitch, -(-(count + max(most * count, 8 + -(-hidden // shards // LANES))) // 8) * 8


def last_rows(
    g0, z0, r2, g2, slope0, wc, we, n0, r1, g1, wo, wi, p0, mixed, m0, x, s2, s1, s0, eb, early, emb, summary, after, shards
):
    count, length, wide = mixed.shape
    width = wide // 3
    hidden = slope0.shape[1]
    chunk = 768
    chunks = hidden // chunk
    groups = shard_groups(shards, wide)
    _, pitch, begin = parcel(count, shards, width, hidden, groups[1], emb.shape[1])
    send = (shards, begin + 2 * count, pitch)

    def part(i):
        return jnp.minimum(i, chunks - 1)

    def seq(i):
        return jnp.maximum(i - chunks, 0)

    def per(*shape):
        return pl.BlockSpec((1,) + shape, lambda i: (seq(i),) + (0,) * len(shape))

    row = fixed((1, width))
    rows = fixed((count, width))
    return pl.pallas_call(
        functools.partial(last_kernel, groups=groups),
        grid=(chunks + count,),
        out_shape=(
            jax.ShapeDtypeStruct((count, ROW_TILE, length), LOW),
            jax.ShapeDtypeStruct((count, ROW_TILE, width), LOW),
            jax.ShapeDtypeStruct((count, ROW_TILE, width), LOW),
            jax.ShapeDtypeStruct((count, width), F32),
            jax.ShapeDtypeStruct(send, LOW),
        ),
        in_specs=[
            rows, rows, fixed((count, LANES)), row,
            pl.BlockSpec((count, chunk), lambda i: (0, part(i))),
            pl.BlockSpec((chunk, width), lambda i: (part(i), 0)),
            pl.BlockSpec((width, chunk), lambda i: (0, part(i))),
            rows, fixed((count, LANES)), row,
            fixed((width, width)),
            ANYWHERE,
            per(ROW_TILE, length),
            per(length, wide),
            fixed((count, wide)),
            per(length, width),
            fixed((8, width)),
            fixed((8, width)),
            fixed((8, width)),
            pl.BlockSpec((1, chunk), lambda i: (0, part(i))),
            fixed(early.shape),
            fixed(emb.shape),
            fixed(summary.shape),
        ]
        + [ANYWHERE] * len(after),
        out_specs=(
            per(ROW_TILE, length),
            fixed((count, ROW_TILE, width)),
            fixed((count, ROW_TILE, width)),
            rows,
            fixed(send),
        ),
        scratch_shapes=[
            pltpu.VMEM((count, width), LOW),
            pltpu.VMEM((count, width), F32),
            pltpu.VMEM((count, hidden), F32),
            pltpu.VMEM((8, hidden), F32),
            pltpu.VMEM((count, wide), F32),
            pltpu.VMEM((8, width), F32),
            pltpu.VMEM(send, F32),
            pltpu.VMEM((count, width), F32),
            pltpu.VMEM((count, width), F32),
            pltpu.VMEM((8, width), F32),
            pltpu.VMEM((8, width), F32),
            pltpu.VMEM((3, ROW_TILE, width), F32),
            pltpu.VMEM((width, wide), LOW),
            pltpu.SemaphoreType.DMA,
        ],
        compiler_params=params(60),
        cost_estimate=LITTLE,
        name="last_rows",
    )(g0, z0, r2, g2, slope0, wc, we, n0, r1, g1, wo, wi, p0, mixed, m0, x, s2, s1, s0, eb, early, emb, summary, *after)


def flip(value, bit, count):
    return lax.ppermute(value, "rows", [(i, i ^ bit) for i in range(count)])


def first_stage(parts, count):
    return [flip(parts[half], BITS[half][0], count) for half in range(2)]


def second_stage(sends, count):
    return [flip(sends[half], BITS[half][1], count) for half in range(2)]


def sum_low(left_ref, right_ref):
    return (left_ref[...].astype(F32) + right_ref[...].astype(F32)).astype(LOW)


def first_sum_kernel(a0, a1, b0, b1, ga0, ga1, gb0, gb1, *refs):
    sa, sb, ka, kb = refs[-4:]
    sa[...] = sum_low(a0, ga0)
    ka[...] = sum_low(a1, ga1)
    sb[...] = sum_low(b0, gb0)
    kb[...] = sum_low(b1, gb1)


def first_sum(parts, got, after):
    keep0, keep1 = parts[2:]
    rows, width = keep0.shape
    tiles = 2
    block = (rows // 2 // tiles, width)
    top = pl.BlockSpec(block, lambda i: (i, 0))
    bottom = pl.BlockSpec(block, lambda i: (i + tiles, 0))
    result = pl.pallas_call(
        first_sum_kernel,
        grid=(tiles,),
        out_shape=(jax.ShapeDtypeStruct((rows // 2, width), LOW),) * 4,
        in_specs=[top, bottom] * 4 + [ANYWHERE] * len(after),
        out_specs=(top,) * 4,
        compiler_params=params(60),
        cost_estimate=LITTLE,
        name="first_sum",
    )(keep0, keep0, keep1, keep1, got[0], got[0], got[1], got[1], *after)
    return result[:2], result[2:]


def second_sum_kernel(*refs, jobs):
    step = pl.program_id(0)
    outs = list(refs[-sum(job[0] for job in jobs) :])
    for index, (count, stacked) in enumerate(jobs):
        a, b, ga, gb = refs[4 * index : 4 * index + 4]
        rows, half = a.shape[0] // 2, a.shape[1]
        left, right = sum_low(a, ga), sum_low(b, gb)
        for number in range(count):
            out = outs.pop(0)

            @pl.when(step == number * 2 // count)
            def _():
                for shard in (0, 1) if count == 2 else (number % 2,):
                    one, two = (part[shard * rows : (shard + 1) * rows] for part in (left, right))
                    if stacked:
                        at = 2 * rows * shard if count == 2 else 0
                        out[at : at + rows, :] = one
                        out[at + rows : at + 2 * rows, :] = two
                    else:
                        at = rows * shard if count == 2 else 0
                        out[at : at + rows, :half] = one
                        out[at : at + rows, half:] = two


def second_sum(buckets, after):
    arrays, blocks, shapes = [], [], []
    for keeps, got, number, stacked in buckets:
        rows, width = keeps[0].shape
        arrays += [*keeps, *got]
        blocks += [pl.BlockSpec((rows // 2, width), lambda i: (i, 0))] * 4
        shape = (2 * rows // number, width) if stacked else (rows // number, 2 * width)
        shapes += [shape] * number
    return pl.pallas_call(
        functools.partial(second_sum_kernel, jobs=tuple(bucket[2:] for bucket in buckets)),
        grid=(2,),
        out_shape=tuple(jax.ShapeDtypeStruct(shape, LOW) for shape in shapes),
        in_specs=blocks + [ANYWHERE] * len(after),
        out_specs=tuple(fixed(shape) for shape in shapes),
        compiler_params=params(60),
        cost_estimate=LITTLE,
        name="second_sum",
    )(*arrays, *after)


def third_sum_kernel(*refs, jobs):
    outs = refs[-2 * jobs :]
    for job in range(jobs):
        a, ga = refs[2 * job : 2 * job + 2]
        for index, out in enumerate(outs[2 * job : 2 * job + 2]):

            @pl.when(pl.program_id(0) == index)
            def _():
                out[...] = sum_low(a, ga)


def third_sum(buckets, after):
    arrays, blocks, shapes = [], [], []
    for keep, got in buckets:
        rows, width = keep.shape
        arrays += [keep, got]
        blocks += [pl.BlockSpec((rows // 2, width), lambda i: (i, 0))] * 2
        shapes += [(rows // 2, width)] * 2
    return pl.pallas_call(
        functools.partial(third_sum_kernel, jobs=len(buckets)),
        grid=(2,),
        out_shape=tuple(jax.ShapeDtypeStruct(shape, LOW) for shape in shapes),
        in_specs=blocks + [ANYWHERE] * len(after),
        out_specs=tuple(fixed(shape) for shape in shapes),
        compiler_params=params(60),
        cost_estimate=MUCH,
        name="third_sum",
    )(*arrays, *after)


def wide_sum(left, right):
    return left.astype(F32) + right.astype(F32)


def line_stage(totals, count):
    got = [totals[0]]
    for step in range(1, count // 4):
        got.append(lax.ppermute(totals[step], "rows", [(i, (i + 4 * step) % count) for i in range(count)]))
    return got


def rest_kernel(*refs, parts):
    got, fix_ref = refs[:parts], refs[parts]
    in_ref, out_ref = refs[-2:]
    span, other = in_ref.shape[0], out_ref.shape[0]
    first, last = cut_up(span), other - cut_up(other)
    total = got[0][...].astype(F32)
    for one in got[1:]:
        total = total + one[...].astype(F32)
    for into, start, size, at in (
        (in_ref, 0, first, 0),
        (out_ref, 0, last, first),
        (in_ref, first, span - first, first + last),
        (out_ref, last, other - last, span + last),
    ):
        add = start + (span if into is out_ref else 0)
        into[start : start + size, :] = total[at : at + size] + fix_ref[add : add + size, :]


def rest_sum(got, fix, span, after):
    rows, width = fix.shape
    return pl.pallas_call(
        functools.partial(rest_kernel, parts=len(got)),
        out_shape=(jax.ShapeDtypeStruct((span, width), F32), jax.ShapeDtypeStruct((rows - span, width), F32)),
        in_specs=[pl.BlockSpec(memory_space=pltpu.VMEM)] * (len(got) + 1) + [ANYWHERE] * len(after),
        compiler_params=params(60),
        name="rest_sum",
    )(*got, fix, *after)


def whole_grad(full):
    return lax.psum_scatter(full.astype(F32), "rows", scatter_dimension=0, tiled=True)


def body(
    token_states, lengths, key_mask, cotangent, attention_in, attention_bias, attention_out, output_bias,
    gain_one, shift_one, expand_weight, expand_bias, contract_weight, contract_bias, gain_two, shift_two,
    projection, passage_table, candidates,
):
    section = lax.axis_index("section")
    is_first = section == 0
    count = lax.axis_size("rows")
    me = lax.axis_index("rows")
    tokens = token_states[0]
    seqs, length, width = tokens.shape
    rows = seqs * length

    bi = attention_bias[0]
    wi, wo, we, wc = attention_in[0], attention_out[0], expand_weight[0], contract_weight[0]
    bo, g1, c1, be, bc, g2, c2 = output_bias, gain_one, shift_one, expand_bias, contract_bias, gain_two, shift_two
    weights = (wi, bi, wo, bo, g1, c1, we, be, wc, bc, g2, c2)
    positions = jnp.arange(length)
    valid = (positions[None, :] < lengths[0][:, None]) & (key_mask[0] == 1) | (positions[None, :] == 0)
    valid = valid.astype(F32)[:, None, :]
    staged = count == 16 and width // count % ROW_TILE == 0
    cuts = count if staged else 2
    place = me.reshape(1).astype(jnp.int32)

    retrieved = jnp.take(passage_table, candidates, axis=0).astype(F32)
    mixed, x0 = project(token_states, wi, bi)
    message = first_rows(mixed, valid, x0, weights, projection)
    received = lax.ppermute(message, "section", [(0, 1)])
    summary_in, embedding_in = received[:, :width], received[:, width:]
    x0 = x0 + summary_in.astype(F32)
    in_bias = jnp.concatenate([bi[0], jnp.zeros_like(bi[0]), bi[1]])
    mixed0 = (dot(x0.astype(LOW), wi) + in_bias.astype(F32)).astype(LOW).astype(F32)
    chance, context, first, first_low, normal, root, x_low, chance0, early, n0, r1 = attention_forward(
        lengths[0], mixed, mixed0, token_states, x0, valid, wo, bo, g1, c1
    )
    match = jnp.sum(embedding_in.astype(F32)[:, None, :] * retrieved, axis=-1)
    chances = jax.nn.softmax(match, axis=-1)
    weight = TOPK * chances[:, 0]
    scal = jnp.concatenate([jnp.where(is_first, 1.0, weight), jnp.where(is_first, 0.0, 1.0)[None]]).astype(F32)
    first_flat = first_low.reshape(rows, width)
    slope, out, z_grad, feed_grad, sums_two, weight_grads, z0, r2, cot0, slope0, *contract = feed_forward(
        place, scal, first_flat, first, we, be, wc, bc, g2, c2, cotangent[0], cuts
    )

    contract_got = first_stage(contract, count) if staged else None
    expand_sum, h_grad, attended, sums_one, h0, *expand = feed_backward(
        place, feed_grad.reshape(rows, width), slope, wc, we, z_grad, normal, root, g1, first_flat, cuts
    )
    contract_send = ()
    if staged:
        contract_send, contract_keep = first_sum(contract, contract_got, (h0,))
        contract_got = second_stage(contract_send, count)
        expand_got = first_stage(expand, count)
    mixed_grad, mg0, sums_in = attention_backward(
        lengths[0], attended, wo, chance, mixed, mixed0, context, tuple(contract_send)
    )
    after = ()
    if staged:
        expand_send, expand_keep = first_sum(expand, expand_got, (mg0,))
        expand_got = second_stage(expand_send, count)
        after = (expand_send[0],)
    *rest, reader_term = attention_grads(
        place, mixed_grad.reshape(rows, 3 * width), attended.reshape(rows, width), x_low.reshape(rows, width),
        context.reshape(rows, width), mg0, h0, wi, after, cuts,
    )
    rest_got = first_stage(rest, count) if staged else None

    after = (rest[0],)
    if staged:
        contract_send, contract_keep, expand_send, expand_keep = second_sum(
            ((contract_keep, contract_got, 2, False), (expand_keep, expand_got, 2, True)), (rest[0],)
        )
        contract_got = flip(contract_send, 4, count)
        expand_got = flip(expand_send, 4, count)
        after = (expand_send, contract_send)
    grad_weight = jnp.sum(weight_grads, axis=1)
    one = jnp.zeros((TOPK,), F32).at[0].set(1.0)
    grad_match = (grad_weight[:, None] * weight[:, None] * (one[None, :] - chances)).astype(LOW)
    embedding_grad = jnp.sum(grad_match.astype(F32)[:, :, None] * retrieved, axis=1).astype(LOW)
    if staged:
        reader_term, _ = lax.optimization_barrier((reader_term, expand_send))
    reader_term = reader_term.astype(LOW)
    back = lax.ppermute(jnp.concatenate([reader_term, embedding_grad], axis=1), "section", [(1, 0)])
    embedding_used = jnp.where(is_first, back[:, width:], embedding_grad)
    summary_grad = dot_nt(back[:, width:], projection) + back[:, :width].astype(F32)
    grad_zero = jnp.where(is_first, cot0 + summary_grad, 0.0)
    used_summary = jnp.where(is_first, message[:, :width], summary_in)
    s_zero, from_key, from_value, from_query, parcels = last_rows(
        grad_zero, z0, r2, g2, slope0, wc, we, n0, r1, g1, wo, wi, chance0, mixed, mixed0, x_low,
        sums_two, sums_one, sums_in, expand_sum, early, embedding_used, used_summary, after, count,
    )
    after = ()
    if staged:
        rest_send, rest_keep = first_sum(rest, rest_got, (parcels,))
        rest_got = second_stage(rest_send, count)
        after = (rest_send[0],)

    got = lax.all_to_all(parcels, "rows", 0, 0, tiled=True)
    if staged:
        contract_send, contract_keep, expand_send, expand_keep = third_sum(
            ((contract_keep, contract_got), (expand_keep, expand_got)), after
        )
        contract_got = flip(contract_send, 8, count)
        expand_got = flip(expand_send, 8, count)
        after = (expand_send,)
    x_grad = input_grad(mixed_grad, wi, h_grad, s_zero, chance0, from_key, from_value, from_query, after)
    if staged:
        rest = second_sum(((rest_keep, rest_got, 4, True),), (x_grad,))
        rest_got = line_stage(rest, count)
        got, me, _ = lax.optimization_barrier((got, me, rest))
    else:
        top, bottom = jnp.concatenate(contract[:2], axis=1), jnp.concatenate(contract[2:], axis=1)
        contract = whole_grad(jnp.concatenate([top, bottom], axis=0))
        expand = whole_grad(jnp.concatenate(expand, axis=0))
        inner = 3 * width // 4
        rest = [jnp.concatenate([part[cut] for part in rest]) for cut in (slice(0, inner), slice(inner, None))]
        rest = [whole_grad(part) for part in rest]
    hidden = we.shape[1]
    span = 3 * width // count
    firsts, most = shard_groups(count, 3 * width)
    starts, pitch, begin = parcel(seqs, count, width, hidden, most, embedding_used.shape[1])

    def sent(name, size):
        return got[:, :seqs, starts[name] : starts[name] + size].reshape(count * seqs, size)

    factors = jnp.concatenate(
        [
            got[:, begin : begin + 2 * seqs].reshape(count * seqs, 2 * pitch),
            got[:, : 2 * seqs, pitch - LANES :].reshape(count * seqs, 2 * LANES),
        ],
        axis=1,
    )
    first_all, context_all, summary_all = (factors[:, i * width : (i + 1) * width] for i in range(3))
    active_all = gelu_both(dot(first_all, we) + be.astype(F32))[0].astype(LOW)
    contract_fix = dot_tn(sent("feed", width // count), active_all)
    projection_grad = dot_tn(summary_all, sent("emb", embedding_used.shape[1]))
    head = (span * me + jnp.arange(span)) // HD - jnp.asarray(firsts, jnp.int32)[me]
    chosen = (head[None, :] == jnp.arange(most)[:, None]).astype(LOW)
    coefs = (sent("coef", span)[:, None, :] * chosen[None]).reshape(count * seqs * most, span)
    groups = got[:, seqs : seqs + seqs * most, :width].reshape(count * seqs * most, width)
    fix = jnp.concatenate([dot_tn(coefs, groups), dot_tn(sent("attended", width // count), context_all)], axis=0)
    expand_fix = dot_tn(sent("hidden", hidden // count), first_all)
    at = starts["vectors"]
    packed = jnp.sum(got[:, seqs : seqs + 8, at : at + width // count].astype(F32), axis=0)
    lines = -(-hidden // count // LANES)
    e_bias = got[:, seqs + 8 : seqs + 8 + lines, at : at + LANES].astype(F32)
    e_bias = jnp.sum(e_bias, axis=0).reshape(-1)[: hidden // count]
    if staged:
        held = (contract_got, expand_got, fix, contract_fix, expand_fix, projection_grad, packed, e_bias)
        contract_got, expand_got, fix, contract_fix, expand_fix, projection_grad, packed, e_bias = (
            lax.optimization_barrier(held)
        )
        contract = contract_fix + wide_sum(contract_keep, contract_got)
        expand = wide_sum(expand_keep, expand_got) + expand_fix
        attention_in_grad, attention_out_grad = rest_sum(rest_got, fix, span, (contract, expand))
    else:
        contract = contract + contract_fix
        attention_in_grad, attention_out_grad = rest[0] + fix[:span], rest[1] + fix[span:]
        expand = expand + expand_fix
    q_bias, v_bias, o_bias, gain1, shift1, c_bias, gain2, shift2 = (packed[i] for i in range(8))
    return (
        out[None],
        x_grad[None],
        attention_in_grad.T[None],
        jnp.stack([q_bias, v_bias])[None],
        attention_out_grad.T[None],
        o_bias[None],
        gain1[None],
        shift1[None],
        expand.T[None],
        e_bias[None],
        contract.T[None],
        c_bias[None],
        gain2[None],
        shift2[None],
        projection_grad,
    )


def solution(mesh):
    in_specs = (
        P("section", "rows", None, None),
        P("section", "rows"),
        P("section", "rows", None),
        P("section", "rows", None, None),
        P("section", None, None),
        P("section", None, None),
        P("section", None, None),
        P("section", None),
        P("section", None),
        P("section", None),
        P("section", None, None),
        P("section", None),
        P("section", None, None),
        P("section", None),
        P("section", None),
        P("section", None),
        P(),
        P(),
        P("rows", None),
    )
    out_specs = (
        P("section", "rows", None, None),
        P("section", "rows", None, None),
        P("section", None, "rows"),
        P("section", None, "rows"),
        P("section", None, "rows"),
        P("section", "rows"),
        P("section", "rows"),
        P("section", "rows"),
        P("section", None, "rows"),
        P("section", "rows"),
        P("section", None, "rows"),
        P("section", "rows"),
        P("section", "rows"),
        P("section", "rows"),
        P(),
    )
    return jax.shard_map(body, mesh=mesh, in_specs=in_specs, out_specs=out_specs, check_vma=False)
```
